32 devices in a mesh: group: 8 (over z, x), rep: 4 (over y, core).
Axes of the slice: x: 2, y: 2, z: 4, core: 2. Of those that a mesh axis runs over, the one named last changes fastest.
Arguments:
- inputs: bfloat16 [16384, 1024], P(('group', 'rep')), may hold values from -6 to 6
- lengths: int32 [32, 4], P(('group', 'rep')), may hold values from 1 to 250, 512 in all within a row
- ln1_gain: bfloat16 [1024], P(('group', 'rep')), may hold values from 0.5 to 1.5
- ln1_bias: bfloat16 [1024], P(('group', 'rep')), may hold values from -1.796875 to 1.796875
- w_qkv: bfloat16 [1024, 3072], P(('group', 'rep')), may hold values from -0.1875 to 0.1875
- w_out: bfloat16 [1024, 1024], P(('group', 'rep')), may hold values from -0.5 to 0.5
- scale_attn: bfloat16 [1024], P(('group', 'rep')), may hold values from 0.5 to 1.5
- ln2_gain: bfloat16 [1024], P(('group', 'rep')), may hold values from 0.5 to 1.5
- ln2_bias: bfloat16 [1024], P(('group', 'rep')), may hold values from -1.796875 to 1.796875
- w_gate: bfloat16 [1024, 4096], P(('group', 'rep')), may hold values from -0.1875 to 0.1875
- w_up: bfloat16 [1024, 4096], P(('group', 'rep')), may hold values from -0.1875 to 0.1875
- w_down: bfloat16 [4096, 1024], P(('group', 'rep')), may hold values from -0.125 to 0.125
- scale_mlp: bfloat16 [1024], P(('group', 'rep')), may hold values from 0.5 to 1.5
- grad_out: bfloat16 [16384, 1024], P(('group', 'rep')), may hold values from -6 to 6
Outputs:
- block_out: bfloat16 [16384, 1024], P(('group', 'rep'))
- input_grad: float32 [16384, 1024], P(('group', 'rep'))
- ln1_gain_grad: float32 [1024], P('group')
- ln1_bias_grad: float32 [1024], P('group')
- w_qkv_grad: float32 [1024, 3072], P('group')
- w_out_grad: float32 [1024, 1024], P('group')
- scale_attn_grad: float32 [1024], P('group')
- ln2_gain_grad: float32 [1024], P('group')
- ln2_bias_grad: float32 [1024], P('group')
- w_gate_grad: float32 [1024, 4096], P('group')
- w_up_grad: float32 [1024, 4096], P('group')
- w_down_grad: float32 [4096, 1024], P('group')
- scale_mlp_grad: float32 [1024], P('group')
The draws below stay inside these ranges and needn't reach their ends.
Inputs may be any that keep to these rules, and one draw needn't show every extreme that they name: Each row of lengths holds one device's clips: 4 lengths that sum to 512, the longest exactly 250.
All inputs are finite; a program needn't handle non-finite values.
Results may differ from the reference program's by a relative error of at most 0.017.
Values may be sent and summed in bfloat16 or wider, within the bound.
No kernel may reach another device: no remote copies, remote signals or barrier semaphores. Data moves between devices by JAX's collectives and lax.ppermute only.
A program may use at most 192 MiB of HBM per device.

```python
import math
import jax
import jax.numpy as jnp
import numpy as np
from jax import lax

D = 1024
HEADS = 16
HEAD_DIM = 64
FF = 4096
WINDOW = 128
MAX_CLIP = 250
TOK_DEV = 512
CLIPS = 4
TOKENS = 16384
N_GROUP = 8
N_REP = 4


def steps_of(stream_key, dims, pieces, low, top_value):
    loudness, own = 1.0, jax.random.fold_in(stream_key, 6)
    for dim, blocks in pieces:
        draws = jnp.exp(jax.random.uniform(jax.random.fold_in(own, dim), (blocks,), jnp.float32, low / len(pieces), top_value / len(pieces)))
        loudness = loudness * jnp.repeat(draws, dims[dim] // blocks).reshape([-1 if axis == dim else 1 for axis in range(len(dims))])
    return loudness


def split_up(count, total, limit, lean):
    weights = [(1 << 20) // math.isqrt(rank ** lean) + 1 for rank in range(2, count + 1)]
    rest, given = total - limit - (count - 1), [1] * (count - 1)
    while rest > 0:
        candidates = [i for i in range(count - 1) if given[i] < limit]
        mass, left = sum([weights[i] for i in candidates]), rest
        for i in candidates:
            addition = min(limit - given[i], max(1, left * weights[i] // mass), rest)
            given[i] = given[i] + addition
            rest = rest - addition
    return np.array([limit] + given)


def ragged_sizes(rng, count, total, reach, skew):
    if count == 2:
        one = jax.random.randint(rng, (), max(1, total - reach), min(reach, total - 1) + 1)
        return jnp.stack([one, total - one])
    tallies = jnp.asarray(split_up(count, total, reach, skew), jnp.int32)
    couples = (count - 1) // 2
    source_of, taker = tallies[1:1 + 2 * couples:2], tallies[2:2 + 2 * couples:2]
    margin = jnp.minimum(source_of - 1, reach - taker)
    shifted = jax.random.randint(jax.random.fold_in(rng, 1), (couples,), 0, 1 << 20) % (margin + 1)
    tallies = tallies.at[1:1 + 2 * couples:2].set(source_of - shifted).at[2:2 + 2 * couples:2].set(taker + shifted)
    return tallies[jax.random.permutation(jax.random.fold_in(rng, 2), count)]


def gaussian(own_key, extent, scale, bound, pieces=(), kind=jnp.bfloat16):
    values = jax.random.normal(own_key, extent, jnp.float32) * scale
    if len(pieces) > 0:
        values = steps_of(own_key, extent, pieces, -0.22, 0.18) * values
    return jnp.clip(values, min=-bound, max=bound).astype(kind)


def setup_inputs(seed: int = 0) -> dict:
    key_of = jax.random.split(jax.random.key(seed), 15)
    inputs = gaussian(key_of[0], (TOKENS, D), 1.0, 6.0, ((0, 32),))
    lengths = jax.vmap(lambda own: ragged_sizes(own, CLIPS, TOK_DEV, MAX_CLIP, 0))(jax.random.split(key_of[1], (N_GROUP * N_REP))).reshape((N_GROUP * N_REP, CLIPS)).astype(jnp.int32)
    ln1_gain = jnp.clip(1.0 + 0.1 * jax.random.normal(key_of[2], (D,), jnp.float32), 0.5, 1.5).astype(jnp.bfloat16)
    ln1_bias = gaussian(key_of[3], (D,), 0.3, 1.796875, ((0, 32),))
    w_qkv = gaussian(key_of[4], (D, 3 * D), D ** -0.5, 0.1875, ((0, 32),))
    w_out = gaussian(key_of[5], (D, D), (D // 8) ** -0.5, 0.5, ((0, 32),))
    scale_attn = jnp.clip(0.5 + 1.0 * jax.random.uniform(key_of[6], (D,), jnp.float32) ** steps_of(key_of[6], (D,), ((0, 32),), -0.2, 0.2), 0.5, 1.5).astype(jnp.bfloat16)
    ln2_gain = jnp.clip(1.0 + 0.1 * jax.random.normal(key_of[7], (D,), jnp.float32), 0.5, 1.5).astype(jnp.bfloat16)
    ln2_bias = gaussian(key_of[8], (D,), 0.3, 1.796875, ((0, 32),))
    w_gate = gaussian(key_of[9], (D, FF), D ** -0.5, 0.1875, ((0, 32),))
    w_up = gaussian(key_of[10], (D, FF), D ** -0.5, 0.1875, ((0, 32),))
    w_down = gaussian(key_of[11], (FF, D), (FF // 2) ** -0.5, 0.125, ((0, 32),))
    scale_mlp = jnp.clip(0.5 + 1.0 * jax.random.uniform(key_of[12], (D,), jnp.float32) ** steps_of(key_of[12], (D,), ((0, 32),), -0.2, 0.2), 0.5, 1.5).astype(jnp.bfloat16)
    grad_out = gaussian(key_of[13], (TOKENS, D), 1.0, 6.0, ((0, 32),))
    return {"inputs": inputs, "lengths": lengths, "ln1_gain": ln1_gain, "ln1_bias": ln1_bias, "w_qkv": w_qkv, "w_out": w_out, "scale_attn": scale_attn, "ln2_gain": ln2_gain, "ln2_bias": ln2_bias, "w_gate": w_gate, "w_up": w_up, "w_down": w_down, "scale_mlp": scale_mlp, "grad_out": grad_out}


EPS = 1e-05
HIGH = lax.Precision.HIGHEST

@jax.custom_vjp
def low(v):
    return lax.optimization_barrier(v.astype(jnp.bfloat16)).astype(jnp.float32)

@jax.custom_vjp
def low_back(v):
    return v

def low_keep(v):
    return (low(v), None)

def low_pass(kept, grad):
    return (grad,)

def back_keep(v):
    return (v, None)

def back_low(kept, grad):
    return (low(grad),)
low.defvjp(low_keep, low_pass)
low_back.defvjp(back_keep, back_low)

def clip_layout(length_row, count):
    clip_ends = jnp.cumsum(length_row).astype(jnp.int32)
    clip_starts = clip_ends - length_row
    row_index = jnp.arange(count, dtype=jnp.int32)
    segment = lax.optimization_barrier(jnp.sum((row_index[:, None] >= clip_ends[None, :]).astype(jnp.int32), axis=1))
    member = (segment[:, None] == jnp.arange(length_row.shape[0], dtype=jnp.int32)[None, :]).astype(jnp.int32)
    position = row_index - lax.optimization_barrier(jnp.sum(member * clip_starts[None, :], axis=1))
    return (segment, position)

def rotary_tables(position, width):
    half = width // 2
    freqs = jnp.power(10000.0, -jnp.arange(half, dtype=jnp.float32) * (2.0 / width))
    angles = position.astype(jnp.float32)[:, None] * freqs[None, :]
    cosine = jnp.concatenate([jnp.cos(angles), jnp.cos(angles)], axis=1)
    sine = jnp.concatenate([jnp.sin(angles), jnp.sin(angles)], axis=1)
    return (cosine[:, None, :], sine[:, None, :])

def rotate(values, cosine, sine):
    half = values.shape[-1] // 2
    turned = jnp.concatenate([-values[..., half:], values[..., :half]], axis=-1)
    return values * cosine + turned * sine

def layer_norm(values, gain, shift):
    mean_value = lax.optimization_barrier(jnp.mean(values, axis=-1, keepdims=True))
    centered = values - mean_value
    variance = lax.optimization_barrier(jnp.mean(centered * centered, axis=-1, keepdims=True))
    return centered * lax.rsqrt(variance + EPS) * gain + shift

def device_forward(inputs, params, segment, position):
    gain_one, bias_one, w_qkv, w_out, scale_attn, gain_two, bias_two, w_gate, w_up, w_down, scale_mlp = params
    count = inputs.shape[0]
    normed = low(layer_norm(inputs, gain_one, bias_one))
    projected = low_back(jnp.dot(normed, w_qkv, precision=HIGH))
    queries = projected[:, :D].reshape(count, HEADS, HEAD_DIM)
    keys_part = projected[:, D:2 * D].reshape(count, HEADS, HEAD_DIM)
    values = low(projected[:, 2 * D:].reshape(count, HEADS, HEAD_DIM))
    cosine, sine = rotary_tables(position, HEAD_DIM)
    queries = low(rotate(queries, cosine, sine))
    keys_part = low(rotate(keys_part, cosine, sine))
    scores = low_back(jnp.einsum('qhd,khd->hqk', queries, keys_part, precision=HIGH) * HEAD_DIM ** (-0.5))
    row_index = jnp.arange(count, dtype=jnp.int32)
    offset = row_index[:, None] - row_index[None, :]
    allowed = (segment[:, None] == segment[None, :]) & (offset >= 0) & (offset < WINDOW)
    masked = jnp.where(allowed[None], scores, -jnp.inf)
    peak = lax.optimization_barrier(jnp.max(masked, axis=-1, keepdims=True))
    expd = jnp.exp(masked - peak)
    probs = expd / lax.optimization_barrier(jnp.sum(expd, axis=-1, keepdims=True))
    attended = jnp.einsum('hqk,khd->qhd', low(probs), values, precision=HIGH).reshape(count, D)
    attended = low_back(low(attended))
    branch = low_back(jnp.dot(attended, w_out, precision=HIGH))
    middle = inputs + scale_attn * branch
    normed_two = low(layer_norm(middle, gain_two, bias_two))
    gate = low_back(jnp.dot(normed_two, w_gate, precision=HIGH))
    up_value = low_back(jnp.dot(normed_two, w_up, precision=HIGH))
    hidden = low(gate * jax.nn.sigmoid(gate) * up_value)
    mlp = low_back(jnp.dot(hidden, w_down, precision=HIGH))
    return middle + scale_mlp * mlp

def reference(inputs, lengths, ln1_gain, ln1_bias, w_qkv, w_out, scale_attn, ln2_gain, ln2_bias, w_gate, w_up, w_down, scale_mlp, grad_out):
    params = tuple((p.astype(jnp.float32) for p in (ln1_gain, ln1_bias, w_qkv, w_out, scale_attn, ln2_gain, ln2_bias, w_gate, w_up, w_down, scale_mlp)))
    devices = N_GROUP * N_REP
    frames = inputs.astype(jnp.float32).reshape(devices, TOK_DEV, D)
    cotangent = grad_out.astype(jnp.float32).reshape(devices, TOK_DEV, D)

    def one_device(totals, item):
        frame_block, cot_block, length_row = item
        segment, position = clip_layout(length_row, TOK_DEV)
        result, pull = jax.vjp(lambda xv, pv: device_forward(xv, pv, segment, position), frame_block, params)
        frame_grad, param_grads = pull(cot_block)
        totals = jax.tree.map(lambda a, b: a + b, totals, param_grads)
        return (totals, (result.astype(jnp.bfloat16), frame_grad))
    zeros = tuple((jnp.zeros(p.shape, jnp.float32) for p in params))
    grads, (results, frame_grads) = lax.scan(one_device, zeros, (frames, cotangent, lengths))
    return (results.reshape(TOKENS, D), frame_grads.reshape(TOKENS, D)) + tuple(grads)
```

```python
import math

import jax
import jax.numpy as jnp
from jax import lax
from jax.sharding import PartitionSpec as P

HEADS = 16
WINDOW = 128
EPS = 1e-05
AXES = ("group", "rep")
BF = jnp.bfloat16
F32 = jnp.float32


def clip_layout(length_row, count):
    clip_ends = jnp.cumsum(length_row)
    clip_starts = clip_ends - length_row
    row_index = jnp.arange(count, dtype=jnp.int32)
    segment = jnp.sum((row_index[:, None] >= clip_ends[None, :]).astype(jnp.int32), axis=1)
    member = (segment[:, None] == jnp.arange(length_row.shape[0], dtype=jnp.int32)[None, :]).astype(
        jnp.int32
    )
    position = row_index - jnp.sum(member * clip_starts[None, :], axis=1)
    return (segment, position)


def rotary_tables(position, width):
    half = width // 2
    freqs = jnp.power(10000.0, -jnp.arange(half, dtype=F32) * (2.0 / width))
    angles = position.astype(F32)[:, None] * freqs[None, :]
    cosine = jnp.concatenate([jnp.cos(angles), jnp.cos(angles)], axis=1)
    sine = jnp.concatenate([jnp.sin(angles), jnp.sin(angles)], axis=1)
    return (cosine[:, None, :], sine[:, None, :])


def rotate(values, cosine, sine):
    half = values.shape[-1] // 2
    turned = jnp.concatenate([-values[..., half:], values[..., :half]], axis=-1)
    return values * cosine + turned * sine


def rotate_back(values, cosine, sine):
    half = values.shape[-1] // 2
    turned = jnp.concatenate([values[..., half:], -values[..., :half]], axis=-1)
    return values * cosine + turned * sine


def norm_parts(values):
    mean_value = jnp.mean(values, axis=-1, keepdims=True)
    centered = values - mean_value
    variance = jnp.mean(centered * centered, axis=-1, keepdims=True)
    inverse = lax.rsqrt(variance + EPS)
    return (centered * inverse, inverse)


def norm_back(grad_normed, unit, inverse, gain):
    scaled = grad_normed * gain
    return inverse * (
        scaled
        - jnp.mean(scaled, axis=-1, keepdims=True)
        - unit * jnp.mean(scaled * unit, axis=-1, keepdims=True)
    )


def block_allowed(segment, segment_pad, start, block, window):
    query_index = start + jnp.arange(block, dtype=jnp.int32)
    key_index = start - window + jnp.arange(block + window, dtype=jnp.int32)
    offset = query_index[:, None] - key_index[None, :]
    same_clip = segment[:, None] == segment_pad[None, :]
    return same_clip & (offset >= 0) & (offset < window)


def pad_front(values, window, fill):
    front = jnp.full((window,) + values.shape[1:], fill, values.dtype)
    return jnp.concatenate([front, values], axis=0)


def attention_forward(queries, keys_rot, values, segment, block, window):
    factor = 1.0 / math.sqrt(queries.shape[-1])
    keys_pad = pad_front(keys_rot, window, 0)
    values_pad = pad_front(values, window, 0)
    segment_pad = pad_front(segment, window, -1)
    allowed = block_allowed(segment, segment_pad, 0, block, window)
    scores = (
        jnp.einsum("qhd,khd->hqk", queries, keys_pad, preferred_element_type=F32) * factor
    )
    masked = jnp.where(allowed[None], scores, -jnp.inf)
    peak = jnp.max(masked, axis=-1, keepdims=True)
    expd = jnp.exp(masked - peak)
    totals = jnp.sum(expd, axis=-1, keepdims=True)
    probs = (expd / totals).astype(BF)
    outputs = jnp.einsum("hqk,khd->qhd", probs, values_pad, preferred_element_type=F32)
    log_totals = peak + jnp.log(totals)
    return (outputs, log_totals)


def attention_backward(
    queries, keys_rot, values, grad_attended, log_totals, segment, block, window
):
    factor = 1.0 / math.sqrt(queries.shape[-1])
    keys_pad = pad_front(keys_rot, window, 0)
    values_pad = pad_front(values, window, 0)
    segment_pad = pad_front(segment, window, -1)
    allowed = block_allowed(segment, segment_pad, 0, block, window)
    scores = (
        jnp.einsum("qhd,khd->hqk", queries, keys_pad, preferred_element_type=F32) * factor
    )
    probs = jnp.where(
        allowed[None], jnp.exp(jnp.where(allowed[None], scores, -jnp.inf) - log_totals), 0.0
    )
    probs_low = probs.astype(BF)
    grad_probs = jnp.einsum("qhd,khd->hqk", grad_attended, values_pad, preferred_element_type=F32)
    delta = jnp.sum(probs * grad_probs, axis=-1, keepdims=True)
    grad_scores = (probs * (grad_probs - delta)).astype(BF)
    grad_queries = (
        jnp.einsum("hqk,khd->qhd", grad_scores, keys_pad, preferred_element_type=F32) * factor
    )
    key_part = (
        jnp.einsum("hqk,qhd->khd", grad_scores, queries, preferred_element_type=F32) * factor
    )
    value_part = jnp.einsum("hqk,qhd->khd", probs_low, grad_attended, preferred_element_type=F32)
    return (grad_queries, key_part[window:], value_part[window:])


def make_links(n_group, n_rep):
    def swap(value, group_bits, rep_bits):
        pairs = [
            (g * n_rep + r, (g ^ group_bits) * n_rep + (r ^ rep_bits))
            for g in range(n_group)
            for r in range(n_rep)
        ]
        return lax.ppermute(value, AXES, pairs)

    return swap


def pick(stacked, index):
    return lax.dynamic_index_in_dim(stacked, index, 0, keepdims=False)


def solution(mesh):
    n_group, n_rep = mesh.shape["group"], mesh.shape["rep"]
    swap = make_links(n_group, n_rep)
    tuned = n_group == 8 and n_rep == 4

    def gather_group(piece, group):
        if not tuned:
            return lax.all_gather(piece, "group", axis=0)
        own = [piece] + [swap(piece, 2 * k, 0) for k in (1, 2, 3)]
        other = [swap(p, 1, 0) for p in own]
        full = jnp.zeros((8,) + piece.shape, piece.dtype)
        for k in range(4):
            for d, p in ((0, own[k]), (1, other[k])):
                at = group ^ (2 * k + d)
                full = lax.dynamic_update_index_in_dim(full, p, at, 0)
        return full

    def gather_all(piece, group, rep):
        if not tuned:
            full = lax.all_gather(piece, AXES, axis=0)
            return full.reshape((n_group, n_rep) + piece.shape)
        base = [piece] + [swap(piece, 2 * k, 0) for k in (1, 2, 3)]
        along_x = [swap(p, 1, 0) for p in base]
        along_y = [swap(p, 0, 2) for p in base]
        both = [swap(along_x[k], 0, 2) if k < 2 else swap(along_y[k], 1, 0) for k in range(4)]
        y = rep // 2
        half = jnp.zeros((8, 2) + piece.shape, piece.dtype)
        zeros = (0,) * piece.ndim
        for k in range(4):
            for dx, dy, p in ((0, 0, base[k]), (1, 0, along_x[k]), (0, 1, along_y[k]), (1, 1, both[k])):
                at = (group ^ (2 * k + dx), y ^ dy) + zeros
                half = lax.dynamic_update_slice(half, p[None, None], at)
        other = swap(half, 0, 1)
        even = rep % 2 == 0
        full = jnp.stack([jnp.where(even, half, other), jnp.where(even, other, half)], axis=2)
        return full.reshape((8, 4) + piece.shape)

    def gather_rep(piece):
        low = jnp.concatenate([piece, swap(piece, 0, 2)], axis=0)
        return jnp.concatenate([low, swap(low, 0, 1)], axis=0)

    def scatter_rep(blocks):
        half = blocks.shape[0] // 2
        low = blocks[:half].astype(F32) + swap(blocks[half:], 0, 1).astype(F32)
        quarter = half // 2
        return low[:quarter] + swap(low[quarter:].astype(BF), 0, 2).astype(F32)

    def scatter_group(grads, group):
        if not tuned:
            return lax.psum_scatter(grads, "group", scatter_dimension=0, tiled=False).astype(F32)
        z, x = group // 2, group % 2
        blocks = grads.reshape((4, 2) + grads.shape[1:])
        there = lax.dynamic_index_in_dim(blocks, x ^ 1, 1, keepdims=False)
        here = lax.dynamic_index_in_dim(blocks, x, 1, keepdims=False)
        came = swap(there, 1, 0)

        def part(k):
            return pick(here, z ^ k).astype(F32) + pick(came, z ^ k).astype(F32)

        arrived = [swap(part(k).astype(BF), 2 * k, 0) for k in (1, 2, 3)]
        return part(0) + (
            arrived[0].astype(F32) + arrived[1].astype(F32) + arrived[2].astype(F32)
        )

    def whole_rep(piece, rep):
        piece = piece.astype(BF)
        if not tuned:
            return lax.all_gather(piece, "rep", axis=0).astype(F32)
        low = jnp.stack([piece, swap(piece, 0, 2)])
        high = swap(low, 0, 1)
        rel = jnp.stack([low[0], high[0], low[1], high[1]])
        return jnp.stack([pick(rel, rep ^ j) for j in range(4)]).astype(F32)

    def scatter_attn(grads, group, rep):
        rows, cols = grads.shape
        if not tuned:
            part = lax.psum_scatter(grads, "group", scatter_dimension=0, tiled=True)
            return lax.psum(part, "rep").astype(F32)
        x, y, core = group % 2, rep // 2, rep % 2
        z = group // 2
        half = cols // 2
        there = lax.dynamic_slice_in_dim(grads, (core ^ 1) * half, half, 1)
        here = lax.dynamic_slice_in_dim(grads, core * half, half, 1)
        chip = (here.astype(F32) + swap(there, 0, 1).astype(F32)).astype(BF)
        chip = chip.reshape(4, 2, rows // 8, 2, half // 2)
        quarter = half // 4

        def add(a, b):
            return (a.astype(F32) + b.astype(F32)).astype(BF)

        def over_x(v):
            return add(
                lax.dynamic_index_in_dim(v, x, 1, keepdims=False),
                swap(lax.dynamic_index_in_dim(v, x ^ 1, 1, keepdims=False), 1, 0),
            )

        def over_y(v):
            return add(
                lax.dynamic_slice_in_dim(v, y * quarter, quarter, v.ndim - 1),
                swap(lax.dynamic_slice_in_dim(v, (y ^ 1) * quarter, quarter, v.ndim - 1), 0, 2),
            )

        first = over_y(over_x(chip[:, :, :, 0]))
        second = over_x(over_y(chip[:, :, :, 1]))
        column = jnp.stack([first, second], axis=2)
        arrived = [swap(pick(column, z ^ k), 2 * k, 0).astype(F32) for k in (1, 2, 3)]
        mine = pick(column, z).astype(F32) + (arrived[0] + arrived[1] + arrived[2])
        full = whole_rep(mine, rep)
        full = full.reshape(2, 2, rows // 8, 2, quarter)
        return full.transpose(2, 1, 3, 0, 4).reshape(rows // 8, cols)

    def sum_all(value):
        if not tuned:
            return lax.psum(value, AXES)
        for bits in ((0, 1), (0, 2), (1, 0), (2, 0), (4, 0)):
            value = value + swap(value, *bits)
        return value

    def shards(
        inputs,
        lengths,
        ln1_gain,
        ln1_bias,
        w_qkv,
        w_out,
        scale_attn,
        ln2_gain,
        ln2_bias,
        w_gate,
        w_up,
        w_down,
        scale_mlp,
        grad_out,
    ):
        count, width = inputs.shape
        head_width = width // HEADS
        group, rep = lax.axis_index("group"), lax.axis_index("rep")
        rows = w_qkv.shape[0]
        ff = w_gate.shape[1]
        part_ff = ff // n_rep
        vectors = jnp.stack([ln1_gain, ln1_bias, scale_attn, ln2_gain, ln2_bias, scale_mlp], axis=1)
        vectors = jnp.pad(vectors, ((0, 0), (0, 128 - vectors.shape[1])))
        bundle = jnp.concatenate([w_qkv, w_out, vectors], axis=1)
        attn_full = gather_all(bundle, group, rep).reshape(width, -1)
        qkv_full = attn_full[:, : 3 * width]
        out_full = attn_full[:, 3 * width : 4 * width]
        vecs = attn_full[:, 4 * width : 4 * width + 6].T.astype(F32)
        gain_one, bias_one, attn_scale, gain_two, bias_two, mlp_scale = [vecs[i] for i in range(6)]

        def columns(w):
            blocks = w.reshape(rows, n_group, n_rep, ff // (n_group * n_rep))
            return blocks.transpose(2, 0, 1, 3).reshape(n_rep, rows, part_ff)

        pair = jnp.stack([columns(w_gate), columns(w_up)], axis=1)
        came = [pick(pair, rep)] + [swap(pick(pair, rep ^ d), 0, d) for d in (1, 2, 3)]
        came = jnp.stack(came)
        gate_up = jnp.stack([pick(came, rep ^ j) for j in range(n_rep)], axis=1)
        gate_up = gate_up.reshape(2, n_rep * rows, part_ff)
        down_rows = w_down.shape[0]
        gate_all = gather_group(gate_up[0], group).reshape(width, part_ff)
        up_all = gather_group(gate_up[1], group).reshape(width, part_ff)
        down_all = gather_group(w_down, group).reshape(part_ff, width)

        cot_all = gather_rep(grad_out)

        segment, position = clip_layout(lengths[0], count)
        cosine, sine = rotary_tables(position, head_width)
        frames = inputs.astype(F32)
        unit_one, inverse_one = norm_parts(frames)
        normed = (unit_one * gain_one + bias_one).astype(BF)
        projected = jnp.dot(normed, qkv_full, preferred_element_type=F32)
        queries = rotate(
            projected[:, :width].reshape(count, HEADS, head_width), cosine, sine
        ).astype(BF)
        keys_rot = rotate(
            projected[:, width : 2 * width].reshape(count, HEADS, head_width), cosine, sine
        ).astype(BF)
        values = projected[:, 2 * width :].reshape(count, HEADS, head_width).astype(BF)
        attended, log_totals = attention_forward(queries, keys_rot, values, segment, count, WINDOW)
        attended = attended.reshape(count, width).astype(BF)
        branch = jnp.dot(attended, out_full, preferred_element_type=F32)
        middle = frames + attn_scale * branch
        unit_two, inverse_two = norm_parts(middle)
        normed_two = (unit_two * gain_two + bias_two).astype(BF)

        normed_all = gather_rep(normed_two)
        gate = jnp.dot(normed_all, gate_all, preferred_element_type=F32)
        up_value = jnp.dot(normed_all, up_all, preferred_element_type=F32)
        sigmoid_gate = jax.nn.sigmoid(gate)
        silu_gate = gate * sigmoid_gate
        hidden = (silu_gate * up_value).astype(BF)
        mlp_part = jnp.dot(hidden, down_all, preferred_element_type=F32).astype(BF)
        mlp = scatter_rep(mlp_part)
        block_out = (middle + mlp_scale * mlp).astype(BF)
        cotangent = grad_out.astype(F32)
        scale_mlp_grad = jnp.sum(cotangent * mlp, axis=0)
        grad_mlp = (mlp_scale * cot_all.astype(F32)).astype(BF)

        def grad_blocks(a, b):
            out = jnp.einsum("td,te->de", a, b, preferred_element_type=F32).astype(BF)
            return out.reshape(n_group, out.shape[0] // n_group, out.shape[1])

        w_down_part = scatter_group(grad_blocks(hidden, grad_mlp), group)
        grad_hidden = jnp.einsum("td,fd->tf", grad_mlp, down_all, preferred_element_type=F32)
        grad_gate = (
            grad_hidden * up_value * sigmoid_gate * (1.0 + gate * (1.0 - sigmoid_gate))
        ).astype(BF)
        grad_up = (grad_hidden * silu_gate).astype(BF)
        grad_normed_part = jnp.einsum(
            "tf,df->td", grad_gate, gate_all, preferred_element_type=F32
        ) + jnp.einsum("tf,df->td", grad_up, up_all, preferred_element_type=F32)
        grad_normed_two = scatter_rep(grad_normed_part.astype(BF))
        w_gate_part = scatter_group(grad_blocks(normed_all, grad_gate), group)
        w_up_part = scatter_group(grad_blocks(normed_all, grad_up), group)

        def hidden_columns(part):
            full = whole_rep(part, rep)
            full = full.reshape(n_rep, full.shape[1], n_group, ff // (n_group * n_rep))
            return full.transpose(1, 2, 0, 3).reshape(full.shape[1], ff)

        w_gate_grad = hidden_columns(w_gate_part)
        w_up_grad = hidden_columns(w_up_part)
        w_down_grad = whole_rep(w_down_part, rep).reshape(n_rep * down_rows, width)

        ln2_gain_grad = jnp.sum(grad_normed_two * unit_two, axis=0)
        ln2_bias_grad = jnp.sum(grad_normed_two, axis=0)
        grad_middle = cotangent + norm_back(grad_normed_two, unit_two, inverse_two, gain_two)
        scale_attn_grad = jnp.sum(grad_middle * branch, axis=0)
        grad_branch = (attn_scale * grad_middle).astype(BF)
        w_out_part = jnp.einsum("td,te->de", attended, grad_branch, preferred_element_type=F32)
        w_out_grad = scatter_attn(w_out_part.astype(BF), group, rep)
        grad_attended = jnp.einsum(
            "te,de->td", grad_branch, out_full, preferred_element_type=F32
        ).astype(BF)
        grad_queries, grad_keys, grad_values = attention_backward(
            queries,
            keys_rot,
            values,
            grad_attended.reshape(count, HEADS, head_width),
            log_totals,
            segment,
            count,
            WINDOW,
        )
        grad_projected = jnp.concatenate(
            [
                rotate_back(grad_queries, cosine, sine).reshape(count, width),
                rotate_back(grad_keys, cosine, sine).reshape(count, width),
                grad_values.reshape(count, width),
            ],
            axis=1,
        ).astype(BF)
        w_qkv_part = jnp.einsum("td,te->de", normed, grad_projected, preferred_element_type=F32)
        w_qkv_grad = scatter_attn(w_qkv_part.astype(BF), group, rep)
        grad_normed = jnp.einsum(
            "te,de->td", grad_projected, qkv_full, preferred_element_type=F32
        )
        ln1_gain_grad = jnp.sum(grad_normed * unit_one, axis=0)
        ln1_bias_grad = jnp.sum(grad_normed, axis=0)
        input_grad = grad_middle + norm_back(grad_normed, unit_one, inverse_one, gain_one)
        small = sum_all(
            jnp.stack(
                [
                    ln1_gain_grad,
                    ln1_bias_grad,
                    scale_attn_grad,
                    ln2_gain_grad,
                    ln2_bias_grad,
                    scale_mlp_grad,
                ]
            )
        )
        own = width // n_group
        small = lax.dynamic_slice_in_dim(small, group * own, own, 1)
        return (
            block_out,
            input_grad,
            small[0],
            small[1],
            w_qkv_grad,
            w_out_grad,
            small[2],
            small[3],
            small[4],
            w_gate_grad,
            w_up_grad,
            w_down_grad,
            small[5],
        )

    rowed, flat = P(AXES, None), P(AXES)
    in_specs = (
        rowed, rowed, flat, flat, rowed, rowed, flat, flat, flat, rowed, rowed, rowed, flat, rowed,
    )
    own_rows, own_flat = P("group", None), P("group")
    out_specs = (
        rowed, rowed, own_flat, own_flat, own_rows, own_rows, own_flat, own_flat, own_flat,
        own_rows, own_rows, own_rows, own_flat,
    )
    return jax.shard_map(shards, mesh=mesh, in_specs=in_specs, out_specs=out_specs, check_vma=False)
```

```python
import math

import jax
import jax.numpy as jnp
from jax import lax
from jax.experimental import pallas as pl
from jax.experimental.pallas import tpu as pltpu
from jax.sharding import PartitionSpec as P

HEADS = 16
WINDOW = 128
EPS = 1e-05
AXES = ("group", "rep")
BF = jnp.bfloat16
F32 = jnp.float32


def clip_layout(length_row, count):
    clip_ends = jnp.cumsum(length_row)
    clip_starts = clip_ends - length_row
    row_index = jnp.arange(count, dtype=jnp.int32)
    segment = jnp.sum((row_index[:, None] >= clip_ends[None, :]).astype(jnp.int32), axis=1)
    member = (segment[:, None] == jnp.arange(length_row.shape[0], dtype=jnp.int32)[None, :]).astype(
        jnp.int32
    )
    position = row_index - jnp.sum(member * clip_starts[None, :], axis=1)
    return (segment, position)


def rotary_tables(position, width):
    half = width // 2
    freqs = jnp.power(10000.0, -jnp.arange(half, dtype=F32) * (2.0 / width))
    angles = position.astype(F32)[:, None] * freqs[None, :]
    cosine = jnp.concatenate([jnp.cos(angles), jnp.cos(angles)], axis=1)
    sine = jnp.concatenate([jnp.sin(angles), jnp.sin(angles)], axis=1)
    return (cosine[:, None, :], sine[:, None, :])


def rotate(values, cosine, sine):
    half = values.shape[-1] // 2
    turned = jnp.concatenate([-values[..., half:], values[..., :half]], axis=-1)
    return values * cosine + turned * sine


def rotate_back(values, cosine, sine):
    half = values.shape[-1] // 2
    turned = jnp.concatenate([values[..., half:], -values[..., :half]], axis=-1)
    return values * cosine + turned * sine


def norm_parts(values):
    mean_value = jnp.mean(values, axis=-1, keepdims=True)
    centered = values - mean_value
    variance = jnp.mean(centered * centered, axis=-1, keepdims=True)
    inverse = lax.rsqrt(variance + EPS)
    return (centered * inverse, inverse)


def norm_back(grad_normed, unit, inverse, gain):
    scaled = grad_normed * gain
    return inverse * (
        scaled
        - jnp.mean(scaled, axis=-1, keepdims=True)
        - unit * jnp.mean(scaled * unit, axis=-1, keepdims=True)
    )


def block_allowed(segment, segment_pad, start, block, window):
    query_index = start + jnp.arange(block, dtype=jnp.int32)
    key_index = start - window + jnp.arange(block + window, dtype=jnp.int32)
    offset = query_index[:, None] - key_index[None, :]
    same_clip = segment[:, None] == segment_pad[None, :]
    return same_clip & (offset >= 0) & (offset < window)


def pad_front(values, window, fill):
    front = jnp.full((window,) + values.shape[1:], fill, values.dtype)
    return jnp.concatenate([front, values], axis=0)


def attention_forward(queries, keys_rot, values, segment, block, window):
    factor = 1.0 / math.sqrt(queries.shape[-1])
    keys_pad = pad_front(keys_rot, window, 0)
    values_pad = pad_front(values, window, 0)
    segment_pad = pad_front(segment, window, -1)
    allowed = block_allowed(segment, segment_pad, 0, block, window)
    scores = (
        jnp.einsum("qhd,khd->hqk", queries, keys_pad, preferred_element_type=F32) * factor
    )
    masked = jnp.where(allowed[None], scores, -jnp.inf)
    peak = jnp.max(masked, axis=-1, keepdims=True)
    expd = jnp.exp(masked - peak)
    totals = jnp.sum(expd, axis=-1, keepdims=True)
    probs = (expd / totals).astype(BF)
    outputs = jnp.einsum("hqk,khd->qhd", probs, values_pad, preferred_element_type=F32)
    log_totals = peak + jnp.log(totals)
    return (outputs, log_totals)


def attention_backward(
    queries, keys_rot, values, grad_attended, log_totals, segment, block, window
):
    factor = 1.0 / math.sqrt(queries.shape[-1])
    keys_pad = pad_front(keys_rot, window, 0)
    values_pad = pad_front(values, window, 0)
    segment_pad = pad_front(segment, window, -1)
    allowed = block_allowed(segment, segment_pad, 0, block, window)
    scores = (
        jnp.einsum("qhd,khd->hqk", queries, keys_pad, preferred_element_type=F32) * factor
    )
    probs = jnp.where(
        allowed[None], jnp.exp(jnp.where(allowed[None], scores, -jnp.inf) - log_totals), 0.0
    )
    probs_low = probs.astype(BF)
    grad_probs = jnp.einsum("qhd,khd->hqk", grad_attended, values_pad, preferred_element_type=F32)
    delta = jnp.sum(probs * grad_probs, axis=-1, keepdims=True)
    grad_scores = (probs * (grad_probs - delta)).astype(BF)
    grad_queries = (
        jnp.einsum("hqk,khd->qhd", grad_scores, keys_pad, preferred_element_type=F32) * factor
    )
    key_part = (
        jnp.einsum("hqk,qhd->khd", grad_scores, queries, preferred_element_type=F32) * factor
    )
    value_part = jnp.einsum("hqk,qhd->khd", probs_low, grad_attended, preferred_element_type=F32)
    return (grad_queries, key_part[window:], value_part[window:])


def make_links(n_group, n_rep):
    def swap(value, group_bits, rep_bits):
        pairs = [
            (g * n_rep + r, (g ^ group_bits) * n_rep + (r ^ rep_bits))
            for g in range(n_group)
            for r in range(n_rep)
        ]
        return lax.ppermute(value, AXES, pairs)

    return swap


def pick(stacked, index):
    return lax.dynamic_index_in_dim(stacked, index, 0, keepdims=False)


BITS = {"z1": (2, 0), "z2": (4, 0), "z3": (6, 0), "x": (1, 0), "y": (0, 2), "core": (0, 1)}
CONTRACT = {
    "nn": (((1,), (0,)), ((), ())),
    "nt": (((1,), (1,)), ((), ())),
    "tn": (((0,), (0,)), ((), ())),
}
BIG = pltpu.CompilerParams(vmem_limit_bytes=56 << 20)


def work(flops):
    return pl.CostEstimate(flops=int(flops), bytes_accessed=0, transcendentals=0)


ANY = pl.BlockSpec(memory_space=pl.ANY)
SMEM = pl.BlockSpec(memory_space=pltpu.SMEM)


def dot(a, b, form="nn"):
    return lax.dot_general(a, b, CONTRACT[form], preferred_element_type=F32)


def after(value, *done):
    return lax.optimization_barrier((value,) + done)[0]


def window(*values):
    return lax.optimization_barrier(values)


def lane_tables(position, width):
    lane = jnp.arange(2 * width, dtype=jnp.int32)
    index = (lane % (width // 2)).astype(F32)
    freqs = jnp.power(10000.0, -index * (2.0 / width))
    angles = position.astype(F32)[:, None] * freqs[None, :]
    sign = jnp.where(lane % width < width // 2, -1.0, 1.0)
    return jnp.cos(angles), jnp.sin(angles) * sign[None, :]


def sds(shape, dtype):
    return jax.ShapeDtypeStruct(shape, dtype)


def whole(shape):
    return pl.BlockSpec(shape, lambda *_: (0,) * len(shape))


def rotate_lanes(u, cosine, signed_sine, first):
    turned = jnp.where(first, pltpu.roll(u, 96, 1), pltpu.roll(u, 32, 1))
    return u * cosine + turned * signed_sine


PIECES = (
    ((0, 0, 0),),
    ((1, 0, 0), (2, 0, 0), (3, 0, 0)),
    ((0, 1, 0), (0, 0, 1), (0, 1, 1)),
    ((1, 1, 0), (2, 1, 0), (3, 1, 0)),
    ((1, 0, 1), (2, 0, 1), (3, 0, 1)),
    ((1, 1, 1),),
    ((2, 1, 1), (3, 1, 1)),
)


def project_kernel(*refs):
    n = len(PIECES)
    idx, own, came = refs[0], refs[1 : 1 + n], refs[1 + n : 1 + 2 * n]
    x_ref, cos_ref, sin_ref = refs[1 + 2 * n : 4 + 2 * n]
    qkv_ref, normed_ref, w_ref, vec_ref, weights, sems, out_sem = refs[4 + 2 * n :]
    j, steps = pl.program_id(0), pl.num_programs(0)
    block = qkv_ref.shape[1]

    def copies():
        out, count = [], 0
        for core_bit, group in ((0, own), (1, came)):
            for ref, owners in zip(group, PIECES):
                for i, (k, dx, dy) in enumerate(owners):
                    owner = (((idx[0] ^ k) * 2 + (idx[1] ^ dx)) * 2 + (idx[2] ^ dy)) * 2
                    row = pl.multiple_of((owner + (idx[3] ^ core_bit)) * 32, 32)
                    out.append(
                        pltpu.make_async_copy(
                            ref.at[i], weights.at[pl.ds(row, 32), :], sems.at[count]
                        )
                    )
                    count += 1
        return out

    def save():
        return pltpu.make_async_copy(weights, w_ref, out_sem)

    @pl.when(j == 0)
    def _():
        pieces = copies()
        for c in pieces:
            c.start()
        x = x_ref[...].astype(F32)
        centered = x - jnp.mean(x, axis=1, keepdims=True)
        unit = centered * lax.rsqrt(jnp.mean(centered * centered, axis=1, keepdims=True) + EPS)
        for c in pieces:
            c.wait()
        save().start()
        vecs = weights[:, weights.shape[1] - 128 :].astype(F32).T
        vec_ref[...] = vecs[:8]
        normed_ref[...] = (unit * vecs[0:1] + vecs[1:2]).astype(BF)

    p = dot(normed_ref[...], weights[:, pl.ds(pl.multiple_of(j * block, block), block)])
    lane = lax.broadcasted_iota(jnp.int32, (1, 128), 1)
    first = (lane % 64) < 32

    @pl.when(j * 3 < 2 * steps)
    def _():
        for c in range(0, block, 128):
            cols = slice(c, c + 128)
            qkv_ref[:, cols] = rotate_lanes(p[:, cols], cos_ref[...], sin_ref[...], first).astype(BF)

    @pl.when(j * 3 >= 2 * steps)
    def _():
        qkv_ref[...] = p.astype(BF)

    @pl.when(j == steps - 1)
    def _():
        save().wait()


def project(idx, own, came, x, cosine, signed_sine, block=512):
    rows, width = x.shape
    cols = own[0].shape[-1]
    return pl.pallas_call(
        project_kernel,
        grid=(3 * width // block,),
        in_specs=[SMEM] + [ANY] * (2 * len(PIECES)) + [whole((rows, width))] + [whole((rows, 128))] * 2,
        out_specs=[
            pl.BlockSpec((rows, block), lambda j: (0, j)),
            whole((rows, width)),
            ANY,
            whole((8, width)),
        ],
        out_shape=[
            sds((rows, 3 * width), BF),
            sds((rows, width), BF),
            sds((width, cols), BF),
            sds((8, width), F32),
        ],
        scratch_shapes=[
            pltpu.VMEM((width, cols), BF),
            pltpu.SemaphoreType.DMA((32,)),
            pltpu.SemaphoreType.DMA,
        ],
        compiler_params=BIG,
        cost_estimate=work(1e9),
        name="project",
    )(idx, *own, *came, x, cosine, signed_sine)


def set_bias(bias_ref, pos_ref, rows):
    for b in range(rows // WINDOW):
        keys = WINDOW if b == 0 else 2 * WINDOW
        offset = (
            lax.broadcasted_iota(jnp.int32, (WINDOW, keys), 0)
            - lax.broadcasted_iota(jnp.int32, (WINDOW, keys), 1)
            + (keys - WINDOW)
        )
        reach = jnp.minimum(pos_ref[b * WINDOW : (b + 1) * WINDOW, :], WINDOW - 1)
        seen = (offset >= 0) & (offset <= reach)
        bias_ref[b, :, 2 * WINDOW - keys :] = jnp.where(seen, 0.0, -1e30)


def split_heads(u, low):
    zero = jnp.zeros_like(u)
    return jnp.concatenate([jnp.where(low, u, zero), jnp.where(low, zero, u)], axis=0)


def pair_probs(q, k, bias, low):
    q = split_heads(q, low) * jnp.asarray(0.125, BF)
    scores = dot(q, k, "nt") + jnp.concatenate([bias, bias], axis=0)
    e = jnp.exp(scores - jnp.max(scores, axis=1, keepdims=True))
    return q, e * (1.0 / jnp.sum(e, axis=1, keepdims=True))


def attend_kernel(q_ref, k_ref, v_ref, pos_ref, o_ref, bias_ref):
    rows = q_ref.shape[0]

    @pl.when(pl.program_id(0) == 0)
    def _():
        set_bias(bias_ref, pos_ref, rows)

    low = lax.broadcasted_iota(jnp.int32, (1, 128), 1) < 64
    for b in range(rows // WINDOW):
        here = slice(b * WINDOW, (b + 1) * WINDOW)
        keys = slice(max(b - 1, 0) * WINDOW, (b + 1) * WINDOW)
        bias = bias_ref[b, :, 2 * WINDOW - (keys.stop - keys.start) :]
        _, probs = pair_probs(q_ref[here, :], k_ref[keys, :], bias, low)
        out = dot(probs.astype(BF), v_ref[keys, :])
        o_ref[here, :] = jnp.where(low, out[:WINDOW], out[WINDOW:]).astype(BF)


def attend(qkv, position):
    rows, width = qkv.shape[0], qkv.shape[1] // 3
    pairs = width // 128
    cols = lambda part: pl.BlockSpec((rows, 128), lambda j: (0, j + part * pairs))
    return pl.pallas_call(
        attend_kernel,
        grid=(pairs,),
        in_specs=[cols(0), cols(1), cols(2), whole((rows, 1))],
        out_specs=cols(0),
        out_shape=sds((rows, width), BF),
        scratch_shapes=[pltpu.VMEM((rows // WINDOW, WINDOW, 2 * WINDOW), F32)],
        compiler_params=BIG,
        cost_estimate=work(1e9),
        name="attend",
    )(qkv, qkv, qkv, position)


def attend_back_kernel(
    q_ref, k_ref, v_ref, do_ref, pos_ref, cos_ref, sin_ref, dq_ref, dk_ref, dv_ref, bias_ref
):
    rows = q_ref.shape[0]
    blocks = rows // WINDOW

    @pl.when(pl.program_id(0) == 0)
    def _():
        set_bias(bias_ref, pos_ref, rows)

    lane = lax.broadcasted_iota(jnp.int32, (1, 128), 1)
    low, first = lane < 64, (lane % 64) < 32

    def turn_back(u, here):
        return rotate_lanes(u, cos_ref[here, :], -sin_ref[here, :], first).astype(BF)

    dk, dv = [None] * blocks, [None] * blocks
    for b in range(blocks):
        here = slice(b * WINDOW, (b + 1) * WINDOW)
        keys = slice(max(b - 1, 0) * WINDOW, (b + 1) * WINDOW)
        bias = bias_ref[b, :, 2 * WINDOW - (keys.stop - keys.start) :]
        q, probs = pair_probs(q_ref[here, :], k_ref[keys, :], bias, low)
        do = split_heads(do_ref[here, :], low)
        dp = dot(do, v_ref[keys, :], "nt")
        delta = jnp.sum(probs * dp, axis=1, keepdims=True)
        ds = (probs * (dp - delta)).astype(BF)
        dq = dot(ds, k_ref[keys, :]) * 0.125
        dq_ref[here, :] = turn_back(jnp.where(low, dq[:WINDOW], dq[WINDOW:]), here)
        k_part = dot(ds, q, "tn")
        v_part = dot(probs.astype(BF), do, "tn")
        for i, kb in enumerate(range(max(b - 1, 0), b + 1)):
            part = slice(i * WINDOW, (i + 1) * WINDOW)
            dk[kb] = k_part[part] if dk[kb] is None else dk[kb] + k_part[part]
            dv[kb] = v_part[part] if dv[kb] is None else dv[kb] + v_part[part]
    for kb in range(blocks):
        here = slice(kb * WINDOW, (kb + 1) * WINDOW)
        dk_ref[here, :] = turn_back(dk[kb], here)
        dv_ref[here, :] = dv[kb].astype(BF)


def attend_back(qkv, grad, position, cosine, signed_sine):
    rows, width = qkv.shape[0], qkv.shape[1] // 3
    pairs = width // 128
    cols = lambda part: pl.BlockSpec((rows, 128), lambda j: (0, j + part * pairs))
    return pl.pallas_call(
        attend_back_kernel,
        grid=(pairs,),
        in_specs=[cols(0), cols(1), cols(2), cols(0), whole((rows, 1))] + [whole((rows, 128))] * 2,
        out_specs=[cols(0)] * 3,
        out_shape=[sds((rows, width), BF)] * 3,
        scratch_shapes=[pltpu.VMEM((rows // WINDOW, WINDOW, 2 * WINDOW), F32)],
        compiler_params=BIG,
        cost_estimate=work(1e9),
        name="attend_back",
    )(qkv, qkv, qkv, grad, position, cosine, signed_sine)


def mlp_copies(idx, pieces, downs, gate, up, down, sems):
    first, second, last = [], [], []
    half = gate.shape[1] // 2

    def copy(src, dst, group):
        n = len(first) + len(second) + len(last)
        group.append(pltpu.make_async_copy(src, dst, sems.at[n]))

    for i, ref in enumerate(pieces):
        rows = ref.shape[1]
        here = pl.ds(pl.multiple_of(((idx[0] * 2 + idx[1]) ^ i) * rows, rows), rows)
        for c, group in ((0, first), (half, second)):
            cols = pl.ds(c, half)
            for m, target in ((0, gate), (1, up)):
                copy(ref.at[m, :, cols], target.at[here, cols], group)
    for i, ref in enumerate(downs):
        rows = ref.shape[0]
        here = pl.ds(pl.multiple_of(((idx[0] * 2 + idx[1]) ^ i) * rows, rows), rows)
        copy(ref, down.at[here, :], last)
    return first, second, last


def store_split(idx, total, send_ref, keep_ref):
    rows = send_ref.shape[1]
    for k in range(send_ref.shape[0]):
        for ref, x in ((send_ref, 1 - idx[1]), (keep_ref, idx[1])):
            at = pl.multiple_of((2 * k + x) * rows, rows)
            ref[k] = total[pl.ds(at, rows), :].astype(BF)


def mlp_kernel(last_half, *refs):
    idx, pieces, downs = refs[0], refs[1:9], refs[9:17]
    n_parts, g_parts, scale_ref = refs[17:19], refs[19:21], refs[21]
    refs = refs[22:]
    if last_half:
        before_ref, refs = refs[0], refs[1:]
    gg_ref, gu_ref = refs[:2]
    gn_parts, mlp_parts = refs[2:4], refs[4:6]
    refs = refs[6:]
    if last_half:
        send_ref, keep_ref, refs = refs[0], refs[1], refs[2:]
    else:
        total_ref, refs = refs[0], refs[1:]
    w_gate, w_up, w_down, total, n_buf, g_buf, sems = refs
    i, last = pl.program_id(0), pl.num_programs(0) - 1
    block, half = gg_ref.shape[0], pl.num_programs(0) // 2
    first, second, down = mlp_copies(idx, pieces, downs, w_gate, w_up, w_down, sems)

    def wait(copies):
        @pl.when(i == 0)
        def _():
            for c in copies:
                c.wait()

    @pl.when(i == 0)
    def _():
        for c in first + second + down:
            c.start()

    here = pl.ds(pl.multiple_of((i % half) * block, block), block)

    def load(which):
        n_buf[...] = n_parts[which][here, :]
        g_buf[...] = (scale_ref[...] * g_parts[which][here, :].astype(F32)).astype(BF)

    pl.when(i < half)(lambda: load(0))
    pl.when(i >= half)(lambda: load(1))
    n, gm = n_buf[...], g_buf[...]
    width = w_gate.shape[1]
    kept = []
    wait(first)
    for c in range(0, width, width // 2):
        cols = slice(c, c + width // 2)
        gate, up = dot(n, w_gate[:, cols]), dot(n, w_up[:, cols])
        if c == 0:
            wait(second)
        s = 0.5 * jnp.tanh(0.5 * gate) + 0.5
        silu = gate * s
        hidden = (silu * up).astype(BF)
        part = dot(hidden, gm, "tn")

        @pl.when(i == 0)
        def _():
            if last_half:
                total[cols, :] = before_ref[cols, :].astype(F32) + part
            else:
                total[cols, :] = part

        @pl.when(i > 0)
        def _():
            total[cols, :] += part

        kept.append((cols, silu, up * (s + silu * (1.0 - s)), hidden))
    wait(down)
    gn = mlp = None
    for cols, silu, slope, hidden in kept:
        gh = dot(gm, w_down[cols, :], "nt")
        gg = (gh * slope).astype(BF)
        gu = (gh * silu).astype(BF)
        gg_ref[:, cols], gu_ref[:, cols] = gg, gu
        gn_c = dot(gg, w_gate[:, cols], "nt") + dot(gu, w_up[:, cols], "nt")
        mlp_c = dot(hidden, w_down[cols, :])
        gn = gn_c if gn is None else gn + gn_c
        mlp = mlp_c if mlp is None else mlp + mlp_c

    def store(which):
        gn_parts[which][here, :] = gn.astype(BF)
        mlp_parts[which][here, :] = mlp.astype(BF)

    pl.when(i < half)(lambda: store(0))
    pl.when(i >= half)(lambda: store(1))

    @pl.when(i == last)
    def _():
        if last_half:
            store_split(idx, total, send_ref, keep_ref)
        else:
            total_ref[...] = total[...].astype(BF)


def mlp_both(idx, pieces, downs, n_parts, g_parts, scale, before=None, block=512):
    rows, width = n_parts[0].shape
    part = pieces[0].shape[2]
    last_half = before is not None
    row = pl.BlockSpec((block, part), lambda i: (i, 0))
    part_spec, part_shape = whole((rows, width)), sds((rows, width), BF)
    split, total = (4, part // 8, width), (part, width)
    in_specs = [SMEM] + [ANY] * 16 + [part_spec] * 4 + [whole((1, width))]
    out_specs = [row, row] + [part_spec] * 4
    out_shape = [sds((2 * rows, part), BF)] * 2 + [part_shape] * 4
    args = (idx, *pieces, *downs, *n_parts, *g_parts, scale)
    if last_half:
        in_specs.append(whole(total))
        args += (before,)
        out_specs += [whole(split)] * 2
        out_shape += [sds(split, BF)] * 2
    else:
        out_specs.append(whole(total))
        out_shape.append(sds(total, BF))
    return pl.pallas_call(
        lambda *refs: mlp_kernel(last_half, *refs),
        grid=(2 * rows // block,),
        in_specs=in_specs,
        out_specs=out_specs,
        out_shape=out_shape,
        scratch_shapes=[
            pltpu.VMEM((width, part), BF),
            pltpu.VMEM((width, part), BF),
            pltpu.VMEM((part, width), BF),
            pltpu.VMEM(total, F32),
            pltpu.VMEM((block, width), BF),
            pltpu.VMEM((block, width), BF),
            pltpu.SemaphoreType.DMA((40,)),
        ],
        compiler_params=BIG,
        cost_estimate=work(1e9),
        name="mlp_both",
    )(*args)


def weight_grad_kernel(idx, *refs):
    a_refs, b_refs, send_ref, keep_ref = refs[:8], refs[8:10], refs[10], refs[11]
    total = None
    for p in range(4):
        a = jnp.concatenate([a_refs[2 * p][...], a_refs[2 * p + 1][...]], axis=1)
        rows = a.shape[0]
        part = dot(a, b_refs[p // 2][pl.ds((p % 2) * rows, rows), :], "tn")
        total = part if total is None else total + part
    total = total.astype(BF).reshape((2,) + send_ref.shape[1:])
    half = pl.num_programs(0) // 2

    @pl.when(pl.program_id(0) < half)
    def _():
        send_ref[...] = total

    @pl.when(pl.program_id(0) >= half)
    def _():
        keep_ref[...] = total


def weight_grad(idx, a_parts, b_parts):
    tokens, width = a_parts[0].shape
    part = b_parts[0].shape[1]
    rows = width // 8
    split = (4, rows, part)

    def column(which):
        def place(i, s):
            mine = jnp.where(i < 2, 1 - s[1], s[1])
            return (0, 2 * (2 * (i % 2) + which) + mine)

        return pl.BlockSpec((tokens, rows), place)

    return pl.pallas_call(
        weight_grad_kernel,
        grid_spec=pltpu.PrefetchScalarGridSpec(
            num_scalar_prefetch=1,
            grid=(4,),
            in_specs=[column(0), column(1)] * 4
            + [pl.BlockSpec((2 * tokens, part), lambda i, s: (0, 0))] * 2,
            out_specs=[
                pl.BlockSpec((2, rows, part), lambda i, s: (jnp.minimum(i, 1), 0, 0)),
                pl.BlockSpec((2, rows, part), lambda i, s: (jnp.maximum(i - 2, 0), 0, 0)),
            ],
        ),
        out_shape=[sds(split, BF)] * 2,
        compiler_params=BIG,
        cost_estimate=work(1e9),
        name="weight_grad",
    )(idx, *[p for p in a_parts for _ in range(2)], *b_parts)


def attn_grad_kernel(idx, q_in, o_in, dq, dk, dv, do, *refs):
    outs, total = refs[:8], refs[8]
    core = idx[3]
    half = dq.shape[1]
    for n, parts in enumerate((((q_in, dq), (q_in, dk)), ((q_in, dv), (o_in, do)))):
        side = idx[1 + n]
        for c, (a, b) in enumerate(parts):
            product = dot(a[...], b[...], "tn").astype(BF)
            total[:, :, :, :, :, c * half : (c + 1) * half] = product.reshape(4, 2, 2, 2, 32, half)
        for m in range(4):
            to_core = (1 - core) if m < 2 else core
            to_side = (1 - side) if m % 2 == 0 else side
            for k in range(4):
                for other in range(2):
                    x, y = (to_side, other) if n == 0 else (other, to_side)
                    outs[4 * n + m][k, other] = total[k, x, y, to_core]


def attn_grad(idx, q_in, o_in, dq, dk, dv, do):
    width = q_in.shape[1]
    vmem = pl.BlockSpec(memory_space=pltpu.VMEM)
    return pl.pallas_call(
        attn_grad_kernel,
        in_specs=[SMEM] + [vmem] * 6,
        out_specs=[vmem] * 8,
        out_shape=[sds((4, 2, 32, 2 * width), BF)] * 8,
        scratch_shapes=[pltpu.VMEM((4, 2, 2, 2, 32, 2 * width), BF)],
        compiler_params=BIG,
        cost_estimate=work(1e9),
        name="attn_grad",
    )(idx, q_in, o_in, dq, dk, dv, do)


def place_kernel(idx, own, y_ref, core_ref, *outs):
    rep = idx[2] * 2 + idx[3]
    for ref, d in ((own, 0), (y_ref, 2), (core_ref.at[0], 1), (core_ref.at[1], 3)):
        low = 0
        for out in outs:
            cols = out.shape[2]
            out[pl.ds(rep ^ d, 1)] = ref[:, low : low + cols].astype(F32)[None]
            low += cols


def place_rows(idx, own, other_y, other_core, widths):
    rows = own.shape[0]
    vmem = pl.BlockSpec(memory_space=pltpu.VMEM)
    outs = pl.pallas_call(
        place_kernel,
        in_specs=[SMEM, vmem, vmem, vmem],
        out_specs=[vmem] * len(widths),
        out_shape=[sds((4, rows, w), F32) for w in widths],
        compiler_params=BIG,
        cost_estimate=work(1e9),
        name="place_rows",
    )(idx, own, other_y, other_core)
    return [out.reshape(4 * rows, -1) for out in outs]


def place_columns_kernel(idx, up_ref, gate_ref, y_ref, core_ref, up_out, gate_out):
    rep = idx[2] * 2 + idx[3]
    for m, (own, out) in enumerate(((up_ref, up_out), (gate_ref, gate_out))):
        parts = ((own, 0), (y_ref.at[m], 2), (core_ref.at[0, m], 1), (core_ref.at[1, m], 3))
        for ref, d in parts:
            for g in range(own.shape[1] // 128):
                at = pl.multiple_of((g * 4 + (rep ^ d)) * 128, 128)
                out[:, pl.ds(at, 128)] = ref[:, g * 128 : (g + 1) * 128].astype(F32)


def place_columns(idx, up, gate, other_y, other_core):
    rows, cols = up.shape
    vmem = pl.BlockSpec(memory_space=pltpu.VMEM)
    return pl.pallas_call(
        place_columns_kernel,
        in_specs=[SMEM] + [vmem] * 4,
        out_specs=[vmem] * 2,
        out_shape=[sds((rows, 4 * cols), F32)] * 2,
        compiler_params=BIG,
        cost_estimate=work(1e9),
        name="place_columns",
    )(idx, up, gate, other_y, other_core)


def share_kernel(idx, gate_ref, up_ref, here_ref, there_ref):
    rep = idx[2] * 2 + idx[3]
    for d in range(4):
        out = (here_ref, there_ref)[d // 2]
        for m, ref in enumerate((gate_ref, up_ref)):
            for g in range(out.shape[3] // 128):
                at = pl.multiple_of((g * 4 + (rep ^ d)) * 128, 128)
                out[d % 2, m, :, g * 128 : (g + 1) * 128] = ref[:, pl.ds(at, 128)]


def share(idx, w_gate, w_up):
    rows, ff = w_gate.shape
    vmem = pl.BlockSpec(memory_space=pltpu.VMEM)
    return pl.pallas_call(
        share_kernel,
        in_specs=[SMEM, vmem, vmem],
        out_specs=[vmem] * 2,
        out_shape=[sds((2, 2, rows, ff // 4), BF)] * 2,
        compiler_params=BIG,
        cost_estimate=work(1e9),
        name="share",
    )(idx, w_gate, w_up)


def join_kernel(idx, own, y_ref, core_ref, out_ref):
    rep = idx[2] * 2 + idx[3]
    rows = own.shape[2]
    parts = ((own.at[0], 0), (y_ref.at[0], 2), (core_ref.at[0], 1), (core_ref.at[1], 3))
    for ref, d in parts:
        at = pl.multiple_of((rep ^ d) * rows, rows)
        out_ref[:, pl.ds(at, rows), :] = ref[...]


def join(idx, own, other_y, other_core):
    rows, part = own.shape[2:]
    vmem = pl.BlockSpec(memory_space=pltpu.VMEM)
    return pl.pallas_call(
        join_kernel,
        in_specs=[SMEM] + [vmem] * 3,
        out_specs=vmem,
        out_shape=sds((2, 4 * rows, part), BF),
        compiler_params=BIG,
        cost_estimate=work(1e9),
        name="join",
    )(idx, own, other_y, other_core)


def tuned(mesh):
    swap_bits = make_links(8, 4)

    def swap(value, name):
        return swap_bits(value, *BITS[name])

    def add(a, b):
        return (a.astype(F32) + b.astype(F32)).astype(BF)

    def along(value, index, axis):
        return lax.dynamic_index_in_dim(value, index, axis, keepdims=False)

    def shards(
        inputs,
        lengths,
        ln1_gain,
        ln1_bias,
        w_qkv,
        w_out,
        scale_attn,
        ln2_gain,
        ln2_bias,
        w_gate,
        w_up,
        w_down,
        scale_mlp,
        grad_out,
    ):
        count, width = inputs.shape
        head_width = width // HEADS
        group, rep = lax.axis_index("group"), lax.axis_index("rep")
        z, x, y, core = group // 2, group % 2, rep // 2, rep % 2
        idx = jnp.stack([z, x, y, core]).astype(jnp.int32)

        vectors = jnp.stack([ln1_gain, ln1_bias, scale_attn, ln2_gain, ln2_bias, scale_mlp], axis=1)
        vectors = jnp.pad(vectors, ((0, 0), (0, 122)))
        bundle = jnp.concatenate([w_qkv, w_out, vectors], axis=1)[None]
        share_here, share_there = share(idx, w_gate, w_up)
        bundle, share_there = window(bundle, share_there)
        from_z = [swap(bundle, "z1"), swap(bundle, "z2")]
        x_own, share_y = swap(bundle, "x"), swap(share_there, "y")
        y_own = swap(bundle, "y")

        segment, position = clip_layout(lengths[0], count)
        cosine, sine = lane_tables(position, head_width)
        position = position[:, None]

        *from_z, x_own, y_own, share_y, share_here, bundle, w_down = window(
            *from_z, x_own, y_own, share_y, share_here, bundle, w_down
        )
        from_z.append(swap(bundle, "z3"))
        share_core = swap(jnp.stack([share_here[1], share_y[1]]), "core")
        gu0 = join(idx, share_here, share_y, share_core)
        both_own, dnx0, came_own = swap(x_own, "y"), swap(w_down, "x"), swap(bundle, "core")
        *from_z, gu0, both_own, x_own, y_own, dnx0, came_own, cosine, sine, position = window(
            *from_z, gu0, both_own, x_own, y_own, dnx0, came_own, cosine, sine, position
        )
        rest = jnp.concatenate(from_z)
        owns = jnp.concatenate([x_own, y_own, both_own])
        rest, owns = window(rest, owns)
        x_rest, y_rest = swap(rest, "x"), swap(rest, "y")
        gu1, gu2, gux0 = swap(gu0, "z1"), swap(gu0, "z2"), swap(gu0, "x")

        x_rest, y_rest, gu1, gu2, gux0, w_down = window(x_rest, y_rest, gu1, gu2, gux0, w_down)
        y_one, x_two, w_down, rest = window(x_rest[:1], y_rest[1:], w_down, rest)
        both_one, both_two = swap(y_one, "y"), swap(x_two, "x")
        dn1, dn2 = swap(w_down, "z1"), swap(w_down, "z2")
        came_rest = swap(rest, "core")

        have = [bundle, rest, owns, x_rest, y_rest, both_one, both_two]
        gu0, gu1, gu2, dn1, dn2, grad_out, came_rest, *have = window(
            gu0, gu1, gu2, dn1, dn2, grad_out, came_rest, *have
        )
        came = [came_own, came_rest] + [swap(p, "core") for p in have[2:]]
        gu3, gux1, go_y = swap(gu0, "z3"), swap(gu1, "x"), swap(grad_out, "y")
        dnx1, dnx2 = swap(dn1, "x"), swap(dn2, "x")
        *came, cosine, sine, position = window(*came, cosine, sine, position)

        qkv, normed, w_attn, vecs = project(idx, have, came, inputs, cosine, sine)
        qkv, gux1, gu2, dnx1, dnx2, gu3, w_down = window(
            qkv, gux1, gu2, dnx1, dnx2, gu3, w_down
        )
        gux2, dn3 = swap(gu2, "x"), swap(w_down, "z3")
        gux3 = swap(gu3, "x")
        attended = attend(qkv, position)
        attended, gux2, go_y, dn3 = window(attended, gux2, go_y, dn3)
        gain_one, bias_one, attn_scale, gain_two, bias_two, mlp_scale = [vecs[i] for i in range(6)]
        out_full = w_attn[:, 3 * width : 4 * width]
        dnx3 = swap(dn3, "x")
        frames = inputs.astype(F32)
        branch = jnp.dot(attended, out_full, preferred_element_type=F32)
        middle = frames + attn_scale * branch
        unit_two, inverse_two = norm_parts(middle)
        n_own = (unit_two * gain_two + bias_two).astype(BF)
        n_own, gux3, dnx3, grad_out, go_y = window(n_own, gux3, dnx3, grad_out, go_y)

        n_y, n_core = swap(n_own, "y"), swap(n_own, "core")
        go_core = swap(grad_out, "core")
        n_core, go_core = window(n_core, go_core)
        go_yc = swap(go_y, "core")
        pieces = (gu0, gux0, gu1, gux1, gu2, gux2, gu3, gux3)
        downs = (w_down, dnx0, dn1, dnx1, dn2, dnx2, dn3, dnx3)
        scale = mlp_scale[None]
        gg_a, gu_a, gn_own, gn_core, mlp_own, mlp_core, total = mlp_both(
            idx, pieces, downs, (n_own, n_core), (grad_out, go_core), scale
        )
        n_y, go_y, go_yc, gn_core = window(n_y, go_y, go_yc, gn_core)
        n_yc = swap(n_y, "core")
        n_y, n_yc = window(n_y, n_yc)
        gn_core, mlp_core = swap(gn_core, "core"), swap(mlp_core, "core")
        gg_b, gu_b, gn_y, gn_yc, mlp_y, mlp_yc, down_send, down_keep = mlp_both(
            idx, pieces, downs, (n_y, n_yc), (go_y, go_yc), scale, total
        )
        gn_y, gn_yc, gn_core, mlp_core, down_send = window(gn_y, gn_yc, gn_core, mlp_core, down_send)
        down_x = swap(down_send, "x")
        gn_yc = swap(gn_yc, "core")
        gn_y, gn_yc = window(gn_y, gn_yc)
        gn_send, gu_b, mlp_yc = window(add(gn_y, gn_yc), gu_b, mlp_yc)
        gn_y = swap(gn_send, "y")
        mlp_yc = swap(mlp_yc, "core")

        def z_pairs(keep, came, bit):
            shape = (2, 2) + keep.shape[1:]
            keep, came = along(keep.reshape(shape), bit, 1), along(came.reshape(shape), bit, 1)
            return keep.astype(F32) + came.astype(F32)

        def z_near(keep, came):
            return z_pairs(keep, came, 1 - z % 2).astype(BF)

        def z_far(keep, came, near):
            return (
                pick(z_pairs(keep, came, z % 2), 1 - z // 2)
                + pick(near, 1 - z // 2).astype(F32)
            ).astype(BF)

        def z_total(keep, came, near, far):
            mine = pick(z_pairs(keep, came, z % 2), z // 2) + pick(near, z // 2).astype(F32)
            return (mine + far.astype(F32)).astype(BF)

        n_all = (n_own, n_core, n_y, n_yc)
        up_send, up_keep = weight_grad(idx, n_all, (gu_a, gu_b))
        gate_send, gate_keep = weight_grad(idx, n_all, (after(gg_a, up_send), gg_b))
        down_x, gate_send, up_send, mlp_yc = window(down_x, gate_send, up_send, mlp_yc)
        down_near = z_near(down_keep, down_x)
        mlp_send = add(mlp_y, mlp_yc)
        down_near, gn_y, mlp_send, up_send = window(down_near, gn_y, mlp_send, up_send)
        up_x, mlp_y, down_near = swap(up_send, "x"), swap(mlp_send, "y"), swap(down_near, "z1")

        cotangent = grad_out.astype(F32)
        grad_normed_two = gn_own.astype(F32) + gn_core.astype(F32) + gn_y.astype(F32)
        ln2_gain_grad = jnp.sum(grad_normed_two * unit_two, axis=0)
        ln2_bias_grad = jnp.sum(grad_normed_two, axis=0)
        grad_middle = cotangent + norm_back(grad_normed_two, unit_two, inverse_two, gain_two)
        scale_attn_grad = jnp.sum(grad_middle * branch, axis=0)
        grad_branch = (attn_scale * grad_middle).astype(BF)
        grad_attended = dot(grad_branch, out_full, "nt").astype(BF)
        grad_attended, gate_send = window(grad_attended, gate_send)
        gate_x = swap(gate_send, "x")

        dq, dk, dv = attend_back(qkv, grad_attended, position, cosine, sine)
        dq, mlp_y, up_x, down_near = window(dq, mlp_y, up_x, down_near)
        up_near, down_far = z_near(up_keep, up_x), z_far(down_keep, down_x, down_near)
        up_near, down_far, dq = window(up_near, down_far, dq)
        up_near, down_far = swap(up_near, "z1"), swap(down_far, "z2")
        grads = attn_grad(idx, normed, attended, dq, dk, dv, grad_branch)
        dq, dk, dv, gate_x, up_near, down_far, *grads = window(
            dq, dk, dv, gate_x, up_near, down_far, *grads
        )
        a_send, a_send_here, a_keep, a_keep_here, b_send, b_send_here, b_keep, b_keep_here = grads

        a_core, b_core = swap(a_send, "core"), swap(b_send, "core")
        gate_near = z_near(gate_keep, gate_x)
        down_mine = z_total(down_keep, down_x, down_near, down_far)
        up_far = z_far(up_keep, up_x, up_near)
        a_core, b_core, gate_near, up_far, down_mine, a_send_here, b_send_here = window(
            a_core, b_core, gate_near, up_far, down_mine, a_send_here, b_send_here
        )
        a_core_here, b_core_here = swap(a_send_here, "core"), swap(b_send_here, "core")
        a_away, b_away, a_core_here, b_core_here, dq, dk, dv, gate_near, up_far = window(
            add(a_keep, a_core),
            add(b_keep, b_core),
            a_core_here,
            b_core_here,
            dq,
            dk,
            dv,
            gate_near,
            up_far,
        )
        a_x, b_y = swap(a_away, "x"), swap(b_away, "y")
        gate_near, up_far = swap(gate_near, "z1"), swap(up_far, "z2")
        w_qkv_full = w_attn[:, : 3 * width]
        grad_normed = (
            dot(dq, w_qkv_full[:, :width], "nt")
            + dot(dk, w_qkv_full[:, width : 2 * width], "nt")
            + dot(dv, w_qkv_full[:, 2 * width :], "nt")
        )
        grad_normed, gate_near, up_far = window(grad_normed, gate_near, up_far)
        gate_far = swap(z_far(gate_keep, gate_x, gate_near), "z2")
        up_mine = z_total(up_keep, up_x, up_near, up_far)
        unit_one, inverse_one = norm_parts(frames)
        ln1_gain_grad = jnp.sum(grad_normed * unit_one, axis=0)
        ln1_bias_grad = jnp.sum(grad_normed, axis=0)
        input_grad = grad_middle + norm_back(grad_normed, unit_one, inverse_one, gain_one)
        mlp = mlp_own.astype(F32) + mlp_core.astype(F32) + mlp_y.astype(F32)
        block_out = (middle + mlp_scale * mlp).astype(BF)
        scale_mlp_grad = jnp.sum(cotangent * mlp, axis=0)
        small = jnp.stack(
            [
                ln1_gain_grad,
                ln1_bias_grad,
                scale_attn_grad,
                ln2_gain_grad,
                ln2_bias_grad,
                scale_mlp_grad,
            ]
        )
        small = small + swap(small, "core")
        a_x, b_y, small, up_mine, gate_far = window(a_x, b_y, small, up_mine, gate_far)
        a_half, b_half = (a_keep_here, a_core_here, a_x), (b_keep_here, b_core_here, b_y)

        def add_three(parts, index):
            p = [along(v, index, 1).astype(F32) for v in parts]
            return p[0] + p[1] + p[2]

        a_away, b_away = add_three(a_half, y ^ 1).astype(BF), add_three(b_half, x ^ 1).astype(BF)
        a_away, b_away, small, down_mine = window(a_away, b_away, small, down_mine)
        a_y, b_x, down_y = swap(a_away, "y"), swap(b_away, "x"), swap(down_mine, "y")
        small = small + swap(small, "x")
        gate_mine = z_total(gate_keep, gate_x, gate_near, gate_far)
        both_mine = jnp.stack([up_mine, gate_mine])
        a_y, b_x, small, down_y, down_mine, both_mine = window(
            a_y, b_x, small, down_y, down_mine, both_mine
        )
        column = jnp.concatenate(
            [
                (add_three(a_half, y) + a_y.astype(F32)).astype(BF),
                (add_three(b_half, x) + b_x.astype(F32)).astype(BF),
            ],
            axis=-1,
        )
        sends = [pick(column, z ^ k) for k in (1, 2, 3)]
        *sends, small = window(*sends, small)
        got = [swap(v, n) for v, n in zip(sends, ("z1", "z2", "z3"))]
        both_y = swap(both_mine, "y")
        small = small + swap(small, "z1")
        down_both = jnp.stack([down_mine, down_y])
        *got, small, both_y, down_both = window(*got, small, both_y, down_both)
        mine = (
            pick(column, z).astype(F32)
            + (got[0].astype(F32) + got[1].astype(F32) + got[2].astype(F32))
        ).astype(BF)
        mine, small, both_y, down_both = window(mine, small, both_y, down_both)
        other, down_core = swap(mine, "y"), swap(down_both, "core")
        both_pair = jnp.stack([both_mine, both_y])
        small = small + swap(small, "z2")
        other, small, both_pair, down_core = window(other, small, both_pair, down_core)
        mine_core = swap(jnp.stack([mine, other]), "core")
        both_core = swap(both_pair, "core")
        small = small + swap(small, "y")
        (w_down_grad,) = place_rows(idx, down_mine, down_y, down_core, (width,))
        w_up_grad, w_gate_grad = place_columns(
            idx, both_mine[0], both_mine[1], both_y, both_core
        )
        w_qkv_grad, w_out_grad = place_rows(idx, mine, other, mine_core, (3 * width, width))
        small = lax.dynamic_slice_in_dim(small, group * (width // 8), width // 8, 1)
        return (
            block_out,
            input_grad,
            small[0],
            small[1],
            w_qkv_grad,
            w_out_grad,
            small[2],
            small[3],
            small[4],
            w_gate_grad,
            w_up_grad,
            w_down_grad,
            small[5],
        )

    return shards


def plain(mesh):
    n_group, n_rep = mesh.shape["group"], mesh.shape["rep"]
    swap = make_links(n_group, n_rep)

    def gather_group(piece, group):
        return lax.all_gather(piece, "group", axis=0)
    def gather_all(piece, group, rep):
        full = lax.all_gather(piece, AXES, axis=0)
        return full.reshape((n_group, n_rep) + piece.shape)

    def gather_rep(piece):
        low = jnp.concatenate([piece, swap(piece, 0, 2)], axis=0)
        return jnp.concatenate([low, swap(low, 0, 1)], axis=0)

    def scatter_rep(blocks):
        half = blocks.shape[0] // 2
        low = blocks[:half].astype(F32) + swap(blocks[half:], 0, 1).astype(F32)
        quarter = half // 2
        return low[:quarter] + swap(low[quarter:].astype(BF), 0, 2).astype(F32)

    def scatter_group(grads, group):
        return lax.psum_scatter(grads, "group", scatter_dimension=0, tiled=False).astype(F32)

    def whole_rep(piece, rep):
        piece = piece.astype(BF)
        return lax.all_gather(piece, "rep", axis=0).astype(F32)

    def scatter_attn(grads, group, rep):
        part = lax.psum_scatter(grads, "group", scatter_dimension=0, tiled=True)
        return lax.psum(part, "rep").astype(F32)

    def sum_all(value):
        return lax.psum(value, AXES)

    def shards(
        inputs,
        lengths,
        ln1_gain,
        ln1_bias,
        w_qkv,
        w_out,
        scale_attn,
        ln2_gain,
        ln2_bias,
        w_gate,
        w_up,
        w_down,
        scale_mlp,
        grad_out,
    ):
        count, width = inputs.shape
        head_width = width // HEADS
        group, rep = lax.axis_index("group"), lax.axis_index("rep")
        rows = w_qkv.shape[0]
        ff = w_gate.shape[1]
        part_ff = ff // n_rep
        vectors = jnp.stack([ln1_gain, ln1_bias, scale_attn, ln2_gain, ln2_bias, scale_mlp], axis=1)
        vectors = jnp.pad(vectors, ((0, 0), (0, 128 - vectors.shape[1])))
        bundle = jnp.concatenate([w_qkv, w_out, vectors], axis=1)
        attn_full = gather_all(bundle, group, rep).reshape(width, -1)
        qkv_full = attn_full[:, : 3 * width]
        out_full = attn_full[:, 3 * width : 4 * width]
        vecs = attn_full[:, 4 * width : 4 * width + 6].T.astype(F32)
        gain_one, bias_one, attn_scale, gain_two, bias_two, mlp_scale = [vecs[i] for i in range(6)]

        def columns(w):
            blocks = w.reshape(rows, n_group, n_rep, ff // (n_group * n_rep))
            return blocks.transpose(2, 0, 1, 3).reshape(n_rep, rows, part_ff)

        pair = jnp.stack([columns(w_gate), columns(w_up)], axis=1)
        came = [pick(pair, rep)] + [swap(pick(pair, rep ^ d), 0, d) for d in (1, 2, 3)]
        came = jnp.stack(came)
        gate_up = jnp.stack([pick(came, rep ^ j) for j in range(n_rep)], axis=1)
        gate_up = gate_up.reshape(2, n_rep * rows, part_ff)
        down_rows = w_down.shape[0]
        gate_all = gather_group(gate_up[0], group).reshape(width, part_ff)
        up_all = gather_group(gate_up[1], group).reshape(width, part_ff)
        down_all = gather_group(w_down, group).reshape(part_ff, width)

        cot_all = gather_rep(grad_out)

        segment, position = clip_layout(lengths[0], count)
        cosine, sine = rotary_tables(position, head_width)
        frames = inputs.astype(F32)
        unit_one, inverse_one = norm_parts(frames)
        normed = (unit_one * gain_one + bias_one).astype(BF)
        projected = jnp.dot(normed, qkv_full, preferred_element_type=F32)
        queries = rotate(
            projected[:, :width].reshape(count, HEADS, head_width), cosine, sine
        ).astype(BF)
        keys_rot = rotate(
            projected[:, width : 2 * width].reshape(count, HEADS, head_width), cosine, sine
        ).astype(BF)
        values = projected[:, 2 * width :].reshape(count, HEADS, head_width).astype(BF)
        attended, log_totals = attention_forward(queries, keys_rot, values, segment, count, WINDOW)
        attended = attended.reshape(count, width).astype(BF)
        branch = jnp.dot(attended, out_full, preferred_element_type=F32)
        middle = frames + attn_scale * branch
        unit_two, inverse_two = norm_parts(middle)
        normed_two = (unit_two * gain_two + bias_two).astype(BF)

        normed_all = gather_rep(normed_two)
        gate = jnp.dot(normed_all, gate_all, preferred_element_type=F32)
        up_value = jnp.dot(normed_all, up_all, preferred_element_type=F32)
        sigmoid_gate = jax.nn.sigmoid(gate)
        silu_gate = gate * sigmoid_gate
        hidden = (silu_gate * up_value).astype(BF)
        mlp_part = jnp.dot(hidden, down_all, preferred_element_type=F32).astype(BF)
        mlp = scatter_rep(mlp_part)
        block_out = (middle + mlp_scale * mlp).astype(BF)
        cotangent = grad_out.astype(F32)
        scale_mlp_grad = jnp.sum(cotangent * mlp, axis=0)
        grad_mlp = (mlp_scale * cot_all.astype(F32)).astype(BF)

        def grad_blocks(a, b):
            out = jnp.einsum("td,te->de", a, b, preferred_element_type=F32).astype(BF)
            return out.reshape(n_group, out.shape[0] // n_group, out.shape[1])

        w_down_part = scatter_group(grad_blocks(hidden, grad_mlp), group)
        grad_hidden = jnp.einsum("td,fd->tf", grad_mlp, down_all, preferred_element_type=F32)
        grad_gate = (
            grad_hidden * up_value * sigmoid_gate * (1.0 + gate * (1.0 - sigmoid_gate))
        ).astype(BF)
        grad_up = (grad_hidden * silu_gate).astype(BF)
        grad_normed_part = jnp.einsum(
            "tf,df->td", grad_gate, gate_all, preferred_element_type=F32
        ) + jnp.einsum("tf,df->td", grad_up, up_all, preferred_element_type=F32)
        grad_normed_two = scatter_rep(grad_normed_part.astype(BF))
        w_gate_part = scatter_group(grad_blocks(normed_all, grad_gate), group)
        w_up_part = scatter_group(grad_blocks(normed_all, grad_up), group)

        def hidden_columns(part):
            full = whole_rep(part, rep)
            full = full.reshape(n_rep, full.shape[1], n_group, ff // (n_group * n_rep))
            return full.transpose(1, 2, 0, 3).reshape(full.shape[1], ff)

        w_gate_grad = hidden_columns(w_gate_part)
        w_up_grad = hidden_columns(w_up_part)
        w_down_grad = whole_rep(w_down_part, rep).reshape(n_rep * down_rows, width)

        ln2_gain_grad = jnp.sum(grad_normed_two * unit_two, axis=0)
        ln2_bias_grad = jnp.sum(grad_normed_two, axis=0)
        grad_middle = cotangent + norm_back(grad_normed_two, unit_two, inverse_two, gain_two)
        scale_attn_grad = jnp.sum(grad_middle * branch, axis=0)
        grad_branch = (attn_scale * grad_middle).astype(BF)
        w_out_part = jnp.einsum("td,te->de", attended, grad_branch, preferred_element_type=F32)
        w_out_grad = scatter_attn(w_out_part.astype(BF), group, rep)
        grad_attended = jnp.einsum(
            "te,de->td", grad_branch, out_full, preferred_element_type=F32
        ).astype(BF)
        grad_queries, grad_keys, grad_values = attention_backward(
            queries,
            keys_rot,
            values,
            grad_attended.reshape(count, HEADS, head_width),
            log_totals,
            segment,
            count,
            WINDOW,
        )
        grad_projected = jnp.concatenate(
            [
                rotate_back(grad_queries, cosine, sine).reshape(count, width),
                rotate_back(grad_keys, cosine, sine).reshape(count, width),
                grad_values.reshape(count, width),
            ],
            axis=1,
        ).astype(BF)
        w_qkv_part = jnp.einsum("td,te->de", normed, grad_projected, preferred_element_type=F32)
        w_qkv_grad = scatter_attn(w_qkv_part.astype(BF), group, rep)
        grad_normed = jnp.einsum(
            "te,de->td", grad_projected, qkv_full, preferred_element_type=F32
        )
        ln1_gain_grad = jnp.sum(grad_normed * unit_one, axis=0)
        ln1_bias_grad = jnp.sum(grad_normed, axis=0)
        input_grad = grad_middle + norm_back(grad_normed, unit_one, inverse_one, gain_one)
        small = sum_all(
            jnp.stack(
                [
                    ln1_gain_grad,
                    ln1_bias_grad,
                    scale_attn_grad,
                    ln2_gain_grad,
                    ln2_bias_grad,
                    scale_mlp_grad,
                ]
            )
        )
        own = width // n_group
        small = lax.dynamic_slice_in_dim(small, group * own, own, 1)
        return (
            block_out,
            input_grad,
            small[0],
            small[1],
            w_qkv_grad,
            w_out_grad,
            small[2],
            small[3],
            small[4],
            w_gate_grad,
            w_up_grad,
            w_down_grad,
            small[5],
        )

    return shards


def solution(mesh):
    n_group, n_rep = mesh.shape["group"], mesh.shape["rep"]
    shards = tuned(mesh) if n_group == 8 and n_rep == 4 else plain(mesh)
    rowed, flat = P(AXES, None), P(AXES)
    in_specs = (
        rowed, rowed, flat, flat, rowed, rowed, flat, flat, flat, rowed, rowed, rowed, flat, rowed,
    )
    own_rows, own_flat = P("group", None), P("group")
    out_specs = (
        rowed, rowed, own_flat, own_flat, own_rows, own_rows, own_flat, own_flat, own_flat,
        own_rows, own_rows, own_rows, own_flat,
    )
    return jax.shard_map(shards, mesh=mesh, in_specs=in_specs, out_specs=out_specs, check_vma=False)
```

```python
import math

import jax
import jax.numpy as jnp
from jax import lax
from jax.experimental import pallas as pl
from jax.experimental.pallas import tpu as pltpu
from jax.sharding import PartitionSpec as P

HEADS = 16
WINDOW = 128
EPS = 1e-05
AXES = ("group", "rep")
BF = jnp.bfloat16
F32 = jnp.float32


def clip_layout(length_row, count):
    clip_ends = jnp.cumsum(length_row)
    clip_starts = clip_ends - length_row
    row_index = jnp.arange(count, dtype=jnp.int32)
    segment = jnp.sum((row_index[:, None] >= clip_ends[None, :]).astype(jnp.int32), axis=1)
    member = (segment[:, None] == jnp.arange(length_row.shape[0], dtype=jnp.int32)[None, :]).astype(
        jnp.int32
    )
    position = row_index - jnp.sum(member * clip_starts[None, :], axis=1)
    return (segment, position)


def rotary_tables(position, width):
    half = width // 2
    freqs = jnp.power(10000.0, -jnp.arange(half, dtype=F32) * (2.0 / width))
    angles = position.astype(F32)[:, None] * freqs[None, :]
    cosine = jnp.concatenate([jnp.cos(angles), jnp.cos(angles)], axis=1)
    sine = jnp.concatenate([jnp.sin(angles), jnp.sin(angles)], axis=1)
    return (cosine[:, None, :], sine[:, None, :])


def rotate(values, cosine, sine):
    half = values.shape[-1] // 2
    turned = jnp.concatenate([-values[..., half:], values[..., :half]], axis=-1)
    return values * cosine + turned * sine


def rotate_back(values, cosine, sine):
    half = values.shape[-1] // 2
    turned = jnp.concatenate([values[..., half:], -values[..., :half]], axis=-1)
    return values * cosine + turned * sine


def norm_parts(values):
    mean_value = jnp.mean(values, axis=-1, keepdims=True)
    centered = values - mean_value
    variance = jnp.mean(centered * centered, axis=-1, keepdims=True)
    inverse = lax.rsqrt(variance + EPS)
    return (centered * inverse, inverse)


def norm_back(grad_normed, unit, inverse, gain):
    scaled = grad_normed * gain
    return inverse * (
        scaled
        - jnp.mean(scaled, axis=-1, keepdims=True)
        - unit * jnp.mean(scaled * unit, axis=-1, keepdims=True)
    )


def block_allowed(segment, segment_pad, start, block, window):
    query_index = start + jnp.arange(block, dtype=jnp.int32)
    key_index = start - window + jnp.arange(block + window, dtype=jnp.int32)
    offset = query_index[:, None] - key_index[None, :]
    same_clip = segment[:, None] == segment_pad[None, :]
    return same_clip & (offset >= 0) & (offset < window)


def pad_front(values, window, fill):
    front = jnp.full((window,) + values.shape[1:], fill, values.dtype)
    return jnp.concatenate([front, values], axis=0)


def attention_forward(queries, keys_rot, values, segment, block, window):
    factor = 1.0 / math.sqrt(queries.shape[-1])
    keys_pad = pad_front(keys_rot, window, 0)
    values_pad = pad_front(values, window, 0)
    segment_pad = pad_front(segment, window, -1)
    allowed = block_allowed(segment, segment_pad, 0, block, window)
    scores = (
        jnp.einsum("qhd,khd->hqk", queries, keys_pad, preferred_element_type=F32) * factor
    )
    masked = jnp.where(allowed[None], scores, -jnp.inf)
    peak = jnp.max(masked, axis=-1, keepdims=True)
    expd = jnp.exp(masked - peak)
    totals = jnp.sum(expd, axis=-1, keepdims=True)
    probs = (expd / totals).astype(BF)
    outputs = jnp.einsum("hqk,khd->qhd", probs, values_pad, preferred_element_type=F32)
    log_totals = peak + jnp.log(totals)
    return (outputs, log_totals)


def attention_backward(
    queries, keys_rot, values, grad_attended, log_totals, segment, block, window
):
    factor = 1.0 / math.sqrt(queries.shape[-1])
    keys_pad = pad_front(keys_rot, window, 0)
    values_pad = pad_front(values, window, 0)
    segment_pad = pad_front(segment, window, -1)
    allowed = block_allowed(segment, segment_pad, 0, block, window)
    scores = (
        jnp.einsum("qhd,khd->hqk", queries, keys_pad, preferred_element_type=F32) * factor
    )
    probs = jnp.where(
        allowed[None], jnp.exp(jnp.where(allowed[None], scores, -jnp.inf) - log_totals), 0.0
    )
    probs_low = probs.astype(BF)
    grad_probs = jnp.einsum("qhd,khd->hqk", grad_attended, values_pad, preferred_element_type=F32)
    delta = jnp.sum(probs * grad_probs, axis=-1, keepdims=True)
    grad_scores = (probs * (grad_probs - delta)).astype(BF)
    grad_queries = (
        jnp.einsum("hqk,khd->qhd", grad_scores, keys_pad, preferred_element_type=F32) * factor
    )
    key_part = (
        jnp.einsum("hqk,qhd->khd", grad_scores, queries, preferred_element_type=F32) * factor
    )
    value_part = jnp.einsum("hqk,qhd->khd", probs_low, grad_attended, preferred_element_type=F32)
    return (grad_queries, key_part[window:], value_part[window:])


def make_links(n_group, n_rep):
    def swap(value, group_bits, rep_bits):
        pairs = [
            (g * n_rep + r, (g ^ group_bits) * n_rep + (r ^ rep_bits))
            for g in range(n_group)
            for r in range(n_rep)
        ]
        return lax.ppermute(value, AXES, pairs)

    return swap


def pick(stacked, index):
    return lax.dynamic_index_in_dim(stacked, index, 0, keepdims=False)


BITS = {"z1": (2, 0), "z2": (4, 0), "z3": (6, 0), "x": (1, 0), "y": (0, 2), "core": (0, 1)}
CONTRACT = {
    "nn": (((1,), (0,)), ((), ())),
    "nt": (((1,), (1,)), ((), ())),
    "tn": (((0,), (0,)), ((), ())),
}
BIG = pltpu.CompilerParams(vmem_limit_bytes=56 << 20)


def work(flops):
    return pl.CostEstimate(flops=int(flops), bytes_accessed=0, transcendentals=0)


ANY = pl.BlockSpec(memory_space=pl.ANY)
SMEM = pl.BlockSpec(memory_space=pltpu.SMEM)


def dot(a, b, form="nn"):
    return lax.dot_general(a, b, CONTRACT[form], preferred_element_type=F32)


def after(value, *done):
    return lax.optimization_barrier((value,) + done)[0]


def window(*values):
    return lax.optimization_barrier(values)


def lane_tables(position, width):
    lane = jnp.arange(2 * width, dtype=jnp.int32)
    index = (lane % (width // 2)).astype(F32)
    freqs = jnp.power(10000.0, -index * (2.0 / width))
    angles = position.astype(F32)[:, None] * freqs[None, :]
    sign = jnp.where(lane % width < width // 2, -1.0, 1.0)
    return jnp.cos(angles), jnp.sin(angles) * sign[None, :]


def sds(shape, dtype):
    return jax.ShapeDtypeStruct(shape, dtype)


def whole(shape):
    return pl.BlockSpec(shape, lambda *_: (0,) * len(shape))


def rotate_lanes(u, cosine, signed_sine, first):
    turned = jnp.where(first, pltpu.roll(u, 96, 1), pltpu.roll(u, 32, 1))
    return u * cosine + turned * signed_sine


PIECES = (
    ((0, 0, 0), (1, 0, 0), (2, 0, 0), (3, 0, 0)),
    ((0, 1, 0), (1, 1, 0), (2, 1, 0), (3, 1, 0)),
    ((0, 0, 1), (1, 0, 1), (2, 0, 1), (3, 0, 1)),
    ((0, 1, 1), (1, 1, 1), (2, 1, 1)),
    ((3, 1, 1),),
)


def project_kernel(*refs):
    n = len(PIECES)
    idx, own, came = refs[0], refs[1 : 1 + n], refs[1 + n : 1 + 2 * n]
    x_ref, cos_ref, sin_ref = refs[1 + 2 * n : 4 + 2 * n]
    qkv_ref, normed_ref, w_ref, vec_ref, weights, sems, out_sem = refs[4 + 2 * n :]
    j, steps = pl.program_id(0), pl.num_programs(0)
    block = qkv_ref.shape[1]

    def copies():
        out, count = [], 0
        for core_bit, group in ((0, own), (1, came)):
            for ref, owners in zip(group, PIECES):
                for i, (k, dx, dy) in enumerate(owners):
                    owner = (((idx[0] ^ k) * 2 + (idx[1] ^ dx)) * 2 + (idx[2] ^ dy)) * 2
                    row = pl.multiple_of((owner + (idx[3] ^ core_bit)) * 32, 32)
                    out.append(
                        pltpu.make_async_copy(
                            ref.at[i], weights.at[pl.ds(row, 32), :], sems.at[count]
                        )
                    )
                    count += 1
        return out

    def save():
        return pltpu.make_async_copy(weights, w_ref, out_sem)

    @pl.when(j == 0)
    def _():
        pieces = copies()
        for c in pieces:
            c.start()
        x = x_ref[...].astype(F32)
        centered = x - jnp.mean(x, axis=1, keepdims=True)
        unit = centered * lax.rsqrt(jnp.mean(centered * centered, axis=1, keepdims=True) + EPS)
        for c in pieces:
            c.wait()
        save().start()
        vecs = weights[:, weights.shape[1] - 128 :].astype(F32).T
        vec_ref[...] = vecs[:8]
        normed_ref[...] = (unit * vecs[0:1] + vecs[1:2]).astype(BF)

    p = dot(normed_ref[...], weights[:, pl.ds(pl.multiple_of(j * block, block), block)])
    lane = lax.broadcasted_iota(jnp.int32, (1, 128), 1)
    first = (lane % 64) < 32

    @pl.when(j * 3 < 2 * steps)
    def _():
        for c in range(0, block, 128):
            cols = slice(c, c + 128)
            qkv_ref[:, cols] = rotate_lanes(p[:, cols], cos_ref[...], sin_ref[...], first).astype(BF)

    @pl.when(j * 3 >= 2 * steps)
    def _():
        qkv_ref[...] = p.astype(BF)

    @pl.when(j == steps - 1)
    def _():
        save().wait()


def project(idx, own, came, x, cosine, signed_sine, block=512):
    rows, width = x.shape
    cols = own[0].shape[-1]
    return pl.pallas_call(
        project_kernel,
        grid=(3 * width // block,),
        in_specs=[SMEM] + [ANY] * (2 * len(PIECES)) + [whole((rows, width))] + [whole((rows, 128))] * 2,
        out_specs=[
            pl.BlockSpec((rows, block), lambda j: (0, j)),
            whole((rows, width)),
            ANY,
            whole((8, width)),
        ],
        out_shape=[
            sds((rows, 3 * width), BF),
            sds((rows, width), BF),
            sds((width, cols), BF),
            sds((8, width), F32),
        ],
        scratch_shapes=[
            pltpu.VMEM((width, cols), BF),
            pltpu.SemaphoreType.DMA((32,)),
            pltpu.SemaphoreType.DMA,
        ],
        compiler_params=BIG,
        cost_estimate=work(1e9),
        name="project",
    )(idx, *own, *came, x, cosine, signed_sine)


def unit_of(values):
    centered = values - jnp.mean(values, axis=1, keepdims=True)
    inverse = lax.rsqrt(jnp.mean(centered * centered, axis=1, keepdims=True) + EPS)
    return centered * inverse, inverse


def unit_back(grad, unit, inverse, gain):
    scaled = grad * gain
    return inverse * (
        scaled
        - jnp.mean(scaled, axis=1, keepdims=True)
        - unit * jnp.mean(scaled * unit, axis=1, keepdims=True)
    )


def add_rows(ref, row, values):
    total = jnp.sum(values, axis=0, keepdims=True)

    @pl.when(pl.program_id(0) == 0)
    def _():
        ref[row : row + 1, :] = total

    @pl.when(pl.program_id(0) > 0)
    def _():
        ref[row : row + 1, :] += total


def leave_kernel(attended_ref, w_ref, x_ref, vec_ref, branch_ref, n_ref):
    branch = dot(attended_ref[...], w_ref[...])
    branch_ref[...] = branch
    unit, _ = unit_of(x_ref[...].astype(F32) + vec_ref[2:3] * branch)
    n_ref[...] = (unit * vec_ref[3:4] + vec_ref[4:5]).astype(BF)


def leave(attended, w_attn, x, vecs, block=256):
    rows, width = x.shape
    row = pl.BlockSpec((block, width), lambda i: (i, 0))
    return pl.pallas_call(
        leave_kernel,
        grid=(rows // block,),
        in_specs=[row, pl.BlockSpec((width, width), lambda i: (0, 3)), row, whole((8, width))],
        out_specs=[row, row],
        out_shape=[sds((rows, width), F32), sds((rows, width), BF)],
        compiler_params=BIG,
        cost_estimate=work(1e9),
        name="leave",
    )(attended, w_attn, x, vecs)


def back_kernel(
    a_ref, b_ref, c_ref, go_ref, branch_ref, x_ref, vec_ref, w_ref, gm_ref, gb_ref, ga_ref, sum_ref
):
    grad = a_ref[...].astype(F32) + b_ref[...].astype(F32) + c_ref[...].astype(F32)
    branch = branch_ref[...]
    unit, inverse = unit_of(x_ref[...].astype(F32) + vec_ref[2:3] * branch)

    @pl.when(pl.program_id(0) == 0)
    def _():
        sum_ref[...] = jnp.zeros_like(sum_ref)

    add_rows(sum_ref, 3, grad * unit)
    add_rows(sum_ref, 4, grad)
    grad_middle = go_ref[...].astype(F32) + unit_back(grad, unit, inverse, vec_ref[3:4])
    gm_ref[...] = grad_middle
    add_rows(sum_ref, 2, grad_middle * branch)
    grad_branch = (vec_ref[2:3] * grad_middle).astype(BF)
    gb_ref[...] = grad_branch
    ga_ref[...] = dot(grad_branch, w_ref[...], "nt").astype(BF)


def back(parts, grad_out, branch, x, vecs, w_attn, block=256):
    rows, width = x.shape
    row = pl.BlockSpec((block, width), lambda i: (i, 0))
    return pl.pallas_call(
        back_kernel,
        grid=(rows // block,),
        in_specs=[row] * 6
        + [whole((8, width)), pl.BlockSpec((width, width), lambda i: (0, 3))],
        out_specs=[row, row, row, whole((8, width))],
        out_shape=[sds((rows, width), F32)] + [sds((rows, width), BF)] * 2 + [sds((8, width), F32)],
        compiler_params=BIG,
        cost_estimate=work(1e9),
        name="back",
    )(*parts, grad_out, branch, x, vecs, w_attn)


def last_kernel(*refs):
    dq, dk, dv, wq, wk, wv, x_ref, vec_ref, gm_ref, m0, m1, m2, go_ref, branch_ref, mid_ref = refs[:15]
    ig_ref, out_ref, sum_ref = refs[15:]
    grad = dot(dq[...], wq[...], "nt") + dot(dk[...], wk[...], "nt") + dot(dv[...], wv[...], "nt")
    x = x_ref[...].astype(F32)
    unit, inverse = unit_of(x)

    @pl.when(pl.program_id(0) == 0)
    def _():
        sum_ref[...] = mid_ref[...]

    add_rows(sum_ref, 0, grad * unit)
    add_rows(sum_ref, 1, grad)
    ig_ref[...] = gm_ref[...] + unit_back(grad, unit, inverse, vec_ref[0:1])
    mlp = m0[...].astype(F32) + m1[...].astype(F32) + m2[...].astype(F32)
    out_ref[...] = (x + vec_ref[2:3] * branch_ref[...] + vec_ref[5:6] * mlp).astype(BF)
    add_rows(sum_ref, 5, go_ref[...].astype(F32) * mlp)


def last(grads, w_attn, x, vecs, grad_middle, mlp_parts, grad_out, branch, mid_sums, block=256):
    rows, width = x.shape
    row = pl.BlockSpec((block, width), lambda i: (i, 0))
    columns = [pl.BlockSpec((width, width), lambda i, n=n: (0, n)) for n in range(3)]
    return pl.pallas_call(
        last_kernel,
        grid=(rows // block,),
        in_specs=[row] * 3
        + columns
        + [row, whole((8, width))]
        + [row] * 6
        + [whole((8, width))],
        out_specs=[row, row, whole((8, width))],
        out_shape=[sds((rows, width), F32), sds((rows, width), BF), sds((8, width), F32)],
        compiler_params=BIG,
        cost_estimate=work(1e9),
        name="last",
    )(*grads, w_attn, w_attn, w_attn, x, vecs, grad_middle, *mlp_parts, grad_out, branch, mid_sums)


def set_bias(bias_ref, pos_ref, rows):
    for b in range(rows // WINDOW):
        keys = WINDOW if b == 0 else 2 * WINDOW
        offset = (
            lax.broadcasted_iota(jnp.int32, (WINDOW, keys), 0)
            - lax.broadcasted_iota(jnp.int32, (WINDOW, keys), 1)
            + (keys - WINDOW)
        )
        reach = jnp.minimum(pos_ref[b * WINDOW : (b + 1) * WINDOW, :], WINDOW - 1)
        seen = (offset >= 0) & (offset <= reach)
        bias_ref[b, :, 2 * WINDOW - keys :] = jnp.where(seen, 0.0, -1e30)


def split_heads(u, low):
    zero = jnp.zeros_like(u)
    return jnp.concatenate([jnp.where(low, u, zero), jnp.where(low, zero, u)], axis=0)


def pair_probs(q, k, bias, low):
    q = split_heads(q, low) * jnp.asarray(0.125, BF)
    scores = dot(q, k, "nt") + jnp.concatenate([bias, bias], axis=0)
    e = jnp.exp(scores - jnp.max(scores, axis=1, keepdims=True))
    return q, e * (1.0 / jnp.sum(e, axis=1, keepdims=True))


def attend_kernel(q_ref, k_ref, v_ref, pos_ref, o_ref, bias_ref):
    rows = q_ref.shape[0]

    @pl.when(pl.program_id(0) == 0)
    def _():
        set_bias(bias_ref, pos_ref, rows)

    low = lax.broadcasted_iota(jnp.int32, (1, 128), 1) < 64
    for b in range(rows // WINDOW):
        here = slice(b * WINDOW, (b + 1) * WINDOW)
        keys = slice(max(b - 1, 0) * WINDOW, (b + 1) * WINDOW)
        bias = bias_ref[b, :, 2 * WINDOW - (keys.stop - keys.start) :]
        _, probs = pair_probs(q_ref[here, :], k_ref[keys, :], bias, low)
        out = dot(probs.astype(BF), v_ref[keys, :])
        o_ref[here, :] = jnp.where(low, out[:WINDOW], out[WINDOW:]).astype(BF)


def attend(qkv, position):
    rows, width = qkv.shape[0], qkv.shape[1] // 3
    pairs = width // 128
    cols = lambda part: pl.BlockSpec((rows, 128), lambda j: (0, j + part * pairs))
    return pl.pallas_call(
        attend_kernel,
        grid=(pairs,),
        in_specs=[cols(0), cols(1), cols(2), whole((rows, 1))],
        out_specs=cols(0),
        out_shape=sds((rows, width), BF),
        scratch_shapes=[pltpu.VMEM((rows // WINDOW, WINDOW, 2 * WINDOW), F32)],
        compiler_params=BIG,
        cost_estimate=work(1e9),
        name="attend",
    )(qkv, qkv, qkv, position)


def attend_back_kernel(
    q_ref, k_ref, v_ref, do_ref, pos_ref, cos_ref, sin_ref, dq_ref, dk_ref, dv_ref, bias_ref
):
    rows = q_ref.shape[0]
    blocks = rows // WINDOW

    @pl.when(pl.program_id(0) == 0)
    def _():
        set_bias(bias_ref, pos_ref, rows)

    lane = lax.broadcasted_iota(jnp.int32, (1, 128), 1)
    low, first = lane < 64, (lane % 64) < 32

    def turn_back(u, here):
        return rotate_lanes(u, cos_ref[here, :], -sin_ref[here, :], first).astype(BF)

    dk, dv = [None] * blocks, [None] * blocks
    for b in range(blocks):
        here = slice(b * WINDOW, (b + 1) * WINDOW)
        keys = slice(max(b - 1, 0) * WINDOW, (b + 1) * WINDOW)
        bias = bias_ref[b, :, 2 * WINDOW - (keys.stop - keys.start) :]
        q, probs = pair_probs(q_ref[here, :], k_ref[keys, :], bias, low)
        do = split_heads(do_ref[here, :], low)
        dp = dot(do, v_ref[keys, :], "nt")
        delta = jnp.sum(probs * dp, axis=1, keepdims=True)
        ds = (probs * (dp - delta)).astype(BF)
        dq = dot(ds, k_ref[keys, :]) * 0.125
        dq_ref[here, :] = turn_back(jnp.where(low, dq[:WINDOW], dq[WINDOW:]), here)
        k_part = dot(ds, q, "tn")
        v_part = dot(probs.astype(BF), do, "tn")
        for i, kb in enumerate(range(max(b - 1, 0), b + 1)):
            part = slice(i * WINDOW, (i + 1) * WINDOW)
            dk[kb] = k_part[part] if dk[kb] is None else dk[kb] + k_part[part]
            dv[kb] = v_part[part] if dv[kb] is None else dv[kb] + v_part[part]
    for kb in range(blocks):
        here = slice(kb * WINDOW, (kb + 1) * WINDOW)
        dk_ref[here, :] = turn_back(dk[kb], here)
        dv_ref[here, :] = dv[kb].astype(BF)


def attend_back(qkv, grad, position, cosine, signed_sine):
    rows, width = qkv.shape[0], qkv.shape[1] // 3
    pairs = width // 128
    cols = lambda part: pl.BlockSpec((rows, 128), lambda j: (0, j + part * pairs))
    return pl.pallas_call(
        attend_back_kernel,
        grid=(pairs,),
        in_specs=[cols(0), cols(1), cols(2), cols(0), whole((rows, 1))] + [whole((rows, 128))] * 2,
        out_specs=[cols(0)] * 3,
        out_shape=[sds((rows, width), BF)] * 3,
        scratch_shapes=[pltpu.VMEM((rows // WINDOW, WINDOW, 2 * WINDOW), F32)],
        compiler_params=BIG,
        cost_estimate=work(1e9),
        name="attend_back",
    )(qkv, qkv, qkv, grad, position, cosine, signed_sine)


def mlp_copies(idx, pieces, downs, gate, up, down, sems):
    first, second, last = [], [], []
    half = gate.shape[1] // 2

    def copy(src, dst, group):
        n = len(first) + len(second) + len(last)
        group.append(pltpu.make_async_copy(src, dst, sems.at[n]))

    for i, ref in enumerate(pieces):
        rows = ref.shape[1]
        here = pl.ds(pl.multiple_of(((idx[0] * 2 + idx[1]) ^ i) * rows, rows), rows)
        for c, group in ((0, first), (half, second)):
            cols = pl.ds(c, half)
            for m, target in ((0, gate), (1, up)):
                copy(ref.at[m, :, cols], target.at[here, cols], group)
    for i, ref in enumerate(downs):
        rows = ref.shape[0]
        here = pl.ds(pl.multiple_of(((idx[0] * 2 + idx[1]) ^ i) * rows, rows), rows)
        copy(ref, down.at[here, :], last)
    return first, second, last


def mlp_kernel(last_half, *refs):
    idx, pieces, downs = refs[0], refs[1:9], refs[9:17]
    n_parts, g_parts, scale_ref = refs[17:19], refs[19:21], refs[21]
    refs = refs[22:]
    if last_half:
        before_ref, refs = refs[0], refs[1:]
    gg_out, gu_out = refs[:2]
    gn_parts, mlp_parts = refs[2:4], refs[4:6]
    refs = refs[6:]
    if last_half:
        send_ref, keep_ref, refs = refs[0], refs[1], refs[2:]
    else:
        total_out, refs = refs[0], refs[1:]
    (w_gate, w_up, w_down, n, gm, silu, slope, hidden, gg, gu, gn, mlp, total) = refs[:13]
    sems, n_sems, out_sems = refs[13:]
    rows, width = n.shape
    half, part = rows // 2, w_gate.shape[1]
    first, second, down = mlp_copies(idx, pieces, downs, w_gate, w_up, w_down, sems)
    n_copies, g_copies = [], []
    for k in range(2):
        here = pl.ds(k * half, half)
        n_copies.append(pltpu.make_async_copy(n_parts[k], n.at[here, :], n_sems.at[k]))
        g_copies.append(pltpu.make_async_copy(g_parts[k], gm.at[here, :], n_sems.at[2 + k]))
    before = [pltpu.make_async_copy(before_ref, total, n_sems.at[4])] if last_half else []
    for c in n_copies + first + second + g_copies + down + before:
        c.start()
    outs = []

    def send(src, dst):
        outs.append(pltpu.make_async_copy(src, dst, out_sems.at[len(outs)]))
        outs[-1].start()

    for c in n_copies + first:
        c.wait()
    chunks = [slice(c, c + part // 2) for c in (0, part // 2)]
    for k, cols in enumerate(chunks):
        if k == 1:
            for c in second:
                c.wait()
        gate, up = dot(n[...], w_gate[:, cols]), dot(n[...], w_up[:, cols])
        s = 0.5 * jnp.tanh(0.5 * gate) + 0.5
        act = gate * s
        silu[:, cols] = act
        slope[:, cols] = up * (s + act * (1.0 - s))
        hidden[:, cols] = (act * up).astype(BF)
    for c in g_copies + before:
        c.wait()
    gm[...] = (scale_ref[5:6] * gm[...].astype(F32)).astype(BF)
    for cols in chunks:
        product = dot(hidden[:, cols], gm[...], "tn")
        if last_half:
            product = product + total[cols, :].astype(F32)
        total[cols, :] = product.astype(BF)
    if last_half:
        block = send_ref.shape[1]
        for k in range(send_ref.shape[0]):
            for ref, x in ((send_ref, 1 - idx[1]), (keep_ref, idx[1])):
                at = pl.multiple_of((2 * k + x) * block, block)
                send(total.at[pl.ds(at, block), :], ref.at[k])
    else:
        send(total, total_out)
    for c in down:
        c.wait()
    for cols in chunks:
        gh = dot(gm[...], w_down[cols, :], "nt")
        gg[:, cols] = (gh * slope[:, cols]).astype(BF)
        gu[:, cols] = (gh * silu[:, cols]).astype(BF)
    send(gg, gg_out)
    send(gu, gu_out)
    for k in range(2):
        here = pl.ds(k * half, half)
        product = dot(gg[here, :], w_gate[...], "nt") + dot(gu[here, :], w_up[...], "nt")
        gn[here, :] = product.astype(BF)
        send(gn.at[here, :], gn_parts[k])
        mlp[here, :] = dot(hidden[here, :], w_down[...]).astype(BF)
        send(mlp.at[here, :], mlp_parts[k])
    for c in outs:
        c.wait()


def mlp_both(idx, pieces, downs, n_parts, g_parts, scale, before=None):
    rows, width = n_parts[0].shape
    part = pieces[0].shape[2]
    last_half = before is not None
    split, total = (4, part // 8, width), (part, width)
    in_specs = [SMEM] + [ANY] * 20 + [pl.BlockSpec(memory_space=pltpu.VMEM)]
    out_shape = [sds((2 * rows, part), BF)] * 2 + [sds((rows, width), BF)] * 4
    args = (idx, *pieces, *downs, *n_parts, *g_parts, scale)
    if last_half:
        in_specs.append(ANY)
        args += (before,)
        out_shape += [sds(split, BF)] * 2
    else:
        out_shape.append(sds(total, BF))
    tokens = (2 * rows, width)
    inner = (2 * rows, part)
    return pl.pallas_call(
        lambda *refs: mlp_kernel(last_half, *refs),
        in_specs=in_specs,
        out_specs=[ANY] * len(out_shape),
        out_shape=out_shape,
        scratch_shapes=[
            pltpu.VMEM((width, part), BF),
            pltpu.VMEM((width, part), BF),
            pltpu.VMEM(total, BF),
            pltpu.VMEM(tokens, BF),
            pltpu.VMEM(tokens, BF),
            pltpu.VMEM(inner, F32),
            pltpu.VMEM(inner, F32),
            pltpu.VMEM(inner, BF),
            pltpu.VMEM(inner, BF),
            pltpu.VMEM(inner, BF),
            pltpu.VMEM(tokens, BF),
            pltpu.VMEM(tokens, BF),
            pltpu.VMEM(total, BF),
            pltpu.SemaphoreType.DMA((40,)),
            pltpu.SemaphoreType.DMA((5,)),
            pltpu.SemaphoreType.DMA((14,)),
        ],
        compiler_params=BIG,
        cost_estimate=work(1e9),
        name="mlp_both",
    )(*args)


def weight_grad_kernel(idx, *refs):
    a_refs, b_refs, send_ref, keep_ref = refs[:8], refs[8:10], refs[10], refs[11]
    total = None
    for p in range(4):
        a = jnp.concatenate([a_refs[2 * p][...], a_refs[2 * p + 1][...]], axis=1)
        rows = a.shape[0]
        part = dot(a, b_refs[p // 2][pl.ds((p % 2) * rows, rows), :], "tn")
        total = part if total is None else total + part
    total = total.astype(BF).reshape((2,) + send_ref.shape[1:])
    half = pl.num_programs(0) // 2

    @pl.when(pl.program_id(0) < half)
    def _():
        send_ref[...] = total

    @pl.when(pl.program_id(0) >= half)
    def _():
        keep_ref[...] = total


def weight_grad(idx, a_parts, b_parts):
    tokens, width = a_parts[0].shape
    part = b_parts[0].shape[1]
    rows = width // 8
    split = (4, rows, part)

    def column(which):
        def place(i, s):
            mine = jnp.where(i < 2, 1 - s[1], s[1])
            return (0, 2 * (2 * (i % 2) + which) + mine)

        return pl.BlockSpec((tokens, rows), place)

    return pl.pallas_call(
        weight_grad_kernel,
        grid_spec=pltpu.PrefetchScalarGridSpec(
            num_scalar_prefetch=1,
            grid=(4,),
            in_specs=[column(0), column(1)] * 4
            + [pl.BlockSpec((2 * tokens, part), lambda i, s: (0, 0))] * 2,
            out_specs=[
                pl.BlockSpec((2, rows, part), lambda i, s: (jnp.minimum(i, 1), 0, 0)),
                pl.BlockSpec((2, rows, part), lambda i, s: (jnp.maximum(i - 2, 0), 0, 0)),
            ],
        ),
        out_shape=[sds(split, BF)] * 2,
        compiler_params=BIG,
        cost_estimate=work(1e9),
        name="weight_grad",
    )(idx, *[p for p in a_parts for _ in range(2)], *b_parts)


def attn_grad_kernel(idx, q_in, o_in, dq, dk, dv, do, *refs):
    outs, totals, sems = refs[:10], refs[10:12], refs[12]
    core = idx[3]
    half = dq.shape[1]
    copies = []
    for n, parts in enumerate((((q_in, dq), (q_in, dk)), ((q_in, dv), (o_in, do)))):
        side, total = idx[1 + n], totals[n]
        for c, (a, b) in enumerate(parts):
            product = dot(a[...], b[...], "tn").astype(BF)
            total[:, :, :, :, :, c * half : (c + 1) * half] = product.reshape(4, 2, 2, 2, 32, half)
        for m in range(5):
            to_core = (1 - core) if m < 3 else core
            to_side = (1 - side) if m in (0, 1, 3) else side
            cols = pl.ds(m * half, half) if m < 2 else pl.ds(0, 2 * half)
            for other in range(2):
                for k in range(4):
                    x, y = (to_side, other) if n == 0 else (other, to_side)
                    copy = pltpu.make_async_copy(
                        total.at[k, x, y, to_core, :, cols],
                        outs[5 * n + m].at[other, k],
                        sems.at[len(copies)],
                    )
                    copy.start()
                    copies.append(copy)
    for copy in copies:
        copy.wait()


def attn_grad(idx, q_in, o_in, dq, dk, dv, do):
    width = q_in.shape[1]
    vmem = pl.BlockSpec(memory_space=pltpu.VMEM)
    one, two = sds((2, 4, 32, width), BF), sds((2, 4, 32, 2 * width), BF)
    return pl.pallas_call(
        attn_grad_kernel,
        in_specs=[SMEM] + [vmem] * 6,
        out_specs=[ANY] * 10,
        out_shape=[one, one, two, two, two] * 2,
        scratch_shapes=[pltpu.VMEM((4, 2, 2, 2, 32, 2 * width), BF)] * 2
        + [pltpu.SemaphoreType.DMA((80,))],
        compiler_params=BIG,
        cost_estimate=work(1e9),
        name="attn_grad",
    )(idx, q_in, o_in, dq, dk, dv, do)


def z_blocks(step, z):
    if step == "near":
        return [1 - z % 2, 3 - z % 2]
    return [2 * (1 - z // 2) + z % 2] if step == "far" else [z]


def z_copies(idx, jobs, buf, sems):
    copies = []
    for step, pairs in jobs:
        for pair in pairs:
            for b in z_blocks(step, idx[0]):
                for ref in pair:
                    at = len(copies)
                    copies.append(pltpu.make_async_copy(ref.at[b], buf.at[at], sems.at[at]))
    return copies


def z_count(jobs):
    return sum(2 * n * (2 if step == "near" else 1) for step, n in jobs)


def z_scratch(jobs, block):
    count = z_count(jobs)
    return [pltpu.VMEM((count,) + block, BF), pltpu.SemaphoreType.DMA((count,))]


def z_near(buf, at, out):
    for k in range(2):
        total = buf[at + 2 * k].astype(F32) + buf[at + 2 * k + 1].astype(F32)
        out[k] = total.astype(BF)


def z_add(buf, at, *more):
    total = buf[at].astype(F32) + buf[at + 1].astype(F32)
    for part in more:
        total = total + part.astype(F32)
    return total.astype(BF)


def near_sum_kernel(n, idx, *refs):
    pairs, (out, buf, sems) = refs[: 2 * n], refs[2 * n :]
    pairs = [pairs[2 * m : 2 * m + 2] for m in range(n)]
    copies = z_copies(idx, [("near", pairs)], buf, sems)
    for copy in copies:
        copy.start()
    for copy in copies:
        copy.wait()
    for m in range(n):
        z_near(buf, 4 * m, out.at[m])


def near_sum(idx, pairs):
    n = len(pairs)
    block = pairs[0][0].shape[1:]
    return pl.pallas_call(
        lambda *refs: near_sum_kernel(n, *refs),
        in_specs=[SMEM] + [ANY] * (2 * n),
        out_specs=pl.BlockSpec(memory_space=pltpu.VMEM),
        out_shape=sds((n, 2) + block, BF),
        scratch_shapes=z_scratch([("near", n)], block),
        compiler_params=BIG,
        cost_estimate=work(1e9),
        name="near_sum",
    )(idx, *[p for pair in pairs for p in pair])


def first_sum_kernel(idx, a_ref, q_ref, k_ref, b_ref, v_ref, o_ref, near, *refs):
    z_refs, (a_out, b_out, far, gate_near, buf, sems) = refs[:6], refs[6:]
    down, up, gate = z_refs[:2], z_refs[2:4], z_refs[4:6]
    copies = z_copies(idx, [("far", [down, up]), ("near", [gate])], buf, sems)
    for copy in copies:
        copy.start()
    half = q_ref.shape[3]
    for keep, left, right, out in ((a_ref, q_ref, k_ref, a_out), (b_ref, v_ref, o_ref, b_out)):
        for ref, cols in ((left, slice(0, half)), (right, slice(half, 2 * half))):
            total = keep[:, :, :, cols].astype(F32) + ref[...].astype(F32)
            out[:, :, :, cols] = total.astype(BF)
    for copy in copies:
        copy.wait()
    high = idx[0] // 2
    for m in range(2):
        far[m] = z_add(buf, 2 * m, near[m, 1 - high])
    z_near(buf, 4, gate_near)


def first_sum(idx, parts, near, pairs):
    block = near.shape[2:]
    vmem = pl.BlockSpec(memory_space=pltpu.VMEM)
    shape = sds(parts[0].shape, BF)
    return pl.pallas_call(
        first_sum_kernel,
        in_specs=[SMEM] + [vmem] * 7 + [ANY] * 6,
        out_specs=[vmem] * 4,
        out_shape=[shape, shape, sds((2,) + block, BF), sds((2,) + block, BF)],
        scratch_shapes=z_scratch([("far", 2), ("near", 1)], block),
        compiler_params=BIG,
        cost_estimate=work(1e9),
        name="first_sum",
    )(idx, *parts, near, *[p for pair in pairs for p in pair])


def second_sum_kernel(idx, a0, a1, a2, b0, b1, b2, gate_near, *refs):
    gate, (a_away, b_away, gate_far, buf, sems) = refs[:2], refs[2:]
    copies = z_copies(idx, [("far", [gate])], buf, sems)
    i = pl.program_id(0)

    @pl.when(i == 0)
    def _():
        for copy in copies:
            copy.start()

    for p0, p1, p2, out in ((a0, a1, a2, a_away), (b0, b1, b2, b_away)):
        out[...] = (p0[...].astype(F32) + p1[...].astype(F32) + p2[...].astype(F32)).astype(BF)

    @pl.when(i == pl.num_programs(0) - 1)
    def _():
        for copy in copies:
            copy.wait()
        gate_far[...] = z_add(buf, 0, gate_near[1 - idx[0] // 2])


def stay_sum_kernel(idx, a0, a1, a2, b0, b1, b2, near, far, *refs):
    pairs, (a_stay, b_stay, own, buf, sems) = refs[:4], refs[4:]
    copies = z_copies(idx, [("total", [pairs[:2], pairs[2:]])], buf, sems)
    i = pl.program_id(0)

    @pl.when(i == 0)
    def _():
        for copy in copies:
            copy.start()

    for p0, p1, p2, out in ((a0, a1, a2, a_stay), (b0, b1, b2, b_stay)):
        out[...] = p0[...].astype(F32) + p1[...].astype(F32) + p2[...].astype(F32)

    @pl.when(i == pl.num_programs(0) - 1)
    def _():
        for copy in copies:
            copy.wait()
        for m in range(2):
            own[m] = z_add(buf, 2 * m, near[m, idx[0] // 2], far[m])


def half_sum(kernel, idx, parts, away, more, pairs, outs, jobs, dtype, name):
    _, blocks, rows, cols = parts[0].shape
    block = pairs[0][0].shape[1:]
    side = lambda at: pl.BlockSpec(
        (None, 2, rows, cols), lambda i, s: (1 - s[at] if away else s[at], i, 0, 0)
    )
    out = pl.BlockSpec((2, rows, cols), lambda i, s: (i, 0, 0))
    return pl.pallas_call(
        kernel,
        grid_spec=pltpu.PrefetchScalarGridSpec(
            num_scalar_prefetch=1,
            grid=(blocks // 2,),
            in_specs=[side(2)] * 3
            + [side(1)] * 3
            + [pl.BlockSpec(p.shape, lambda i, s, n=p.ndim: (0,) * n) for p in more]
            + [ANY] * (2 * len(pairs)),
            out_specs=[out, out]
            + [pl.BlockSpec(shape, lambda i, s, n=len(shape): (0,) * n) for shape in outs],
            scratch_shapes=z_scratch(jobs, block),
        ),
        out_shape=[sds((blocks, rows, cols), dtype)] * 2 + [sds(shape, BF) for shape in outs],
        compiler_params=BIG,
        cost_estimate=work(1e9),
        name=name,
    )(idx, *parts, *more, *[p for pair in pairs for p in pair])


def second_sum(idx, parts, gate_near, pair):
    block = gate_near.shape[1:]
    return half_sum(
        second_sum_kernel, idx, parts, True, [gate_near], [pair], [block], [("far", 1)], BF, "second_sum"
    )


def stay_sum(idx, parts, near, far, pairs):
    return half_sum(
        stay_sum_kernel, idx, parts, False, [near, far], pairs, [far.shape], [("total", 2)], F32, "stay_sum"
    )


def third_sum_kernel(idx, a0, a1, b0, b1, small, own, gate_near, gate_far, *refs):
    gate, (own_out, mine, s1, s2, s3, buf, sems) = refs[:2], refs[2:]
    copies = z_copies(idx, [("total", [gate])], buf, sems)
    for copy in copies:
        copy.start()
    half, width = a0.shape[2], 2 * a0.shape[2]
    for k, out in enumerate((mine, s1, s2, s3)):
        z = idx[0] ^ k
        for p0, p1, low in ((a0, a1, 0), (b0, b1, half)):
            total = p0[z].astype(F32) + p1[z].astype(F32)
            out[:, low : low + half] = total.astype(out.dtype)
        out[:, width:] = small[z].astype(out.dtype)
    for copy in copies:
        copy.wait()
    own_out[pl.ds(0, 2)] = own[...]
    own_out[2] = z_add(buf, 0, gate_near[idx[0] // 2], gate_far[...])


def third_sum(idx, a_stay, a_y, b_stay, b_x, small, own, gate_near, gate_far, pair):
    vmem = pl.BlockSpec(memory_space=pltpu.VMEM)
    _, rows, half = a_stay.shape
    cols = 2 * half + small.shape[2]
    block = gate_far.shape
    return pl.pallas_call(
        third_sum_kernel,
        in_specs=[SMEM] + [vmem] * 8 + [ANY] * 2,
        out_specs=[vmem] * 5,
        out_shape=[sds((3,) + block, BF), sds((rows, cols), F32)] + [sds((rows, cols), BF)] * 3,
        scratch_shapes=z_scratch([("total", 1)], block),
        compiler_params=BIG,
        cost_estimate=work(1e9),
        name="third_sum",
    )(idx, a_stay, a_y, b_stay, b_x, small, own, gate_near, gate_far, *pair)


def place_kernel(n_small, idx, own, y_ref, core_ref, both_ref, *outs):
    rep = idx[2] * 2 + idx[3]
    rows = own.shape[0]
    wide, narrow = outs, ()
    if n_small:
        wide, narrow, tall = outs[: -1 - n_small], outs[-1 - n_small : -1], outs[-1]
    for ref, d in ((own, 0), (y_ref, 2), (core_ref, 1), (both_ref, 3)):
        low = 0
        for out in wide:
            cols = out.shape[2]
            out[pl.ds(rep ^ d, 1)] = ref[:, low : low + cols].astype(F32)[None]
            low += cols
        if n_small:
            at = pl.multiple_of((rep ^ d) * rows, rows)
            tall[pl.ds(at, rows), :] = ref[:, low : low + 128].astype(F32)
    if n_small:
        turned = tall[...].T
        for k, out in enumerate(narrow):
            out[...] = turned[k : k + 1]


def place_rows(idx, own, other_y, other_core, other_both, widths, n_small=0):
    rows = own.shape[0]
    vmem = pl.BlockSpec(memory_space=pltpu.VMEM)
    outs = pl.pallas_call(
        lambda *refs: place_kernel(n_small, *refs),
        in_specs=[SMEM] + [vmem] * 4,
        out_specs=[vmem] * (len(widths) + n_small),
        out_shape=[sds((4, rows, w), F32) for w in widths] + [sds((1, 4 * rows), F32)] * n_small,
        scratch_shapes=[pltpu.VMEM((4 * rows, 128), F32)] if n_small else [],
        compiler_params=BIG,
        cost_estimate=work(1e9),
        name="place_rows",
    )(idx, own, other_y, other_core, other_both)
    n = len(widths)
    return [out.reshape(4 * rows, -1) for out in outs[:n]] + [out[0] for out in outs[n:]]


def place_mlp_kernel(idx, own_ref, y_ref, core_ref, both_ref, down_out, up_out, gate_out):
    rep = idx[2] * 2 + idx[3]
    parts = ((own_ref, 0), (y_ref, 2), (core_ref, 1), (both_ref, 3))
    for ref, d in parts:
        down_out[pl.ds(rep ^ d, 1)] = ref[0].astype(F32)[None]
    for m, out in ((1, up_out), (2, gate_out)):
        for ref, d in parts:
            for g in range(own_ref.shape[2] // 128):
                at = pl.multiple_of((g * 4 + (rep ^ d)) * 128, 128)
                out[:, pl.ds(at, 128)] = ref[m, :, g * 128 : (g + 1) * 128].astype(F32)


def place_mlp(idx, own, other_y, other_core, other_both):
    _, rows, cols = own.shape
    vmem = pl.BlockSpec(memory_space=pltpu.VMEM)
    down, up, gate = pl.pallas_call(
        place_mlp_kernel,
        in_specs=[SMEM] + [vmem] * 4,
        out_specs=[vmem] * 3,
        out_shape=[sds((4, rows, cols), F32)] + [sds((rows, 4 * cols), F32)] * 2,
        compiler_params=BIG,
        cost_estimate=work(1e9),
        name="place_mlp",
    )(idx, own, other_y, other_core, other_both)
    return down.reshape(4 * rows, cols), up, gate


def share_kernel(idx, raw_ref, here_ref, there_ref):
    rep = idx[2] * 2 + idx[3]
    for d in range(4):
        out = (here_ref, there_ref)[d // 2]
        for g in range(out.shape[3] // 128):
            at = pl.multiple_of((g * 4 + (rep ^ d)) * 128, 128)
            out[d % 2, :, :, g * 128 : (g + 1) * 128] = raw_ref[:, :, pl.ds(at, 128)]


def share(idx, raw):
    _, rows, ff = raw.shape
    vmem = pl.BlockSpec(memory_space=pltpu.VMEM)
    return pl.pallas_call(
        share_kernel,
        in_specs=[SMEM, vmem],
        out_specs=[vmem] * 2,
        out_shape=[sds((2, 2, rows, ff // 4), BF)] * 2,
        compiler_params=BIG,
        cost_estimate=work(1e9),
        name="share",
    )(idx, raw)


def join_kernel(idx, own, y_ref, core_ref, out_ref):
    rep = idx[2] * 2 + idx[3]
    rows = own.shape[2]
    parts = ((own.at[0], 0), (y_ref.at[0], 2), (core_ref.at[0], 1), (core_ref.at[1], 3))
    for ref, d in parts:
        at = pl.multiple_of((rep ^ d) * rows, rows)
        out_ref[:, pl.ds(at, rows), :] = ref[...]


def join(idx, own, other_y, other_core):
    rows, part = own.shape[2:]
    vmem = pl.BlockSpec(memory_space=pltpu.VMEM)
    return pl.pallas_call(
        join_kernel,
        in_specs=[SMEM] + [vmem] * 3,
        out_specs=vmem,
        out_shape=sds((2, 4 * rows, part), BF),
        compiler_params=BIG,
        cost_estimate=work(1e9),
        name="join",
    )(idx, own, other_y, other_core)


def tuned(mesh):
    swap_bits = make_links(8, 4)

    def swap(value, name):
        return swap_bits(value, *BITS[name])

    def add(a, b):
        return (a.astype(F32) + b.astype(F32)).astype(BF)

    def along(value, index, axis):
        return lax.dynamic_index_in_dim(value, index, axis, keepdims=False)

    def shards(
        inputs,
        lengths,
        ln1_gain,
        ln1_bias,
        w_qkv,
        w_out,
        scale_attn,
        ln2_gain,
        ln2_bias,
        w_gate,
        w_up,
        w_down,
        scale_mlp,
        grad_out,
    ):
        count, width = inputs.shape
        head_width = width // HEADS
        group, rep = lax.axis_index("group"), lax.axis_index("rep")
        z, x, y, core = group // 2, group % 2, rep // 2, rep % 2
        idx = jnp.stack([z, x, y, core]).astype(jnp.int32)

        vectors = jnp.stack([ln1_gain, ln1_bias, scale_attn, ln2_gain, ln2_bias, scale_mlp], axis=1)
        vectors = jnp.pad(vectors, ((0, 0), (0, 122)))
        bundle = jnp.concatenate([w_qkv, w_out, vectors], axis=1)[None]
        from_z = [swap(bundle, n) for n in ("z1", "z2", "z3")]
        raw = jnp.stack([w_gate, w_up])
        raw_x = swap(raw, "x")
        share_here, share_there = share(idx, raw)
        share_y = swap(share_there, "y")

        segment, position = clip_layout(lengths[0], count)
        cosine, sine = lane_tables(position, head_width)
        position = position[:, None]

        share_core = swap(jnp.stack([share_here[1], share_y[1]]), "core")
        gu0 = join(idx, share_here, share_y, share_core)
        dnx0 = swap(w_down, "x")
        share_here, share_there = share(idx, raw_x)
        *from_z, gu0, dnx0, cosine, sine, position, share_here, share_there = window(
            *from_z, gu0, dnx0, cosine, sine, position, share_here, share_there
        )
        near = jnp.concatenate([bundle] + from_z)
        near, gu0, share_here, share_there = window(near, gu0, share_here, share_there)
        far_x, far_y = swap(near, "x"), swap(near, "y")
        gu1, gu2 = swap(gu0, "z1"), swap(gu0, "z2")
        share_y = swap(share_there, "y")
        far_x, far_y, gu1, gu2, share_y, share_here, w_down = window(
            far_x, far_y, gu1, gu2, share_y, share_here, w_down
        )
        by_y, by_x, w_down, near = window(far_x[:3], far_y[3:], w_down, near)
        both_y, both_x = swap(by_y, "y"), swap(by_x, "x")
        dn1, dn2 = swap(w_down, "z1"), swap(w_down, "z2")
        came_near = swap(near, "core")

        have = [near, far_x, far_y, both_y, both_x]
        gu0, gu1, gu2, dn1, dn2, grad_out, came_near, *have = window(
            gu0, gu1, gu2, dn1, dn2, grad_out, came_near, *have
        )
        came = [came_near] + [swap(p, "core") for p in have[1:]]
        gu3, go_y = swap(gu0, "z3"), swap(grad_out, "y")
        gux1, dnx1, dnx2 = swap(gu1, "x"), swap(dn1, "x"), swap(dn2, "x")
        *came, cosine, sine, position = window(*came, cosine, sine, position)

        qkv, normed, w_attn, vecs = project(idx, have, came, inputs, cosine, sine)
        qkv, gu2, dnx1, dnx2, gux1, gu3, w_down, share_here, share_y = window(
            qkv, gu2, dnx1, dnx2, gux1, gu3, w_down, share_here, share_y
        )
        share_core = swap(jnp.stack([share_here[1], share_y[1]]), "core")
        gux2, dn3 = swap(gu2, "x"), swap(w_down, "z3")
        gux3 = swap(gu3, "x")
        attended = attend(qkv, position)
        attended, gux2, go_y, dn3, share_core = window(attended, gux2, go_y, dn3, share_core)
        gux0 = join(idx, share_here, share_y, share_core)
        dnx3 = swap(dn3, "x")
        branch, n_own = leave(attended, w_attn, inputs, vecs)
        n_own, gux0, gux3, dnx3, grad_out, go_y = window(n_own, gux0, gux3, dnx3, grad_out, go_y)

        n_y, n_core = swap(n_own, "y"), swap(n_own, "core")
        go_core = swap(grad_out, "core")
        n_core, go_core = window(n_core, go_core)
        go_yc = swap(go_y, "core")
        pieces = (gu0, gux0, gu1, gux1, gu2, gux2, gu3, gux3)
        downs = (w_down, dnx0, dn1, dnx1, dn2, dnx2, dn3, dnx3)
        gg_a, gu_a, gn_own, gn_core, mlp_own, mlp_core, total = mlp_both(
            idx, pieces, downs, (n_own, n_core), (grad_out, go_core), vecs
        )
        n_y, go_y, go_yc, gn_core = window(n_y, go_y, go_yc, gn_core)
        n_yc = swap(n_y, "core")
        n_y, n_yc = window(n_y, n_yc)
        gn_core, mlp_core = swap(gn_core, "core"), swap(mlp_core, "core")
        gg_b, gu_b, gn_y, gn_yc, mlp_y, mlp_yc, down_send, down_keep = mlp_both(
            idx, pieces, downs, (n_y, n_yc), (go_y, go_yc), vecs, total
        )
        gn_y, gn_yc, gn_core, mlp_core, down_send = window(gn_y, gn_yc, gn_core, mlp_core, down_send)
        down_x = swap(down_send, "x")
        gn_yc = swap(gn_yc, "core")
        gn_y, gn_yc = window(gn_y, gn_yc)
        gn_send, gu_b, mlp_yc = window(add(gn_y, gn_yc), gu_b, mlp_yc)
        gn_y = swap(gn_send, "y")
        mlp_yc = swap(mlp_yc, "core")

        n_all = (n_own, n_core, n_y, n_yc)
        up_send, up_keep = weight_grad(idx, n_all, (gu_a, gu_b))
        gate_send, gate_keep = weight_grad(idx, n_all, (after(gg_a, up_send), gg_b))
        gate_send, up_send, mlp_yc, down_x = window(gate_send, up_send, mlp_yc, down_x)
        down_near = near_sum(idx, [(down_keep, down_x)])
        gn_y, mlp_send, up_send, down_near = window(
            gn_y, add(mlp_y, mlp_yc), up_send, down_near
        )
        up_x, mlp_y, down_near = swap(up_send, "x"), swap(mlp_send, "y"), swap(down_near, "z1")

        grad_middle, grad_branch, grad_attended, mid_sums = back(
            (gn_own, gn_core, gn_y), grad_out, branch, inputs, vecs, w_attn
        )
        grad_attended, gate_send = window(grad_attended, gate_send)
        gate_x = swap(gate_send, "x")

        dq, dk, dv = attend_back(qkv, grad_attended, position, cosine, sine)
        dq, mlp_y, up_x, down_near = window(dq, mlp_y, up_x, down_near)
        up_near, dq = window(near_sum(idx, [(up_keep, up_x)]), dq)
        up_near = swap(up_near, "z1")
        grads = attn_grad(idx, normed, attended, dq, dk, dv, grad_branch)
        gate_x, up_near, *grads = window(gate_x, up_near, *grads)
        near = jnp.concatenate([down_near, up_near])
        pairs = [(down_keep, down_x), (up_keep, up_x), (gate_keep, gate_x)]
        q_send, k_send, a_send, a_keep, a_keep_here = grads[:5]
        v_send, o_send, b_send, b_keep, b_keep_here = grads[5:]

        away = [swap(v, "core") for v in (q_send, k_send, v_send, o_send)]
        late = (near, dq, dk, dv, mlp_y, a_send, b_send)
        *away, near, dq, dk, dv, mlp_y, a_send, b_send = window(*away, *late)
        a_core, b_core = swap(a_send, "core"), swap(b_send, "core")
        a_away, b_away, far, gate_near = first_sum(
            idx, (a_keep, *away[:2], b_keep, *away[2:]), near, pairs
        )
        late = (a_core, b_core, dq, dk, dv, mlp_y)
        a_away, b_away, far, gate_near, *late = window(a_away, b_away, far, gate_near, *late)
        a_core, b_core, dq, dk, dv, mlp_y = late
        a_x, b_y = swap(a_away, "x"), swap(b_away, "y")
        far, gate_near = swap(far, "z2"), swap(gate_near, "z1")
        input_grad, block_out, small = last(
            (dq, dk, dv),
            w_attn,
            inputs,
            vecs,
            grad_middle,
            (mlp_own, mlp_core, mlp_y),
            grad_out,
            branch,
            mid_sums,
        )
        small = small + swap(small, "core")
        small = small + swap(small, "x")
        a_x, b_y, small, gate_near, far = window(a_x, b_y, small, gate_near, far)
        parts = (a_keep_here, a_core, a_x, b_keep_here, b_core, b_y)
        a_away, b_away, gate_far = second_sum(idx, parts, gate_near, pairs[2])
        a_away, b_away, gate_far, small, *parts = window(a_away, b_away, gate_far, small, *parts)
        a_y, b_x, gate_far = swap(a_away, "y"), swap(b_away, "x"), swap(gate_far, "z2")
        a_stay, b_stay, own = stay_sum(idx, parts, near, far, pairs[:2])
        small = small + swap(small, "y")
        rows_of = small[:6].reshape(6, 4, 2, 2, 2, 32)
        rows_of = along(along(along(rows_of, x, 2), y, 2), core, 2)
        rows_of = jnp.pad(rows_of.transpose(1, 2, 0), ((0, 0), (0, 0), (0, 122))).astype(BF)
        a_y, b_x, rows_of, gate_far = window(a_y, b_x, rows_of, gate_far)
        own, mine, *sends = third_sum(
            idx, a_stay, a_y, b_stay, b_x, rows_of, own, gate_near, gate_far, pairs[2]
        )
        *sends, own, mine = window(*sends, own, mine)
        got = [swap(v, n) for v, n in zip(sends, ("z1", "z2", "z3"))]
        own_y, own_core = swap(own, "y"), swap(own, "core")
        *got, own, own_y, own_core = window(*got, own, own_y, own_core)
        mine = mine + (got[0].astype(F32) + got[1].astype(F32) + got[2].astype(F32))
        mine, own, own_y, own_core = window(mine.astype(BF), own, own_y, own_core)
        other, mine_core, own_both = swap(mine, "y"), swap(mine, "core"), swap(own_y, "core")
        w_down_grad, w_up_grad, w_gate_grad = place_mlp(idx, own, own_y, own_core, own_both)
        other, mine_core, w_down_grad, w_up_grad, w_gate_grad = window(
            other, mine_core, w_down_grad, w_up_grad, w_gate_grad
        )
        other_core = swap(other, "core")
        w_qkv_grad, w_out_grad, *small = place_rows(
            idx, mine, other, mine_core, other_core, (3 * width, width), 6
        )
        return (
            block_out,
            input_grad,
            small[0],
            small[1],
            w_qkv_grad,
            w_out_grad,
            small[2],
            small[3],
            small[4],
            w_gate_grad,
            w_up_grad,
            w_down_grad,
            small[5],
        )

    return shards


def plain(mesh):
    n_group, n_rep = mesh.shape["group"], mesh.shape["rep"]
    swap = make_links(n_group, n_rep)

    def gather_group(piece, group):
        return lax.all_gather(piece, "group", axis=0)
    def gather_all(piece, group, rep):
        full = lax.all_gather(piece, AXES, axis=0)
        return full.reshape((n_group, n_rep) + piece.shape)

    def gather_rep(piece):
        low = jnp.concatenate([piece, swap(piece, 0, 2)], axis=0)
        return jnp.concatenate([low, swap(low, 0, 1)], axis=0)

    def scatter_rep(blocks):
        half = blocks.shape[0] // 2
        low = blocks[:half].astype(F32) + swap(blocks[half:], 0, 1).astype(F32)
        quarter = half // 2
        return low[:quarter] + swap(low[quarter:].astype(BF), 0, 2).astype(F32)

    def scatter_group(grads, group):
        return lax.psum_scatter(grads, "group", scatter_dimension=0, tiled=False).astype(F32)

    def whole_rep(piece, rep):
        piece = piece.astype(BF)
        return lax.all_gather(piece, "rep", axis=0).astype(F32)

    def scatter_attn(grads, group, rep):
        part = lax.psum_scatter(grads, "group", scatter_dimension=0, tiled=True)
        return lax.psum(part, "rep").astype(F32)

    def sum_all(value):
        return lax.psum(value, AXES)

    def shards(
        inputs,
        lengths,
        ln1_gain,
        ln1_bias,
        w_qkv,
        w_out,
        scale_attn,
        ln2_gain,
        ln2_bias,
        w_gate,
        w_up,
        w_down,
        scale_mlp,
        grad_out,
    ):
        count, width = inputs.shape
        head_width = width // HEADS
        group, rep = lax.axis_index("group"), lax.axis_index("rep")
        rows = w_qkv.shape[0]
        ff = w_gate.shape[1]
        part_ff = ff // n_rep
        vectors = jnp.stack([ln1_gain, ln1_bias, scale_attn, ln2_gain, ln2_bias, scale_mlp], axis=1)
        vectors = jnp.pad(vectors, ((0, 0), (0, 128 - vectors.shape[1])))
        bundle = jnp.concatenate([w_qkv, w_out, vectors], axis=1)
        attn_full = gather_all(bundle, group, rep).reshape(width, -1)
        qkv_full = attn_full[:, : 3 * width]
        out_full = attn_full[:, 3 * width : 4 * width]
        vecs = attn_full[:, 4 * width : 4 * width + 6].T.astype(F32)
        gain_one, bias_one, attn_scale, gain_two, bias_two, mlp_scale = [vecs[i] for i in range(6)]

        def columns(w):
            blocks = w.reshape(rows, n_group, n_rep, ff // (n_group * n_rep))
            return blocks.transpose(2, 0, 1, 3).reshape(n_rep, rows, part_ff)

        pair = jnp.stack([columns(w_gate), columns(w_up)], axis=1)
        came = [pick(pair, rep)] + [swap(pick(pair, rep ^ d), 0, d) for d in (1, 2, 3)]
        came = jnp.stack(came)
        gate_up = jnp.stack([pick(came, rep ^ j) for j in range(n_rep)], axis=1)
        gate_up = gate_up.reshape(2, n_rep * rows, part_ff)
        down_rows = w_down.shape[0]
        gate_all = gather_group(gate_up[0], group).reshape(width, part_ff)
        up_all = gather_group(gate_up[1], group).reshape(width, part_ff)
        down_all = gather_group(w_down, group).reshape(part_ff, width)

        cot_all = gather_rep(grad_out)

        segment, position = clip_layout(lengths[0], count)
        cosine, sine = rotary_tables(position, head_width)
        frames = inputs.astype(F32)
        unit_one, inverse_one = norm_parts(frames)
        normed = (unit_one * gain_one + bias_one).astype(BF)
        projected = jnp.dot(normed, qkv_full, preferred_element_type=F32)
        queries = rotate(
            projected[:, :width].reshape(count, HEADS, head_width), cosine, sine
        ).astype(BF)
        keys_rot = rotate(
            projected[:, width : 2 * width].reshape(count, HEADS, head_width), cosine, sine
        ).astype(BF)
        values = projected[:, 2 * width :].reshape(count, HEADS, head_width).astype(BF)
        attended, log_totals = attention_forward(queries, keys_rot, values, segment, count, WINDOW)
        attended = attended.reshape(count, width).astype(BF)
        branch = jnp.dot(attended, out_full, preferred_element_type=F32)
        middle = frames + attn_scale * branch
        unit_two, inverse_two = norm_parts(middle)
        normed_two = (unit_two * gain_two + bias_two).astype(BF)

        normed_all = gather_rep(normed_two)
        gate = jnp.dot(normed_all, gate_all, preferred_element_type=F32)
        up_value = jnp.dot(normed_all, up_all, preferred_element_type=F32)
        sigmoid_gate = jax.nn.sigmoid(gate)
        silu_gate = gate * sigmoid_gate
        hidden = (silu_gate * up_value).astype(BF)
        mlp_part = jnp.dot(hidden, down_all, preferred_element_type=F32).astype(BF)
        mlp = scatter_rep(mlp_part)
        block_out = (middle + mlp_scale * mlp).astype(BF)
        cotangent = grad_out.astype(F32)
        scale_mlp_grad = jnp.sum(cotangent * mlp, axis=0)
        grad_mlp = (mlp_scale * cot_all.astype(F32)).astype(BF)

        def grad_blocks(a, b):
            out = jnp.einsum("td,te->de", a, b, preferred_element_type=F32).astype(BF)
            return out.reshape(n_group, out.shape[0] // n_group, out.shape[1])

        w_down_part = scatter_group(grad_blocks(hidden, grad_mlp), group)
        grad_hidden = jnp.einsum("td,fd->tf", grad_mlp, down_all, preferred_element_type=F32)
        grad_gate = (
            grad_hidden * up_value * sigmoid_gate * (1.0 + gate * (1.0 - sigmoid_gate))
        ).astype(BF)
        grad_up = (grad_hidden * silu_gate).astype(BF)
        grad_normed_part = jnp.einsum(
            "tf,df->td", grad_gate, gate_all, preferred_element_type=F32
        ) + jnp.einsum("tf,df->td", grad_up, up_all, preferred_element_type=F32)
        grad_normed_two = scatter_rep(grad_normed_part.astype(BF))
        w_gate_part = scatter_group(grad_blocks(normed_all, grad_gate), group)
        w_up_part = scatter_group(grad_blocks(normed_all, grad_up), group)

        def hidden_columns(part):
            full = whole_rep(part, rep)
            full = full.reshape(n_rep, full.shape[1], n_group, ff // (n_group * n_rep))
            return full.transpose(1, 2, 0, 3).reshape(full.shape[1], ff)

        w_gate_grad = hidden_columns(w_gate_part)
        w_up_grad = hidden_columns(w_up_part)
        w_down_grad = whole_rep(w_down_part, rep).reshape(n_rep * down_rows, width)

        ln2_gain_grad = jnp.sum(grad_normed_two * unit_two, axis=0)
        ln2_bias_grad = jnp.sum(grad_normed_two, axis=0)
        grad_middle = cotangent + norm_back(grad_normed_two, unit_two, inverse_two, gain_two)
        scale_attn_grad = jnp.sum(grad_middle * branch, axis=0)
        grad_branch = (attn_scale * grad_middle).astype(BF)
        w_out_part = jnp.einsum("td,te->de", attended, grad_branch, preferred_element_type=F32)
        w_out_grad = scatter_attn(w_out_part.astype(BF), group, rep)
        grad_attended = jnp.einsum(
            "te,de->td", grad_branch, out_full, preferred_element_type=F32
        ).astype(BF)
        grad_queries, grad_keys, grad_values = attention_backward(
            queries,
            keys_rot,
            values,
            grad_attended.reshape(count, HEADS, head_width),
            log_totals,
            segment,
            count,
            WINDOW,
        )
        grad_projected = jnp.concatenate(
            [
                rotate_back(grad_queries, cosine, sine).reshape(count, width),
                rotate_back(grad_keys, cosine, sine).reshape(count, width),
                grad_values.reshape(count, width),
            ],
            axis=1,
        ).astype(BF)
        w_qkv_part = jnp.einsum("td,te->de", normed, grad_projected, preferred_element_type=F32)
        w_qkv_grad = scatter_attn(w_qkv_part.astype(BF), group, rep)
        grad_normed = jnp.einsum(
            "te,de->td", grad_projected, qkv_full, preferred_element_type=F32
        )
        ln1_gain_grad = jnp.sum(grad_normed * unit_one, axis=0)
        ln1_bias_grad = jnp.sum(grad_normed, axis=0)
        input_grad = grad_middle + norm_back(grad_normed, unit_one, inverse_one, gain_one)
        small = sum_all(
            jnp.stack(
                [
                    ln1_gain_grad,
                    ln1_bias_grad,
                    scale_attn_grad,
                    ln2_gain_grad,
                    ln2_bias_grad,
                    scale_mlp_grad,
                ]
            )
        )
        own = width // n_group
        small = lax.dynamic_slice_in_dim(small, group * own, own, 1)
        return (
            block_out,
            input_grad,
            small[0],
            small[1],
            w_qkv_grad,
            w_out_grad,
            small[2],
            small[3],
            small[4],
            w_gate_grad,
            w_up_grad,
            w_down_grad,
            small[5],
        )

    return shards


def solution(mesh):
    n_group, n_rep = mesh.shape["group"], mesh.shape["rep"]
    shards = tuned(mesh) if n_group == 8 and n_rep == 4 else plain(mesh)
    rowed, flat = P(AXES, None), P(AXES)
    in_specs = (
        rowed, rowed, flat, flat, rowed, rowed, flat, flat, flat, rowed, rowed, rowed, flat, rowed,
    )
    own_rows, own_flat = P("group", None), P("group")
    out_specs = (
        rowed, rowed, own_flat, own_flat, own_rows, own_rows, own_flat, own_flat, own_flat,
        own_rows, own_rows, own_rows, own_flat,
    )
    return jax.shard_map(shards, mesh=mesh, in_specs=in_specs, out_specs=out_specs, check_vma=False)
```

```python
import math

import jax
import jax.numpy as jnp
from jax import lax
from jax.experimental import pallas as pl
from jax.experimental.pallas import tpu as pltpu
from jax.sharding import PartitionSpec as P

HEADS = 16
WINDOW = 128
EPS = 1e-05
AXES = ("group", "rep")
BF = jnp.bfloat16
F32 = jnp.float32


def clip_layout(length_row, count):
    clip_ends = jnp.cumsum(length_row)
    clip_starts = clip_ends - length_row
    row_index = jnp.arange(count, dtype=jnp.int32)
    segment = jnp.sum((row_index[:, None] >= clip_ends[None, :]).astype(jnp.int32), axis=1)
    member = (segment[:, None] == jnp.arange(length_row.shape[0], dtype=jnp.int32)[None, :]).astype(
        jnp.int32
    )
    position = row_index - jnp.sum(member * clip_starts[None, :], axis=1)
    return (segment, position)


def rotary_tables(position, width):
    half = width // 2
    freqs = jnp.power(10000.0, -jnp.arange(half, dtype=F32) * (2.0 / width))
    angles = position.astype(F32)[:, None] * freqs[None, :]
    cosine = jnp.concatenate([jnp.cos(angles), jnp.cos(angles)], axis=1)
    sine = jnp.concatenate([jnp.sin(angles), jnp.sin(angles)], axis=1)
    return (cosine[:, None, :], sine[:, None, :])


def rotate(values, cosine, sine):
    half = values.shape[-1] // 2
    turned = jnp.concatenate([-values[..., half:], values[..., :half]], axis=-1)
    return values * cosine + turned * sine


def rotate_back(values, cosine, sine):
    half = values.shape[-1] // 2
    turned = jnp.concatenate([values[..., half:], -values[..., :half]], axis=-1)
    return values * cosine + turned * sine


def norm_parts(values):
    mean_value = jnp.mean(values, axis=-1, keepdims=True)
    centered = values - mean_value
    variance = jnp.mean(centered * centered, axis=-1, keepdims=True)
    inverse = lax.rsqrt(variance + EPS)
    return (centered * inverse, inverse)


def norm_back(grad_normed, unit, inverse, gain):
    scaled = grad_normed * gain
    return inverse * (
        scaled
        - jnp.mean(scaled, axis=-1, keepdims=True)
        - unit * jnp.mean(scaled * unit, axis=-1, keepdims=True)
    )


def block_allowed(segment, segment_pad, start, block, window):
    query_index = start + jnp.arange(block, dtype=jnp.int32)
    key_index = start - window + jnp.arange(block + window, dtype=jnp.int32)
    offset = query_index[:, None] - key_index[None, :]
    same_clip = segment[:, None] == segment_pad[None, :]
    return same_clip & (offset >= 0) & (offset < window)


def pad_front(values, window, fill):
    front = jnp.full((window,) + values.shape[1:], fill, values.dtype)
    return jnp.concatenate([front, values], axis=0)


def attention_forward(queries, keys_rot, values, segment, block, window):
    factor = 1.0 / math.sqrt(queries.shape[-1])
    keys_pad = pad_front(keys_rot, window, 0)
    values_pad = pad_front(values, window, 0)
    segment_pad = pad_front(segment, window, -1)
    allowed = block_allowed(segment, segment_pad, 0, block, window)
    scores = (
        jnp.einsum("qhd,khd->hqk", queries, keys_pad, preferred_element_type=F32) * factor
    )
    masked = jnp.where(allowed[None], scores, -jnp.inf)
    peak = jnp.max(masked, axis=-1, keepdims=True)
    expd = jnp.exp(masked - peak)
    totals = jnp.sum(expd, axis=-1, keepdims=True)
    probs = (expd / totals).astype(BF)
    outputs = jnp.einsum("hqk,khd->qhd", probs, values_pad, preferred_element_type=F32)
    log_totals = peak + jnp.log(totals)
    return (outputs, log_totals)


def attention_backward(
    queries, keys_rot, values, grad_attended, log_totals, segment, block, window
):
    factor = 1.0 / math.sqrt(queries.shape[-1])
    keys_pad = pad_front(keys_rot, window, 0)
    values_pad = pad_front(values, window, 0)
    segment_pad = pad_front(segment, window, -1)
    allowed = block_allowed(segment, segment_pad, 0, block, window)
    scores = (
        jnp.einsum("qhd,khd->hqk", queries, keys_pad, preferred_element_type=F32) * factor
    )
    probs = jnp.where(
        allowed[None], jnp.exp(jnp.where(allowed[None], scores, -jnp.inf) - log_totals), 0.0
    )
    probs_low = probs.astype(BF)
    grad_probs = jnp.einsum("qhd,khd->hqk", grad_attended, values_pad, preferred_element_type=F32)
    delta = jnp.sum(probs * grad_probs, axis=-1, keepdims=True)
    grad_scores = (probs * (grad_probs - delta)).astype(BF)
    grad_queries = (
        jnp.einsum("hqk,khd->qhd", grad_scores, keys_pad, preferred_element_type=F32) * factor
    )
    key_part = (
        jnp.einsum("hqk,qhd->khd", grad_scores, queries, preferred_element_type=F32) * factor
    )
    value_part = jnp.einsum("hqk,qhd->khd", probs_low, grad_attended, preferred_element_type=F32)
    return (grad_queries, key_part[window:], value_part[window:])


def make_links(n_group, n_rep):
    def swap(value, group_bits, rep_bits):
        pairs = [
            (g * n_rep + r, (g ^ group_bits) * n_rep + (r ^ rep_bits))
            for g in range(n_group)
            for r in range(n_rep)
        ]
        return lax.ppermute(value, AXES, pairs)

    return swap


def pick(stacked, index):
    return lax.dynamic_index_in_dim(stacked, index, 0, keepdims=False)


BITS = {"z1": (2, 0), "z2": (4, 0), "z3": (6, 0), "x": (1, 0), "y": (0, 2), "core": (0, 1)}
CONTRACT = {
    "nn": (((1,), (0,)), ((), ())),
    "nt": (((1,), (1,)), ((), ())),
    "tn": (((0,), (0,)), ((), ())),
}


def vmem_of(mib):
    return pltpu.CompilerParams(vmem_limit_bytes=mib << 20)


def work(flops):
    return pl.CostEstimate(flops=int(flops), bytes_accessed=0, transcendentals=0)


ANY = pl.BlockSpec(memory_space=pl.ANY)
SMEM = pl.BlockSpec(memory_space=pltpu.SMEM)


def dot(a, b, form="nn"):
    return lax.dot_general(a, b, CONTRACT[form], preferred_element_type=F32)


def after(value, *done):
    return lax.optimization_barrier((value,) + done)[0]


def window(*values):
    return lax.optimization_barrier(values)


def lane_tables(position, width):
    lane = jnp.arange(2 * width, dtype=jnp.int32)
    index = (lane % (width // 2)).astype(F32)
    freqs = jnp.power(10000.0, -index * (2.0 / width))
    angles = position.astype(F32)[:, None] * freqs[None, :]
    sign = jnp.where(lane % width < width // 2, -1.0, 1.0)
    return jnp.cos(angles), jnp.sin(angles) * sign[None, :]


def sds(shape, dtype):
    return jax.ShapeDtypeStruct(shape, dtype)


def whole(shape):
    return pl.BlockSpec(shape, lambda *_: (0,) * len(shape))


def rotate_lanes(u, cosine, signed_sine, first):
    turned = jnp.where(first, pltpu.roll(u, 96, 1), pltpu.roll(u, 32, 1))
    return u * cosine + turned * signed_sine


PIECES = (
    ((0, 0, 0), (1, 0, 0), (2, 0, 0), (3, 0, 0)),
    ((0, 1, 0), (1, 1, 0), (2, 1, 0), (3, 1, 0)),
    ((0, 0, 1), (1, 0, 1), (2, 0, 1), (3, 0, 1)),
    ((0, 1, 1), (1, 1, 1), (2, 1, 1), (3, 1, 1)),
)


def project_kernel(*refs):
    n = len(PIECES)
    idx, own, came = refs[0], refs[1 : 1 + n], refs[1 + n : 1 + 2 * n]
    x_ref, cos_ref, sin_ref = refs[1 + 2 * n : 4 + 2 * n]
    qkv_ref, normed_ref, w_ref, vec_ref, weights, sems, out_sem = refs[4 + 2 * n :]
    j, steps = pl.program_id(0), pl.num_programs(0)
    block = qkv_ref.shape[1]

    def copies():
        out, count = [], 0
        for core_bit, group in ((0, own), (1, came)):
            for ref, owners in zip(group, PIECES):
                for i, (k, dx, dy) in enumerate(owners):
                    owner = (((idx[0] ^ k) * 2 + (idx[1] ^ dx)) * 2 + (idx[2] ^ dy)) * 2
                    row = pl.multiple_of((owner + (idx[3] ^ core_bit)) * 32, 32)
                    out.append(
                        pltpu.make_async_copy(
                            ref.at[i], weights.at[pl.ds(row, 32), :], sems.at[count]
                        )
                    )
                    count += 1
        return out

    def save():
        return pltpu.make_async_copy(weights, w_ref, out_sem)

    @pl.when(j == 0)
    def _():
        pieces = copies()
        for c in pieces:
            c.start()
        x = x_ref[...].astype(F32)
        centered = x - jnp.mean(x, axis=1, keepdims=True)
        unit = centered * lax.rsqrt(jnp.mean(centered * centered, axis=1, keepdims=True) + EPS)
        for c in pieces:
            c.wait()
        save().start()
        vecs = weights[:, weights.shape[1] - 128 :].astype(F32).T
        vec_ref[...] = vecs[:8]
        normed_ref[...] = (unit * vecs[0:1] + vecs[1:2]).astype(BF)

    p = dot(normed_ref[...], weights[:, pl.ds(pl.multiple_of(j * block, block), block)])
    lane = lax.broadcasted_iota(jnp.int32, (1, 128), 1)
    first = (lane % 64) < 32

    @pl.when(j * 3 < 2 * steps)
    def _():
        for c in range(0, block, 128):
            cols = slice(c, c + 128)
            qkv_ref[:, cols] = rotate_lanes(p[:, cols], cos_ref[...], sin_ref[...], first).astype(BF)

    @pl.when(j * 3 >= 2 * steps)
    def _():
        qkv_ref[...] = p.astype(BF)

    @pl.when(j == steps - 1)
    def _():
        save().wait()


def project(idx, own, came, x, cosine, signed_sine, block=1024):
    rows, width = x.shape
    cols = own[0].shape[-1]
    return pl.pallas_call(
        project_kernel,
        grid=(3 * width // block,),
        in_specs=[SMEM] + [ANY] * (2 * len(PIECES)) + [whole((rows, width))] + [whole((rows, 128))] * 2,
        out_specs=[
            pl.BlockSpec((rows, block), lambda j: (0, j)),
            whole((rows, width)),
            ANY,
            whole((8, width)),
        ],
        out_shape=[
            sds((rows, 3 * width), BF),
            sds((rows, width), BF),
            sds((width, cols), BF),
            sds((8, width), F32),
        ],
        scratch_shapes=[
            pltpu.VMEM((width, cols), BF),
            pltpu.SemaphoreType.DMA((32,)),
            pltpu.SemaphoreType.DMA,
        ],
        compiler_params=vmem_of(28),
        cost_estimate=work(1e9),
        name="project",
    )(idx, *own, *came, x, cosine, signed_sine)


def unit_of(values):
    centered = values - jnp.mean(values, axis=1, keepdims=True)
    inverse = lax.rsqrt(jnp.mean(centered * centered, axis=1, keepdims=True) + EPS)
    return centered * inverse, inverse


def unit_back(grad, unit, inverse, gain):
    scaled = grad * gain
    return inverse * (
        scaled
        - jnp.mean(scaled, axis=1, keepdims=True)
        - unit * jnp.mean(scaled * unit, axis=1, keepdims=True)
    )


def add_rows(ref, row, values):
    total = jnp.sum(values, axis=0, keepdims=True)

    @pl.when(pl.program_id(0) == 0)
    def _():
        ref[row : row + 1, :] = total

    @pl.when(pl.program_id(0) > 0)
    def _():
        ref[row : row + 1, :] += total


def leave_kernel(attended_ref, w_ref, x_ref, vec_ref, branch_ref, n_ref):
    branch = dot(attended_ref[...], w_ref[...])
    branch_ref[...] = branch
    unit, _ = unit_of(x_ref[...].astype(F32) + vec_ref[2:3] * branch)
    n_ref[...] = (unit * vec_ref[3:4] + vec_ref[4:5]).astype(BF)


def leave(attended, w_attn, x, vecs, block=256):
    rows, width = x.shape
    row = pl.BlockSpec((block, width), lambda i: (i, 0))
    return pl.pallas_call(
        leave_kernel,
        grid=(rows // block,),
        in_specs=[row, pl.BlockSpec((width, width), lambda i: (0, 3)), row, whole((8, width))],
        out_specs=[row, row],
        out_shape=[sds((rows, width), F32), sds((rows, width), BF)],
        compiler_params=vmem_of(20),
        cost_estimate=work(1e9),
        name="leave",
    )(attended, w_attn, x, vecs)


def back_kernel(
    a_ref, b_ref, c_ref, go_ref, branch_ref, x_ref, vec_ref, w_ref, gm_ref, gb_ref, ga_ref, sum_ref
):
    grad = a_ref[...].astype(F32) + b_ref[...].astype(F32) + c_ref[...].astype(F32)
    branch = branch_ref[...]
    unit, inverse = unit_of(x_ref[...].astype(F32) + vec_ref[2:3] * branch)

    @pl.when(pl.program_id(0) == 0)
    def _():
        sum_ref[...] = jnp.zeros_like(sum_ref)

    add_rows(sum_ref, 3, grad * unit)
    add_rows(sum_ref, 4, grad)
    grad_middle = go_ref[...].astype(F32) + unit_back(grad, unit, inverse, vec_ref[3:4])
    gm_ref[...] = grad_middle
    add_rows(sum_ref, 2, grad_middle * branch)
    grad_branch = (vec_ref[2:3] * grad_middle).astype(BF)
    gb_ref[...] = grad_branch
    ga_ref[...] = dot(grad_branch, w_ref[...], "nt").astype(BF)


def back(parts, grad_out, branch, x, vecs, w_attn, block=256):
    rows, width = x.shape
    row = pl.BlockSpec((block, width), lambda i: (i, 0))
    return pl.pallas_call(
        back_kernel,
        grid=(rows // block,),
        in_specs=[row] * 6
        + [whole((8, width)), pl.BlockSpec((width, width), lambda i: (0, 3))],
        out_specs=[row, row, row, whole((8, width))],
        out_shape=[sds((rows, width), F32)] + [sds((rows, width), BF)] * 2 + [sds((8, width), F32)],
        compiler_params=vmem_of(28),
        cost_estimate=work(1e9),
        name="back",
    )(*parts, grad_out, branch, x, vecs, w_attn)


def last_kernel(*refs):
    dq, dk, dv, wq, wk, wv, x_ref, vec_ref, gm_ref, m0, m1, m2, go_ref, branch_ref, mid_ref = refs[:15]
    ig_ref, out_ref, sum_ref = refs[15:]
    grad = dot(dq[...], wq[...], "nt") + dot(dk[...], wk[...], "nt") + dot(dv[...], wv[...], "nt")
    x = x_ref[...].astype(F32)
    unit, inverse = unit_of(x)

    @pl.when(pl.program_id(0) == 0)
    def _():
        sum_ref[...] = mid_ref[...]

    add_rows(sum_ref, 0, grad * unit)
    add_rows(sum_ref, 1, grad)
    ig_ref[...] = gm_ref[...] + unit_back(grad, unit, inverse, vec_ref[0:1])
    mlp = m0[...].astype(F32) + m1[...].astype(F32) + m2[...].astype(F32)
    out_ref[...] = (x + vec_ref[2:3] * branch_ref[...] + vec_ref[5:6] * mlp).astype(BF)
    add_rows(sum_ref, 5, go_ref[...].astype(F32) * mlp)


def last(grads, w_attn, x, vecs, grad_middle, mlp_parts, grad_out, branch, mid_sums, block=256):
    rows, width = x.shape
    row = pl.BlockSpec((block, width), lambda i: (i, 0))
    columns = [pl.BlockSpec((width, width), lambda i, n=n: (0, n)) for n in range(3)]
    return pl.pallas_call(
        last_kernel,
        grid=(rows // block,),
        in_specs=[row] * 3
        + columns
        + [row, whole((8, width))]
        + [row] * 6
        + [whole((8, width))],
        out_specs=[row, row, whole((8, width))],
        out_shape=[sds((rows, width), F32), sds((rows, width), BF), sds((8, width), F32)],
        compiler_params=vmem_of(36),
        cost_estimate=work(1e9),
        name="last",
    )(*grads, w_attn, w_attn, w_attn, x, vecs, grad_middle, *mlp_parts, grad_out, branch, mid_sums)


def set_bias(bias_ref, pos_ref, rows):
    for b in range(rows // WINDOW):
        keys = WINDOW if b == 0 else 2 * WINDOW
        offset = (
            lax.broadcasted_iota(jnp.int32, (keys, WINDOW), 1)
            - lax.broadcasted_iota(jnp.int32, (keys, WINDOW), 0)
            + (keys - WINDOW)
        )
        reach = jnp.minimum(pos_ref[:, b * WINDOW : (b + 1) * WINDOW], WINDOW - 1)
        bias = jnp.where((offset >= 0) & (offset <= reach), 0.0, -1e30)
        bias_ref[b, 2 * WINDOW - keys :, :WINDOW] = bias
        bias_ref[b, 2 * WINDOW - keys :, WINDOW:] = bias


def split_heads(u, low):
    zero = jnp.zeros_like(u)
    return jnp.concatenate([jnp.where(low, u, zero), jnp.where(low, zero, u)], axis=0)


def pair_probs(q, k, bias, low):
    q = split_heads(q, low) * jnp.asarray(0.125, BF)
    scores = dot(k, q, "nt") + bias
    e = jnp.exp(scores - jnp.max(scores, axis=0, keepdims=True))
    return q, e * (1.0 / jnp.sum(e, axis=0, keepdims=True))


def attend_kernel(q_ref, k_ref, v_ref, pos_ref, o_ref, bias_ref):
    rows = q_ref.shape[0]

    @pl.when(pl.program_id(0) == 0)
    def _():
        set_bias(bias_ref, pos_ref, rows)

    low = lax.broadcasted_iota(jnp.int32, (1, 128), 1) < 64
    for c in range(0, q_ref.shape[1], 128):
        pair = slice(c, c + 128)
        for b in range(rows // WINDOW):
            here = slice(b * WINDOW, (b + 1) * WINDOW)
            keys = slice(max(b - 1, 0) * WINDOW, (b + 1) * WINDOW)
            bias = bias_ref[b, 2 * WINDOW - (keys.stop - keys.start) :, :]
            _, probs = pair_probs(q_ref[here, pair], k_ref[keys, pair], bias, low)
            out = dot(probs.astype(BF), v_ref[keys, pair], "tn")
            o_ref[here, pair] = jnp.where(low, out[:WINDOW], out[WINDOW:]).astype(BF)


def attend(qkv, position, pairs=4):
    rows, width = qkv.shape[0], qkv.shape[1] // 3
    steps = width // 128 // pairs
    cols = lambda part: pl.BlockSpec((rows, 128 * pairs), lambda j: (0, j + part * steps))
    return pl.pallas_call(
        attend_kernel,
        grid=(steps,),
        in_specs=[cols(0), cols(1), cols(2), whole((1, rows))],
        out_specs=cols(0),
        out_shape=sds((rows, width), BF),
        scratch_shapes=[pltpu.VMEM((rows // WINDOW, 2 * WINDOW, 2 * WINDOW), F32)],
        compiler_params=vmem_of(16),
        cost_estimate=work(1e9),
        name="attend",
    )(qkv, qkv, qkv, position)


def attend_back_kernel(
    q_ref, k_ref, v_ref, do_ref, pos_ref, cos_ref, sin_ref, dq_ref, dk_ref, dv_ref, bias_ref
):
    rows = q_ref.shape[0]
    blocks = rows // WINDOW

    @pl.when(pl.program_id(0) == 0)
    def _():
        set_bias(bias_ref, pos_ref, rows)

    lane = lax.broadcasted_iota(jnp.int32, (1, 128), 1)
    low, first = lane < 64, (lane % 64) < 32

    def turn_back(u, here):
        return rotate_lanes(u, cos_ref[here, :], -sin_ref[here, :], first).astype(BF)

    for c in range(0, q_ref.shape[1], 128):
        pair = slice(c, c + 128)
        dk, dv = [None] * blocks, [None] * blocks
        for b in range(blocks):
            here = slice(b * WINDOW, (b + 1) * WINDOW)
            keys = slice(max(b - 1, 0) * WINDOW, (b + 1) * WINDOW)
            bias = bias_ref[b, 2 * WINDOW - (keys.stop - keys.start) :, :]
            k = k_ref[keys, pair]
            q, probs = pair_probs(q_ref[here, pair], k, bias, low)
            do = split_heads(do_ref[here, pair], low)
            dp = dot(v_ref[keys, pair], do, "nt")
            delta = jnp.sum(probs * dp, axis=0, keepdims=True)
            ds = (probs * (dp - delta)).astype(BF)
            dq = dot(ds, k, "tn") * 0.125
            dq_ref[here, pair] = turn_back(jnp.where(low, dq[:WINDOW], dq[WINDOW:]), here)
            k_part = dot(ds, q)
            v_part = dot(probs.astype(BF), do)
            for i, kb in enumerate(range(max(b - 1, 0), b + 1)):
                part = slice(i * WINDOW, (i + 1) * WINDOW)
                dk[kb] = k_part[part] if dk[kb] is None else dk[kb] + k_part[part]
                dv[kb] = v_part[part] if dv[kb] is None else dv[kb] + v_part[part]
        for kb in range(blocks):
            here = slice(kb * WINDOW, (kb + 1) * WINDOW)
            dk_ref[here, pair] = turn_back(dk[kb], here)
            dv_ref[here, pair] = dv[kb].astype(BF)


def attend_back(qkv, grad, position, cosine, signed_sine, pairs=2):
    rows, width = qkv.shape[0], qkv.shape[1] // 3
    steps = width // 128 // pairs
    cols = lambda part: pl.BlockSpec((rows, 128 * pairs), lambda j: (0, j + part * steps))
    return pl.pallas_call(
        attend_back_kernel,
        grid=(steps,),
        in_specs=[cols(0), cols(1), cols(2), cols(0), whole((1, rows))] + [whole((rows, 128))] * 2,
        out_specs=[cols(0)] * 3,
        out_shape=[sds((rows, width), BF)] * 3,
        scratch_shapes=[pltpu.VMEM((rows // WINDOW, 2 * WINDOW, 2 * WINDOW), F32)],
        compiler_params=vmem_of(20),
        cost_estimate=work(1e9),
        name="attend_back",
    )(qkv, qkv, qkv, grad, position, cosine, signed_sine)


def mlp_copies(idx, pieces, downs, gate, up, down, sems):
    first, second, last = [], [], []
    half = gate.shape[1] // 2

    def copy(src, dst, group):
        n = len(first) + len(second) + len(last)
        group.append(pltpu.make_async_copy(src, dst, sems.at[n]))

    for i, ref in enumerate(pieces):
        rows = ref.shape[1]
        here = pl.ds(pl.multiple_of(((idx[0] * 2 + idx[1]) ^ i) * rows, rows), rows)
        for c, group in ((0, first), (half, second)):
            cols = pl.ds(c, half)
            for m, target in ((0, gate), (1, up)):
                copy(ref.at[m, :, cols], target.at[here, cols], group)
    for i, ref in enumerate(downs):
        rows = ref.shape[0]
        here = pl.ds(pl.multiple_of(((idx[0] * 2 + idx[1]) ^ i) * rows, rows), rows)
        copy(ref, down.at[here, :], last)
    return first, second, last


def mlp_kernel(last_half, *refs):
    idx, pieces, downs = refs[0], refs[1:9], refs[9:17]
    n_parts, g_parts, scale_ref = refs[17:19], refs[19:21], refs[21]
    refs = refs[22:]
    if last_half:
        before_ref, refs = refs[0], refs[1:]
    gg_out, gu_out = refs[:2]
    gn_parts, mlp_parts = refs[2:4], refs[4:6]
    refs = refs[6:]
    if last_half:
        send_ref, keep_ref, refs = refs[0], refs[1], refs[2:]
    else:
        total_out, refs = refs[0], refs[1:]
    (w_gate, w_up, w_down, n, gm, silu, slope, hidden, gg, gu, gn, mlp, total) = refs[:13]
    sems, n_sems, out_sems = refs[13:]
    rows, width = n.shape
    half, part = rows // 2, w_gate.shape[1]
    first, second, down = mlp_copies(idx, pieces, downs, w_gate, w_up, w_down, sems)
    n_copies, g_copies = [], []
    for k in range(2):
        here = pl.ds(k * half, half)
        n_copies.append(pltpu.make_async_copy(n_parts[k], n.at[here, :], n_sems.at[k]))
        g_copies.append(pltpu.make_async_copy(g_parts[k], gm.at[here, :], n_sems.at[2 + k]))
    before = [pltpu.make_async_copy(before_ref, total, n_sems.at[4])] if last_half else []
    for c in n_copies + first + second + g_copies + down + before:
        c.start()
    outs = []

    def send(src, dst):
        outs.append(pltpu.make_async_copy(src, dst, out_sems.at[len(outs)]))
        outs[-1].start()

    for c in n_copies + first:
        c.wait()
    chunks = [slice(c, c + part // 2) for c in (0, part // 2)]
    for k, cols in enumerate(chunks):
        if k == 1:
            for c in second:
                c.wait()
        gate, up = dot(n[...], w_gate[:, cols]), dot(n[...], w_up[:, cols])
        s = 0.5 * jnp.tanh(0.5 * gate) + 0.5
        act = gate * s
        silu[:, cols] = act
        slope[:, cols] = up * (s + act * (1.0 - s))
        hidden[:, cols] = (act * up).astype(BF)
    for c in g_copies + before:
        c.wait()
    gm[...] = (scale_ref[5:6] * gm[...].astype(F32)).astype(BF)
    for cols in chunks:
        product = dot(hidden[:, cols], gm[...], "tn")
        if last_half:
            product = product + total[cols, :].astype(F32)
        total[cols, :] = product.astype(BF)
    if last_half:
        block = send_ref.shape[1]
        for k in range(send_ref.shape[0]):
            for ref, x in ((send_ref, 1 - idx[1]), (keep_ref, idx[1])):
                at = pl.multiple_of((2 * k + x) * block, block)
                send(total.at[pl.ds(at, block), :], ref.at[k])
    else:
        send(total, total_out)
    for c in down:
        c.wait()
    for cols in chunks:
        gh = dot(gm[...], w_down[cols, :], "nt")
        gg[:, cols] = (gh * slope[:, cols]).astype(BF)
        gu[:, cols] = (gh * silu[:, cols]).astype(BF)
    send(gg, gg_out)
    send(gu, gu_out)
    for k in range(2):
        here = pl.ds(k * half, half)
        product = dot(gg[here, :], w_gate[...], "nt") + dot(gu[here, :], w_up[...], "nt")
        gn[here, :] = product.astype(BF)
        send(gn.at[here, :], gn_parts[k])
        mlp[here, :] = dot(hidden[here, :], w_down[...]).astype(BF)
        send(mlp.at[here, :], mlp_parts[k])
    for c in outs:
        c.wait()


def mlp_both(idx, pieces, downs, n_parts, g_parts, scale, before=None):
    rows, width = n_parts[0].shape
    part = pieces[0].shape[2]
    last_half = before is not None
    split, total = (4, part // 8, width), (part, width)
    in_specs = [SMEM] + [ANY] * 20 + [pl.BlockSpec(memory_space=pltpu.VMEM)]
    out_shape = [sds((2 * rows, part), BF)] * 2 + [sds((rows, width), BF)] * 4
    args = (idx, *pieces, *downs, *n_parts, *g_parts, scale)
    if last_half:
        in_specs.append(ANY)
        args += (before,)
        out_shape += [sds(split, BF)] * 2
    else:
        out_shape.append(sds(total, BF))
    tokens = (2 * rows, width)
    inner = (2 * rows, part)
    return pl.pallas_call(
        lambda *refs: mlp_kernel(last_half, *refs),
        in_specs=in_specs,
        out_specs=[ANY] * len(out_shape),
        out_shape=out_shape,
        scratch_shapes=[
            pltpu.VMEM((width, part), BF),
            pltpu.VMEM((width, part), BF),
            pltpu.VMEM(total, BF),
            pltpu.VMEM(tokens, BF),
            pltpu.VMEM(tokens, BF),
            pltpu.VMEM(inner, F32),
            pltpu.VMEM(inner, F32),
            pltpu.VMEM(inner, BF),
            pltpu.VMEM(inner, BF),
            pltpu.VMEM(inner, BF),
            pltpu.VMEM(tokens, BF),
            pltpu.VMEM(tokens, BF),
            pltpu.VMEM(total, BF),
            pltpu.SemaphoreType.DMA((40,)),
            pltpu.SemaphoreType.DMA((5,)),
            pltpu.SemaphoreType.DMA((14,)),
        ],
        compiler_params=vmem_of(46),
        cost_estimate=work(1e9),
        name="mlp_both",
    )(*args)


def weight_grad_kernel(idx, *refs):
    a_refs, b_refs, send_ref, keep_ref = refs[:8], refs[8:10], refs[10], refs[11]
    total = None
    for p in range(4):
        a = jnp.concatenate([a_refs[2 * p][...], a_refs[2 * p + 1][...]], axis=1)
        rows = a.shape[0]
        part = dot(a, b_refs[p // 2][pl.ds((p % 2) * rows, rows), :], "tn")
        total = part if total is None else total + part
    total = total.astype(BF).reshape((2,) + send_ref.shape[1:])
    half = pl.num_programs(0) // 2

    @pl.when(pl.program_id(0) < half)
    def _():
        send_ref[...] = total

    @pl.when(pl.program_id(0) >= half)
    def _():
        keep_ref[...] = total


def weight_grad(idx, a_parts, b_parts):
    tokens, width = a_parts[0].shape
    part = b_parts[0].shape[1]
    rows = width // 8
    split = (4, rows, part)

    def column(which):
        def place(i, s):
            mine = jnp.where(i < 2, 1 - s[1], s[1])
            return (0, 2 * (2 * (i % 2) + which) + mine)

        return pl.BlockSpec((tokens, rows), place)

    return pl.pallas_call(
        weight_grad_kernel,
        grid_spec=pltpu.PrefetchScalarGridSpec(
            num_scalar_prefetch=1,
            grid=(4,),
            in_specs=[column(0), column(1)] * 4
            + [pl.BlockSpec((2 * tokens, part), lambda i, s: (0, 0))] * 2,
            out_specs=[
                pl.BlockSpec((2, rows, part), lambda i, s: (jnp.minimum(i, 1), 0, 0)),
                pl.BlockSpec((2, rows, part), lambda i, s: (jnp.maximum(i - 2, 0), 0, 0)),
            ],
        ),
        out_shape=[sds(split, BF)] * 2,
        compiler_params=vmem_of(22),
        cost_estimate=work(1e9),
        name="weight_grad",
    )(idx, *[p for p in a_parts for _ in range(2)], *b_parts)


def attn_grad_kernel(idx, q_in, o_in, dq, dk, dv, do, *refs):
    outs, total = refs[:10], refs[10]
    core = idx[3]
    half = dq.shape[1]
    for n, parts in enumerate((((q_in, dq), (q_in, dk)), ((q_in, dv), (o_in, do)))):
        side = idx[1 + n]
        for c, (a, b) in enumerate(parts):
            cols = slice(c * half, (c + 1) * half)
            product = dot(a[...], b[...], "tn").astype(BF)
            total[:, :, :, :, :, cols] = product.reshape(4, 2, 2, 2, 32, half)
            for m in (c, 2, 3, 4):
                to_core = (1 - core) if m < 3 else core
                to_side = (1 - side) if m in (0, 1, 3) else side
                for other in range(2):
                    for k in range(4):
                        x, y = (to_side, other) if n == 0 else (other, to_side)
                        block = total[k, x, y, to_core, :, cols]
                        if m < 2:
                            outs[5 * n + m][other, k] = block
                        else:
                            outs[5 * n + m][other, k, :, cols] = block


def attn_grad(idx, q_in, o_in, dq, dk, dv, do):
    width = q_in.shape[1]
    vmem = pl.BlockSpec(memory_space=pltpu.VMEM)
    one, two = sds((2, 4, 32, width), BF), sds((2, 4, 32, 2 * width), BF)
    return pl.pallas_call(
        attn_grad_kernel,
        in_specs=[SMEM] + [vmem] * 6,
        out_specs=[vmem] * 10,
        out_shape=[one, one, two, two, two] * 2,
        scratch_shapes=[pltpu.VMEM((4, 2, 2, 2, 32, 2 * width), BF)],
        compiler_params=vmem_of(30),
        cost_estimate=work(1e9),
        name="attn_grad",
    )(idx, q_in, o_in, dq, dk, dv, do)


def z_blocks(step, z):
    if step == "near":
        return [1 - z % 2, 3 - z % 2]
    return [2 * (1 - z // 2) + z % 2] if step == "far" else [z]


def z_copies(idx, jobs, buf, sems):
    copies = []
    for step, pairs in jobs:
        for pair in pairs:
            for b in z_blocks(step, idx[0]):
                for ref in pair:
                    at = len(copies)
                    copies.append(pltpu.make_async_copy(ref.at[b], buf.at[at], sems.at[at]))
    return copies


def z_count(jobs):
    return sum(2 * n * (2 if step == "near" else 1) for step, n in jobs)


def z_scratch(jobs, block):
    count = z_count(jobs)
    return [pltpu.VMEM((count,) + block, BF), pltpu.SemaphoreType.DMA((count,))]


def z_near(buf, at, out):
    for k in range(2):
        total = buf[at + 2 * k].astype(F32) + buf[at + 2 * k + 1].astype(F32)
        out[k] = total.astype(BF)


def z_add(buf, at, *more):
    total = buf[at].astype(F32) + buf[at + 1].astype(F32)
    for part in more:
        total = total + part.astype(F32)
    return total.astype(BF)


def near_sum_kernel(n, idx, *refs):
    pairs, (out, buf, sems) = refs[: 2 * n], refs[2 * n :]
    pairs = [pairs[2 * m : 2 * m + 2] for m in range(n)]
    copies = z_copies(idx, [("near", pairs)], buf, sems)
    for copy in copies:
        copy.start()
    for copy in copies:
        copy.wait()
    for m in range(n):
        z_near(buf, 4 * m, out.at[m])


def near_sum(idx, pairs):
    n = len(pairs)
    block = pairs[0][0].shape[1:]
    return pl.pallas_call(
        lambda *refs: near_sum_kernel(n, *refs),
        in_specs=[SMEM] + [ANY] * (2 * n),
        out_specs=pl.BlockSpec(memory_space=pltpu.VMEM),
        out_shape=sds((n, 2) + block, BF),
        scratch_shapes=z_scratch([("near", n)], block),
        compiler_params=vmem_of(10),
        cost_estimate=work(1e9),
        name="near_sum",
    )(idx, *[p for pair in pairs for p in pair])


def first_sum_kernel(idx, a_ref, q_ref, k_ref, b_ref, v_ref, o_ref, near, *refs):
    z_refs, (a_out, b_out, far, gate_near, buf, sems) = refs[:6], refs[6:]
    down, up, gate = z_refs[:2], z_refs[2:4], z_refs[4:6]
    copies = z_copies(idx, [("far", [down, up]), ("near", [gate])], buf, sems)
    for copy in copies:
        copy.start()
    half = q_ref.shape[3]
    for keep, left, right, out in ((a_ref, q_ref, k_ref, a_out), (b_ref, v_ref, o_ref, b_out)):
        for ref, cols in ((left, slice(0, half)), (right, slice(half, 2 * half))):
            total = keep[:, :, :, cols].astype(F32) + ref[...].astype(F32)
            out[:, :, :, cols] = total.astype(BF)
    for copy in copies:
        copy.wait()
    high = idx[0] // 2
    for m in range(2):
        far[m] = z_add(buf, 2 * m, near[m, 1 - high])
    z_near(buf, 4, gate_near)


def first_sum(idx, parts, near, pairs):
    block = near.shape[2:]
    vmem = pl.BlockSpec(memory_space=pltpu.VMEM)
    shape = sds(parts[0].shape, BF)
    return pl.pallas_call(
        first_sum_kernel,
        in_specs=[SMEM] + [vmem] * 7 + [ANY] * 6,
        out_specs=[vmem] * 4,
        out_shape=[shape, shape, sds((2,) + block, BF), sds((2,) + block, BF)],
        scratch_shapes=z_scratch([("far", 2), ("near", 1)], block),
        compiler_params=vmem_of(22),
        cost_estimate=work(1e9),
        name="first_sum",
    )(idx, *parts, near, *[p for pair in pairs for p in pair])


def second_sum_kernel(idx, a0, a1, a2, b0, b1, b2, gate_near, *refs):
    gate, (a_away, b_away, gate_far, buf, sems) = refs[:2], refs[2:]
    copies = z_copies(idx, [("far", [gate])], buf, sems)
    i = pl.program_id(0)

    @pl.when(i == 0)
    def _():
        for copy in copies:
            copy.start()

    for p0, p1, p2, out in ((a0, a1, a2, a_away), (b0, b1, b2, b_away)):
        out[...] = (p0[...].astype(F32) + p1[...].astype(F32) + p2[...].astype(F32)).astype(BF)

    @pl.when(i == pl.num_programs(0) - 1)
    def _():
        for copy in copies:
            copy.wait()
        gate_far[...] = z_add(buf, 0, gate_near[1 - idx[0] // 2])


def stay_sum_kernel(idx, a0, a1, a2, b0, b1, b2, near, far, *refs):
    pairs, (a_stay, b_stay, own, buf, sems) = refs[:4], refs[4:]
    copies = z_copies(idx, [("total", [pairs[:2], pairs[2:]])], buf, sems)
    i = pl.program_id(0)

    @pl.when(i == 0)
    def _():
        for copy in copies:
            copy.start()

    for p0, p1, p2, out in ((a0, a1, a2, a_stay), (b0, b1, b2, b_stay)):
        out[...] = (p0[...].astype(F32) + p1[...].astype(F32) + p2[...].astype(F32)).astype(BF)

    @pl.when(i == pl.num_programs(0) - 1)
    def _():
        for copy in copies:
            copy.wait()
        for m in range(2):
            own[m] = z_add(buf, 2 * m, near[m, idx[0] // 2], far[m])


def half_sum(kernel, idx, parts, away, more, pairs, outs, jobs, mib, name):
    _, blocks, rows, cols = parts[0].shape
    block = pairs[0][0].shape[1:]
    side = lambda at: pl.BlockSpec(
        (None, 2, rows, cols), lambda i, s: (1 - s[at] if away else s[at], i, 0, 0)
    )
    out = pl.BlockSpec((2, rows, cols), lambda i, s: (i, 0, 0))
    return pl.pallas_call(
        kernel,
        grid_spec=pltpu.PrefetchScalarGridSpec(
            num_scalar_prefetch=1,
            grid=(blocks // 2,),
            in_specs=[side(2)] * 3
            + [side(1)] * 3
            + [pl.BlockSpec(p.shape, lambda i, s, n=p.ndim: (0,) * n) for p in more]
            + [ANY] * (2 * len(pairs)),
            out_specs=[out, out]
            + [pl.BlockSpec(shape, lambda i, s, n=len(shape): (0,) * n) for shape in outs],
            scratch_shapes=z_scratch(jobs, block),
        ),
        out_shape=[sds((blocks, rows, cols), BF)] * 2 + [sds(shape, BF) for shape in outs],
        compiler_params=vmem_of(mib),
        cost_estimate=work(1e9),
        name=name,
    )(idx, *parts, *more, *[p for pair in pairs for p in pair])


def second_sum(idx, parts, gate_near, pair):
    block = gate_near.shape[1:]
    return half_sum(
        second_sum_kernel, idx, parts, True, [gate_near], [pair], [block], [("far", 1)], 14, "second_sum"
    )


def stay_sum(idx, parts, near, far, pairs):
    return half_sum(
        stay_sum_kernel, idx, parts, False, [near, far], pairs, [far.shape], [("total", 2)], 56, "stay_sum"
    )


def third_sum_kernel(idx, a0, a1, b0, b1, small, own, gate_near, gate_far, *refs):
    gate, (own_out, mine, s1, s2, s3, buf, sems) = refs[:2], refs[2:]
    copies = z_copies(idx, [("total", [gate])], buf, sems)
    for copy in copies:
        copy.start()
    half, width = a0.shape[2], 2 * a0.shape[2]
    for k, out in enumerate((mine, s1, s2, s3)):
        z = idx[0] ^ k
        for p0, p1, low in ((a0, a1, 0), (b0, b1, half)):
            total = p0[z].astype(F32) + p1[z].astype(F32)
            out[:, low : low + half] = total.astype(out.dtype)
        out[:, width:] = small[z].astype(out.dtype)
    for copy in copies:
        copy.wait()
    own_out[pl.ds(0, 2)] = own[...]
    own_out[2] = z_add(buf, 0, gate_near[idx[0] // 2], gate_far[...])


def third_sum(idx, a_stay, a_y, b_stay, b_x, small, own, gate_near, gate_far, pair):
    vmem = pl.BlockSpec(memory_space=pltpu.VMEM)
    _, rows, half = a_stay.shape
    cols = 2 * half + small.shape[2]
    block = gate_far.shape
    return pl.pallas_call(
        third_sum_kernel,
        in_specs=[SMEM] + [vmem] * 8 + [ANY] * 2,
        out_specs=[vmem] * 5,
        out_shape=[sds((3,) + block, BF), sds((rows, cols), F32)] + [sds((rows, cols), BF)] * 3,
        scratch_shapes=z_scratch([("total", 1)], block),
        compiler_params=vmem_of(16),
        cost_estimate=work(1e9),
        name="third_sum",
    )(idx, a_stay, a_y, b_stay, b_x, small, own, gate_near, gate_far, *pair)


def place_kernel(n_small, idx, own, y_ref, core_ref, both_ref, *outs):
    rep = idx[2] * 2 + idx[3]
    rows = own.shape[0]
    wide, narrow = outs, ()
    if n_small:
        wide, narrow, tall = outs[: -1 - n_small], outs[-1 - n_small : -1], outs[-1]
    for ref, d in ((own, 0), (y_ref, 2), (core_ref, 1), (both_ref, 3)):
        low = 0
        for out in wide:
            cols = out.shape[2]
            out[pl.ds(rep ^ d, 1)] = ref[:, low : low + cols].astype(F32)[None]
            low += cols
        if n_small:
            at = pl.multiple_of((rep ^ d) * rows, rows)
            tall[pl.ds(at, rows), :] = ref[:, low : low + 128].astype(F32)
    if n_small:
        turned = tall[...].T
        for k, out in enumerate(narrow):
            out[...] = turned[k : k + 1]


def place_rows(idx, own, other_y, other_core, other_both, widths, n_small=0):
    rows = own.shape[0]
    vmem = pl.BlockSpec(memory_space=pltpu.VMEM)
    outs = pl.pallas_call(
        lambda *refs: place_kernel(n_small, *refs),
        in_specs=[SMEM] + [vmem] * 4,
        out_specs=[vmem] * (len(widths) + n_small),
        out_shape=[sds((4, rows, w), F32) for w in widths] + [sds((1, 4 * rows), F32)] * n_small,
        scratch_shapes=[pltpu.VMEM((4 * rows, 128), F32)] if n_small else [],
        compiler_params=vmem_of(16),
        cost_estimate=work(1e9),
        name="place_rows",
    )(idx, own, other_y, other_core, other_both)
    n = len(widths)
    return [out.reshape(4 * rows, -1) for out in outs[:n]] + [out[0] for out in outs[n:]]


def place_mlp_kernel(idx, own_ref, y_ref, core_ref, both_ref, down_out, up_out, gate_out):
    rep = idx[2] * 2 + idx[3]
    parts = ((own_ref, 0), (y_ref, 2), (core_ref, 1), (both_ref, 3))
    for ref, d in parts:
        down_out[pl.ds(rep ^ d, 1)] = ref[0].astype(F32)[None]
    for m, out in ((1, up_out), (2, gate_out)):
        for ref, d in parts:
            for g in range(own_ref.shape[2] // 128):
                at = pl.multiple_of((g * 4 + (rep ^ d)) * 128, 128)
                out[:, pl.ds(at, 128)] = ref[m, :, g * 128 : (g + 1) * 128].astype(F32)


def place_mlp(idx, own, other_y, other_core, other_both):
    _, rows, cols = own.shape
    vmem = pl.BlockSpec(memory_space=pltpu.VMEM)
    down, up, gate = pl.pallas_call(
        place_mlp_kernel,
        in_specs=[SMEM] + [vmem] * 4,
        out_specs=[vmem] * 3,
        out_shape=[sds((4, rows, cols), F32)] + [sds((rows, 4 * cols), F32)] * 2,
        compiler_params=vmem_of(16),
        cost_estimate=work(1e9),
        name="place_mlp",
    )(idx, own, other_y, other_core, other_both)
    return down.reshape(4 * rows, cols), up, gate


def share_kernel(idx, raw_ref, here_ref, there_ref):
    rep = idx[2] * 2 + idx[3]
    for d in range(4):
        out = (here_ref, there_ref)[d // 2]
        for g in range(out.shape[3] // 128):
            at = pl.multiple_of((g * 4 + (rep ^ d)) * 128, 128)
            out[d % 2, :, :, g * 128 : (g + 1) * 128] = raw_ref[:, :, pl.ds(at, 128)]


def share(idx, raw):
    _, rows, ff = raw.shape
    vmem = pl.BlockSpec(memory_space=pltpu.VMEM)
    return pl.pallas_call(
        share_kernel,
        in_specs=[SMEM, vmem],
        out_specs=[vmem] * 2,
        out_shape=[sds((2, 2, rows, ff // 4), BF)] * 2,
        compiler_params=vmem_of(8),
        cost_estimate=work(1e9),
        name="share",
    )(idx, raw)


def join_kernel(idx, own, y_ref, core_ref, out_ref):
    rep = idx[2] * 2 + idx[3]
    rows = own.shape[2]
    parts = ((own.at[0], 0), (y_ref.at[0], 2), (core_ref.at[0], 1), (core_ref.at[1], 3))
    for ref, d in parts:
        at = pl.multiple_of((rep ^ d) * rows, rows)
        out_ref[:, pl.ds(at, rows), :] = ref[...]


def join(idx, own, other_y, other_core):
    rows, part = own.shape[2:]
    vmem = pl.BlockSpec(memory_space=pltpu.VMEM)
    return pl.pallas_call(
        join_kernel,
        in_specs=[SMEM] + [vmem] * 3,
        out_specs=vmem,
        out_shape=sds((2, 4 * rows, part), BF),
        compiler_params=vmem_of(8),
        cost_estimate=work(1e9),
        name="join",
    )(idx, own, other_y, other_core)


def tuned(mesh):
    swap_bits = make_links(8, 4)

    def swap(value, name):
        return swap_bits(value, *BITS[name])

    def add(a, b):
        return (a.astype(F32) + b.astype(F32)).astype(BF)

    def along(value, index, axis):
        return lax.dynamic_index_in_dim(value, index, axis, keepdims=False)

    def shards(
        inputs,
        lengths,
        ln1_gain,
        ln1_bias,
        w_qkv,
        w_out,
        scale_attn,
        ln2_gain,
        ln2_bias,
        w_gate,
        w_up,
        w_down,
        scale_mlp,
        grad_out,
    ):
        count, width = inputs.shape
        head_width = width // HEADS
        group, rep = lax.axis_index("group"), lax.axis_index("rep")
        z, x, y, core = group // 2, group % 2, rep // 2, rep % 2
        idx = jnp.stack([z, x, y, core]).astype(jnp.int32)

        vectors = jnp.stack([ln1_gain, ln1_bias, scale_attn, ln2_gain, ln2_bias, scale_mlp], axis=1)
        vectors = jnp.pad(vectors, ((0, 0), (0, 122)))
        bundle = jnp.concatenate([w_qkv, w_out, vectors], axis=1)[None]
        from_z = [swap(bundle, n) for n in ("z1", "z2", "z3")]
        raw = jnp.stack([w_gate, w_up])
        raw_x = swap(raw, "x")
        share_here, share_there = share(idx, raw)
        share_y = swap(share_there, "y")

        segment, position = clip_layout(lengths[0], count)
        cosine, sine = lane_tables(position, head_width)
        position = position[None, :]

        share_core = swap(jnp.stack([share_here[1], share_y[1]]), "core")
        gu0 = join(idx, share_here, share_y, share_core)
        dnx0 = swap(w_down, "x")
        share_here, share_there = share(idx, raw_x)
        *from_z, gu0, dnx0, cosine, sine, position, share_here, share_there = window(
            *from_z, gu0, dnx0, cosine, sine, position, share_here, share_there
        )
        near = jnp.concatenate([bundle] + from_z)
        near, gu0, share_here, share_there = window(near, gu0, share_here, share_there)
        far_x, far_y = swap(near, "x"), swap(near, "y")
        gu1, dn1, dn2 = swap(gu0, "z1"), swap(w_down, "z1"), swap(w_down, "z2")

        far_x, far_y, gu0, gu1, dn1, dn2, near = window(far_x, far_y, gu0, gu1, dn1, dn2, near)
        both, came_near = swap(far_x, "y"), swap(near, "core")
        gu2, gux1, dnx1 = swap(gu0, "z2"), swap(gu1, "x"), swap(dn1, "x")

        have = [near, far_x, far_y, both]
        gu0, gu2, gux1, dnx1, dn2, grad_out, came_near, *have = window(
            gu0, gu2, gux1, dnx1, dn2, grad_out, came_near, *have
        )
        came = [came_near] + [swap(p, "core") for p in have[1:]]
        gu3, go_y = swap(gu0, "z3"), swap(grad_out, "y")
        gux2, dnx2 = swap(gu2, "x"), swap(dn2, "x")
        *came, cosine, sine, position = window(*came, cosine, sine, position)

        qkv, normed, w_attn, vecs = project(idx, have, came, inputs, cosine, sine)
        qkv, gux2, dnx2, gu3, w_down, share_there = window(
            qkv, gux2, dnx2, gu3, w_down, share_there
        )
        gux3, dn3, share_y = swap(gu3, "x"), swap(w_down, "z3"), swap(share_there, "y")
        attended = attend(qkv, position)
        attended, go_y, gux3, dn3, share_y, share_here, grad_out = window(
            attended, go_y, gux3, dn3, share_y, share_here, grad_out
        )
        share_core = swap(jnp.stack([share_here[1], share_y[1]]), "core")
        gux0 = join(idx, share_here, share_y, share_core)
        dnx3, go_core = swap(dn3, "x"), swap(grad_out, "core")
        branch, n_own = leave(attended, w_attn, inputs, vecs)
        n_own, gux0, dnx3, go_core, go_y = window(n_own, gux0, dnx3, go_core, go_y)

        n_y, n_core = swap(n_own, "y"), swap(n_own, "core")
        n_core, go_y = window(n_core, go_y)
        go_yc = swap(go_y, "core")
        pieces = (gu0, gux0, gu1, gux1, gu2, gux2, gu3, gux3)
        downs = (w_down, dnx0, dn1, dnx1, dn2, dnx2, dn3, dnx3)
        gg_a, gu_a, gn_own, gn_core, mlp_own, mlp_core, total = mlp_both(
            idx, pieces, downs, (n_own, n_core), (grad_out, go_core), vecs
        )
        n_y, go_y, go_yc, gn_core = window(n_y, go_y, go_yc, gn_core)
        n_yc = swap(n_y, "core")
        n_y, n_yc = window(n_y, n_yc)
        gn_core, mlp_core = swap(gn_core, "core"), swap(mlp_core, "core")
        gg_b, gu_b, gn_y, gn_yc, mlp_y, mlp_yc, down_send, down_keep = mlp_both(
            idx, pieces, downs, (n_y, n_yc), (go_y, go_yc), vecs, total
        )
        gn_y, gn_yc, gn_core, mlp_core, down_send = window(gn_y, gn_yc, gn_core, mlp_core, down_send)
        down_x = swap(down_send, "x")
        gn_yc = swap(gn_yc, "core")
        gn_y, gn_yc = window(gn_y, gn_yc)
        gn_send, gu_b, mlp_yc = window(add(gn_y, gn_yc), gu_b, mlp_yc)
        gn_y = swap(gn_send, "y")
        mlp_yc = swap(mlp_yc, "core")

        n_all = (n_own, n_core, n_y, n_yc)
        up_send, up_keep = weight_grad(idx, n_all, (gu_a, gu_b))
        gate_send, gate_keep = weight_grad(idx, n_all, (after(gg_a, up_send), gg_b))
        gate_send, up_send, mlp_yc, down_x = window(gate_send, up_send, mlp_yc, down_x)
        up_x = swap(up_send, "x")
        down_near = near_sum(idx, [(down_keep, down_x)])
        gn_y, mlp_send, down_near = window(gn_y, add(mlp_y, mlp_yc), down_near)
        mlp_y, down_near = swap(mlp_send, "y"), swap(down_near, "z1")

        grad_middle, grad_branch, grad_attended, mid_sums = back(
            (gn_own, gn_core, gn_y), grad_out, branch, inputs, vecs, w_attn
        )
        grad_attended, gate_send = window(grad_attended, gate_send)
        gate_x = swap(gate_send, "x")

        dq, dk, dv = attend_back(qkv, grad_attended, position, cosine, sine)
        dq, up_x, down_near = window(dq, up_x, down_near)
        up_near, dq = window(near_sum(idx, [(up_keep, up_x)]), dq)
        up_near = swap(up_near, "z1")
        grads = attn_grad(idx, normed, attended, dq, dk, dv, grad_branch)
        gate_x, up_near, mlp_y, *grads = window(gate_x, up_near, mlp_y, *grads)
        near = jnp.concatenate([down_near, up_near])
        pairs = [(down_keep, down_x), (up_keep, up_x), (gate_keep, gate_x)]
        q_send, k_send, a_send, a_keep, a_keep_here = grads[:5]
        v_send, o_send, b_send, b_keep, b_keep_here = grads[5:]

        away = [swap(v, "core") for v in (q_send, k_send, v_send, o_send)]
        late = (near, dq, dk, dv, mlp_y, a_send, b_send)
        *away, near, dq, dk, dv, mlp_y, a_send, b_send = window(*away, *late)
        a_core, b_core = swap(a_send, "core"), swap(b_send, "core")
        a_away, b_away, far, gate_near = first_sum(
            idx, (a_keep, *away[:2], b_keep, *away[2:]), near, pairs
        )
        late = (a_core, b_core, dq, dk, dv, mlp_y)
        a_away, b_away, far, gate_near, *late = window(a_away, b_away, far, gate_near, *late)
        a_core, b_core, dq, dk, dv, mlp_y = late
        a_x, b_y = swap(a_away, "x"), swap(b_away, "y")
        far, gate_near = swap(far, "z2"), swap(gate_near, "z1")
        input_grad, block_out, small = last(
            (dq, dk, dv),
            w_attn,
            inputs,
            vecs,
            grad_middle,
            (mlp_own, mlp_core, mlp_y),
            grad_out,
            branch,
            mid_sums,
        )
        small = small + swap(small, "core")
        small = small + swap(small, "x")
        a_x, b_y, small, gate_near, far = window(a_x, b_y, small, gate_near, far)
        parts = (a_keep_here, a_core, a_x, b_keep_here, b_core, b_y)
        a_away, b_away, gate_far = second_sum(idx, parts, gate_near, pairs[2])
        a_away, b_away, gate_far, small, *parts = window(a_away, b_away, gate_far, small, *parts)
        a_y, b_x, gate_far = swap(a_away, "y"), swap(b_away, "x"), swap(gate_far, "z2")
        a_stay, b_stay, own = stay_sum(idx, parts, near, far, pairs[:2])
        small = small + swap(small, "y")
        rows_of = small[:6].reshape(6, 4, 2, 2, 2, 32)
        rows_of = along(along(along(rows_of, x, 2), y, 2), core, 2)
        rows_of = jnp.pad(rows_of.transpose(1, 2, 0), ((0, 0), (0, 0), (0, 122))).astype(BF)
        a_y, b_x, rows_of, gate_far = window(a_y, b_x, rows_of, gate_far)
        own, mine, *sends = third_sum(
            idx, a_stay, a_y, b_stay, b_x, rows_of, own, gate_near, gate_far, pairs[2]
        )
        *sends, own, mine = window(*sends, own, mine)
        got = [swap(v, n) for v, n in zip(sends, ("z1", "z2", "z3"))]
        own_y, own_core = swap(own, "y"), swap(own, "core")
        *got, own, own_y, own_core = window(*got, own, own_y, own_core)
        mine = mine + (got[0].astype(F32) + got[1].astype(F32) + got[2].astype(F32))
        mine, own, own_y, own_core = window(mine.astype(BF), own, own_y, own_core)
        other, mine_core, own_both = swap(mine, "y"), swap(mine, "core"), swap(own_y, "core")
        w_down_grad, w_up_grad, w_gate_grad = place_mlp(idx, own, own_y, own_core, own_both)
        other, mine_core, w_down_grad, w_up_grad, w_gate_grad = window(
            other, mine_core, w_down_grad, w_up_grad, w_gate_grad
        )
        other_core = swap(other, "core")
        w_qkv_grad, w_out_grad, *small = place_rows(
            idx, mine, other, mine_core, other_core, (3 * width, width), 6
        )
        return (
            block_out,
            input_grad,
            small[0],
            small[1],
            w_qkv_grad,
            w_out_grad,
            small[2],
            small[3],
            small[4],
            w_gate_grad,
            w_up_grad,
            w_down_grad,
            small[5],
        )

    return shards


def plain(mesh):
    n_group, n_rep = mesh.shape["group"], mesh.shape["rep"]
    swap = make_links(n_group, n_rep)

    def gather_group(piece, group):
        return lax.all_gather(piece, "group", axis=0)
    def gather_all(piece, group, rep):
        full = lax.all_gather(piece, AXES, axis=0)
        return full.reshape((n_group, n_rep) + piece.shape)

    def gather_rep(piece):
        low = jnp.concatenate([piece, swap(piece, 0, 2)], axis=0)
        return jnp.concatenate([low, swap(low, 0, 1)], axis=0)

    def scatter_rep(blocks):
        half = blocks.shape[0] // 2
        low = blocks[:half].astype(F32) + swap(blocks[half:], 0, 1).astype(F32)
        quarter = half // 2
        return low[:quarter] + swap(low[quarter:].astype(BF), 0, 2).astype(F32)

    def scatter_group(grads, group):
        return lax.psum_scatter(grads, "group", scatter_dimension=0, tiled=False).astype(F32)

    def whole_rep(piece, rep):
        piece = piece.astype(BF)
        return lax.all_gather(piece, "rep", axis=0).astype(F32)

    def scatter_attn(grads, group, rep):
        part = lax.psum_scatter(grads, "group", scatter_dimension=0, tiled=True)
        return lax.psum(part, "rep").astype(F32)

    def sum_all(value):
        return lax.psum(value, AXES)

    def shards(
        inputs,
        lengths,
        ln1_gain,
        ln1_bias,
        w_qkv,
        w_out,
        scale_attn,
        ln2_gain,
        ln2_bias,
        w_gate,
        w_up,
        w_down,
        scale_mlp,
        grad_out,
    ):
        count, width = inputs.shape
        head_width = width // HEADS
        group, rep = lax.axis_index("group"), lax.axis_index("rep")
        rows = w_qkv.shape[0]
        ff = w_gate.shape[1]
        part_ff = ff // n_rep
        vectors = jnp.stack([ln1_gain, ln1_bias, scale_attn, ln2_gain, ln2_bias, scale_mlp], axis=1)
        vectors = jnp.pad(vectors, ((0, 0), (0, 128 - vectors.shape[1])))
        bundle = jnp.concatenate([w_qkv, w_out, vectors], axis=1)
        attn_full = gather_all(bundle, group, rep).reshape(width, -1)
        qkv_full = attn_full[:, : 3 * width]
        out_full = attn_full[:, 3 * width : 4 * width]
        vecs = attn_full[:, 4 * width : 4 * width + 6].T.astype(F32)
        gain_one, bias_one, attn_scale, gain_two, bias_two, mlp_scale = [vecs[i] for i in range(6)]

        def columns(w):
            blocks = w.reshape(rows, n_group, n_rep, ff // (n_group * n_rep))
            return blocks.transpose(2, 0, 1, 3).reshape(n_rep, rows, part_ff)

        pair = jnp.stack([columns(w_gate), columns(w_up)], axis=1)
        came = [pick(pair, rep)] + [swap(pick(pair, rep ^ d), 0, d) for d in (1, 2, 3)]
        came = jnp.stack(came)
        gate_up = jnp.stack([pick(came, rep ^ j) for j in range(n_rep)], axis=1)
        gate_up = gate_up.reshape(2, n_rep * rows, part_ff)
        down_rows = w_down.shape[0]
        gate_all = gather_group(gate_up[0], group).reshape(width, part_ff)
        up_all = gather_group(gate_up[1], group).reshape(width, part_ff)
        down_all = gather_group(w_down, group).reshape(part_ff, width)

        cot_all = gather_rep(grad_out)

        segment, position = clip_layout(lengths[0], count)
        cosine, sine = rotary_tables(position, head_width)
        frames = inputs.astype(F32)
        unit_one, inverse_one = norm_parts(frames)
        normed = (unit_one * gain_one + bias_one).astype(BF)
        projected = jnp.dot(normed, qkv_full, preferred_element_type=F32)
        queries = rotate(
            projected[:, :width].reshape(count, HEADS, head_width), cosine, sine
        ).astype(BF)
        keys_rot = rotate(
            projected[:, width : 2 * width].reshape(count, HEADS, head_width), cosine, sine
        ).astype(BF)
        values = projected[:, 2 * width :].reshape(count, HEADS, head_width).astype(BF)
        attended, log_totals = attention_forward(queries, keys_rot, values, segment, count, WINDOW)
        attended = attended.reshape(count, width).astype(BF)
        branch = jnp.dot(attended, out_full, preferred_element_type=F32)
        middle = frames + attn_scale * branch
        unit_two, inverse_two = norm_parts(middle)
        normed_two = (unit_two * gain_two + bias_two).astype(BF)

        normed_all = gather_rep(normed_two)
        gate = jnp.dot(normed_all, gate_all, preferred_element_type=F32)
        up_value = jnp.dot(normed_all, up_all, preferred_element_type=F32)
        sigmoid_gate = jax.nn.sigmoid(gate)
        silu_gate = gate * sigmoid_gate
        hidden = (silu_gate * up_value).astype(BF)
        mlp_part = jnp.dot(hidden, down_all, preferred_element_type=F32).astype(BF)
        mlp = scatter_rep(mlp_part)
        block_out = (middle + mlp_scale * mlp).astype(BF)
        cotangent = grad_out.astype(F32)
        scale_mlp_grad = jnp.sum(cotangent * mlp, axis=0)
        grad_mlp = (mlp_scale * cot_all.astype(F32)).astype(BF)

        def grad_blocks(a, b):
            out = jnp.einsum("td,te->de", a, b, preferred_element_type=F32).astype(BF)
            return out.reshape(n_group, out.shape[0] // n_group, out.shape[1])

        w_down_part = scatter_group(grad_blocks(hidden, grad_mlp), group)
        grad_hidden = jnp.einsum("td,fd->tf", grad_mlp, down_all, preferred_element_type=F32)
        grad_gate = (
            grad_hidden * up_value * sigmoid_gate * (1.0 + gate * (1.0 - sigmoid_gate))
        ).astype(BF)
        grad_up = (grad_hidden * silu_gate).astype(BF)
        grad_normed_part = jnp.einsum(
            "tf,df->td", grad_gate, gate_all, preferred_element_type=F32
        ) + jnp.einsum("tf,df->td", grad_up, up_all, preferred_element_type=F32)
        grad_normed_two = scatter_rep(grad_normed_part.astype(BF))
        w_gate_part = scatter_group(grad_blocks(normed_all, grad_gate), group)
        w_up_part = scatter_group(grad_blocks(normed_all, grad_up), group)

        def hidden_columns(part):
            full = whole_rep(part, rep)
            full = full.reshape(n_rep, full.shape[1], n_group, ff // (n_group * n_rep))
            return full.transpose(1, 2, 0, 3).reshape(full.shape[1], ff)

        w_gate_grad = hidden_columns(w_gate_part)
        w_up_grad = hidden_columns(w_up_part)
        w_down_grad = whole_rep(w_down_part, rep).reshape(n_rep * down_rows, width)

        ln2_gain_grad = jnp.sum(grad_normed_two * unit_two, axis=0)
        ln2_bias_grad = jnp.sum(grad_normed_two, axis=0)
        grad_middle = cotangent + norm_back(grad_normed_two, unit_two, inverse_two, gain_two)
        scale_attn_grad = jnp.sum(grad_middle * branch, axis=0)
        grad_branch = (attn_scale * grad_middle).astype(BF)
        w_out_part = jnp.einsum("td,te->de", attended, grad_branch, preferred_element_type=F32)
        w_out_grad = scatter_attn(w_out_part.astype(BF), group, rep)
        grad_attended = jnp.einsum(
            "te,de->td", grad_branch, out_full, preferred_element_type=F32
        ).astype(BF)
        grad_queries, grad_keys, grad_values = attention_backward(
            queries,
            keys_rot,
            values,
            grad_attended.reshape(count, HEADS, head_width),
            log_totals,
            segment,
            count,
            WINDOW,
        )
        grad_projected = jnp.concatenate(
            [
                rotate_back(grad_queries, cosine, sine).reshape(count, width),
                rotate_back(grad_keys, cosine, sine).reshape(count, width),
                grad_values.reshape(count, width),
            ],
            axis=1,
        ).astype(BF)
        w_qkv_part = jnp.einsum("td,te->de", normed, grad_projected, preferred_element_type=F32)
        w_qkv_grad = scatter_attn(w_qkv_part.astype(BF), group, rep)
        grad_normed = jnp.einsum(
            "te,de->td", grad_projected, qkv_full, preferred_element_type=F32
        )
        ln1_gain_grad = jnp.sum(grad_normed * unit_one, axis=0)
        ln1_bias_grad = jnp.sum(grad_normed, axis=0)
        input_grad = grad_middle + norm_back(grad_normed, unit_one, inverse_one, gain_one)
        small = sum_all(
            jnp.stack(
                [
                    ln1_gain_grad,
                    ln1_bias_grad,
                    scale_attn_grad,
                    ln2_gain_grad,
                    ln2_bias_grad,
                    scale_mlp_grad,
                ]
            )
        )
        own = width // n_group
        small = lax.dynamic_slice_in_dim(small, group * own, own, 1)
        return (
            block_out,
            input_grad,
            small[0],
            small[1],
            w_qkv_grad,
            w_out_grad,
            small[2],
            small[3],
            small[4],
            w_gate_grad,
            w_up_grad,
            w_down_grad,
            small[5],
        )

    return shards


def solution(mesh):
    n_group, n_rep = mesh.shape["group"], mesh.shape["rep"]
    shards = tuned(mesh) if n_group == 8 and n_rep == 4 else plain(mesh)
    rowed, flat = P(AXES, None), P(AXES)
    in_specs = (
        rowed, rowed, flat, flat, rowed, rowed, flat, flat, flat, rowed, rowed, rowed, flat, rowed,
    )
    own_rows, own_flat = P("group", None), P("group")
    out_specs = (
        rowed, rowed, own_flat, own_flat, own_rows, own_rows, own_flat, own_flat, own_flat,
        own_rows, own_rows, own_rows, own_flat,
    )
    return jax.shard_map(shards, mesh=mesh, in_specs=in_specs, out_specs=out_specs, check_vma=False)
```

```python
import math

import jax
import jax.numpy as jnp
from jax import lax
from jax.experimental import pallas as pl
from jax.experimental.pallas import tpu as pltpu
from jax.sharding import PartitionSpec as P

HEADS = 16
WINDOW = 128
EPS = 1e-05
AXES = ("group", "rep")
BF = jnp.bfloat16
F32 = jnp.float32


def clip_layout(length_row, count):
    clip_ends = jnp.cumsum(length_row)
    clip_starts = clip_ends - length_row
    row_index = jnp.arange(count, dtype=jnp.int32)
    segment = jnp.sum((row_index[:, None] >= clip_ends[None, :]).astype(jnp.int32), axis=1)
    member = (segment[:, None] == jnp.arange(length_row.shape[0], dtype=jnp.int32)[None, :]).astype(
        jnp.int32
    )
    position = row_index - jnp.sum(member * clip_starts[None, :], axis=1)
    return (segment, position)


def rotary_tables(position, width):
    half = width // 2
    freqs = jnp.power(10000.0, -jnp.arange(half, dtype=F32) * (2.0 / width))
    angles = position.astype(F32)[:, None] * freqs[None, :]
    cosine = jnp.concatenate([jnp.cos(angles), jnp.cos(angles)], axis=1)
    sine = jnp.concatenate([jnp.sin(angles), jnp.sin(angles)], axis=1)
    return (cosine[:, None, :], sine[:, None, :])


def rotate(values, cosine, sine):
    half = values.shape[-1] // 2
    turned = jnp.concatenate([-values[..., half:], values[..., :half]], axis=-1)
    return values * cosine + turned * sine


def rotate_back(values, cosine, sine):
    half = values.shape[-1] // 2
    turned = jnp.concatenate([values[..., half:], -values[..., :half]], axis=-1)
    return values * cosine + turned * sine


def norm_parts(values):
    mean_value = jnp.mean(values, axis=-1, keepdims=True)
    centered = values - mean_value
    variance = jnp.mean(centered * centered, axis=-1, keepdims=True)
    inverse = lax.rsqrt(variance + EPS)
    return (centered * inverse, inverse)


def norm_back(grad_normed, unit, inverse, gain):
    scaled = grad_normed * gain
    return inverse * (
        scaled
        - jnp.mean(scaled, axis=-1, keepdims=True)
        - unit * jnp.mean(scaled * unit, axis=-1, keepdims=True)
    )


def block_allowed(segment, segment_pad, start, block, window):
    query_index = start + jnp.arange(block, dtype=jnp.int32)
    key_index = start - window + jnp.arange(block + window, dtype=jnp.int32)
    offset = query_index[:, None] - key_index[None, :]
    same_clip = segment[:, None] == segment_pad[None, :]
    return same_clip & (offset >= 0) & (offset < window)


def pad_front(values, window, fill):
    front = jnp.full((window,) + values.shape[1:], fill, values.dtype)
    return jnp.concatenate([front, values], axis=0)


def attention_forward(queries, keys_rot, values, segment, block, window):
    factor = 1.0 / math.sqrt(queries.shape[-1])
    keys_pad = pad_front(keys_rot, window, 0)
    values_pad = pad_front(values, window, 0)
    segment_pad = pad_front(segment, window, -1)
    allowed = block_allowed(segment, segment_pad, 0, block, window)
    scores = (
        jnp.einsum("qhd,khd->hqk", queries, keys_pad, preferred_element_type=F32) * factor
    )
    masked = jnp.where(allowed[None], scores, -jnp.inf)
    peak = jnp.max(masked, axis=-1, keepdims=True)
    expd = jnp.exp(masked - peak)
    totals = jnp.sum(expd, axis=-1, keepdims=True)
    probs = (expd / totals).astype(BF)
    outputs = jnp.einsum("hqk,khd->qhd", probs, values_pad, preferred_element_type=F32)
    log_totals = peak + jnp.log(totals)
    return (outputs, log_totals)


def attention_backward(
    queries, keys_rot, values, grad_attended, log_totals, segment, block, window
):
    factor = 1.0 / math.sqrt(queries.shape[-1])
    keys_pad = pad_front(keys_rot, window, 0)
    values_pad = pad_front(values, window, 0)
    segment_pad = pad_front(segment, window, -1)
    allowed = block_allowed(segment, segment_pad, 0, block, window)
    scores = (
        jnp.einsum("qhd,khd->hqk", queries, keys_pad, preferred_element_type=F32) * factor
    )
    probs = jnp.where(
        allowed[None], jnp.exp(jnp.where(allowed[None], scores, -jnp.inf) - log_totals), 0.0
    )
    probs_low = probs.astype(BF)
    grad_probs = jnp.einsum("qhd,khd->hqk", grad_attended, values_pad, preferred_element_type=F32)
    delta = jnp.sum(probs * grad_probs, axis=-1, keepdims=True)
    grad_scores = (probs * (grad_probs - delta)).astype(BF)
    grad_queries = (
        jnp.einsum("hqk,khd->qhd", grad_scores, keys_pad, preferred_element_type=F32) * factor
    )
    key_part = (
        jnp.einsum("hqk,qhd->khd", grad_scores, queries, preferred_element_type=F32) * factor
    )
    value_part = jnp.einsum("hqk,qhd->khd", probs_low, grad_attended, preferred_element_type=F32)
    return (grad_queries, key_part[window:], value_part[window:])


def make_links(n_group, n_rep):
    def swap(value, group_bits, rep_bits):
        pairs = [
            (g * n_rep + r, (g ^ group_bits) * n_rep + (r ^ rep_bits))
            for g in range(n_group)
            for r in range(n_rep)
        ]
        return lax.ppermute(value, AXES, pairs)

    return swap


def pick(stacked, index):
    return lax.dynamic_index_in_dim(stacked, index, 0, keepdims=False)


BITS = {"z1": (2, 0), "z2": (4, 0), "z3": (6, 0), "x": (1, 0), "y": (0, 2), "core": (0, 1)}
CONTRACT = {
    "nn": (((1,), (0,)), ((), ())),
    "nt": (((1,), (1,)), ((), ())),
    "tn": (((0,), (0,)), ((), ())),
}


def vmem_of(mib):
    return pltpu.CompilerParams(vmem_limit_bytes=mib << 20)


def work(flops):
    return pl.CostEstimate(flops=int(flops), bytes_accessed=0, transcendentals=0)


ANY = pl.BlockSpec(memory_space=pl.ANY)
SMEM = pl.BlockSpec(memory_space=pltpu.SMEM)


def dot(a, b, form="nn"):
    return lax.dot_general(a, b, CONTRACT[form], preferred_element_type=F32)


def after(value, *done):
    return lax.optimization_barrier((value,) + done)[0]


def window(*values):
    return lax.optimization_barrier(values)


def lane_tables(position, width):
    lane = jnp.arange(2 * width, dtype=jnp.int32)
    index = (lane % (width // 2)).astype(F32)
    freqs = jnp.power(10000.0, -index * (2.0 / width))
    angles = position.astype(F32)[:, None] * freqs[None, :]
    sign = jnp.where(lane % width < width // 2, -1.0, 1.0)
    return jnp.cos(angles), jnp.sin(angles) * sign[None, :]


def sds(shape, dtype):
    return jax.ShapeDtypeStruct(shape, dtype)


def whole(shape):
    return pl.BlockSpec(shape, lambda *_: (0,) * len(shape))


def rotate_lanes(u, cosine, signed_sine, first):
    turned = jnp.where(first, pltpu.roll(u, 96, 1), pltpu.roll(u, 32, 1))
    return u * cosine + turned * signed_sine


PIECES = (
    ((0, 0, 0), (1, 0, 0), (2, 0, 0), (3, 0, 0)),
    ((0, 1, 0), (1, 1, 0), (2, 1, 0), (3, 1, 0)),
    ((0, 0, 1), (1, 0, 1), (2, 0, 1), (3, 0, 1)),
    ((0, 1, 1), (1, 1, 1), (2, 1, 1), (3, 1, 1)),
)


def project_kernel(*refs):
    n = len(PIECES)
    idx, own, came = refs[0], refs[1 : 1 + n], refs[1 + n : 1 + 2 * n]
    x_ref, cos_ref, sin_ref = refs[1 + 2 * n : 4 + 2 * n]
    qkv_ref, normed_ref, w_ref, vec_ref, weights, sems, out_sem = refs[4 + 2 * n :]
    j, steps = pl.program_id(0), pl.num_programs(0)
    block = qkv_ref.shape[1]

    def copies():
        out, count = [], 0
        for core_bit, group in ((0, own), (1, came)):
            for ref, owners in zip(group, PIECES):
                for i, (k, dx, dy) in enumerate(owners):
                    owner = (((idx[0] ^ k) * 2 + (idx[1] ^ dx)) * 2 + (idx[2] ^ dy)) * 2
                    row = pl.multiple_of((owner + (idx[3] ^ core_bit)) * 32, 32)
                    out.append(
                        pltpu.make_async_copy(
                            ref.at[i], weights.at[pl.ds(row, 32), :], sems.at[count]
                        )
                    )
                    count += 1
        return out

    def save():
        return pltpu.make_async_copy(weights, w_ref, out_sem)

    @pl.when(j == 0)
    def _():
        pieces = copies()
        for c in pieces:
            c.start()
        x = x_ref[...].astype(F32)
        centered = x - jnp.mean(x, axis=1, keepdims=True)
        unit = centered * lax.rsqrt(jnp.mean(centered * centered, axis=1, keepdims=True) + EPS)
        for c in pieces:
            c.wait()
        save().start()
        vecs = weights[:, weights.shape[1] - 128 :].astype(F32).T
        vec_ref[...] = vecs[:8]
        normed_ref[...] = (unit * vecs[0:1] + vecs[1:2]).astype(BF)

    p = dot(normed_ref[...], weights[:, pl.ds(pl.multiple_of(j * block, block), block)])
    lane = lax.broadcasted_iota(jnp.int32, (1, 128), 1)
    first = (lane % 64) < 32

    @pl.when(j * 3 < 2 * steps)
    def _():
        for c in range(0, block, 128):
            cols = slice(c, c + 128)
            qkv_ref[:, cols] = rotate_lanes(p[:, cols], cos_ref[...], sin_ref[...], first).astype(BF)

    @pl.when(j * 3 >= 2 * steps)
    def _():
        qkv_ref[...] = p.astype(BF)

    @pl.when(j == steps - 1)
    def _():
        save().wait()


def project(idx, own, came, x, cosine, signed_sine, block=1024):
    rows, width = x.shape
    cols = own[0].shape[-1]
    return pl.pallas_call(
        project_kernel,
        grid=(3 * width // block,),
        in_specs=[SMEM] + [ANY] * (2 * len(PIECES)) + [whole((rows, width))] + [whole((rows, 128))] * 2,
        out_specs=[
            pl.BlockSpec((rows, block), lambda j: (0, j)),
            whole((rows, width)),
            ANY,
            whole((8, width)),
        ],
        out_shape=[
            sds((rows, 3 * width), BF),
            sds((rows, width), BF),
            sds((width, cols), BF),
            sds((8, width), F32),
        ],
        scratch_shapes=[
            pltpu.VMEM((width, cols), BF),
            pltpu.SemaphoreType.DMA((32,)),
            pltpu.SemaphoreType.DMA,
        ],
        compiler_params=vmem_of(28),
        cost_estimate=work(1e9),
        name="project",
    )(idx, *own, *came, x, cosine, signed_sine)


def unit_of(values):
    centered = values - jnp.mean(values, axis=1, keepdims=True)
    inverse = lax.rsqrt(jnp.mean(centered * centered, axis=1, keepdims=True) + EPS)
    return centered * inverse, inverse


def unit_back(grad, unit, inverse, gain):
    scaled = grad * gain
    return inverse * (
        scaled
        - jnp.mean(scaled, axis=1, keepdims=True)
        - unit * jnp.mean(scaled * unit, axis=1, keepdims=True)
    )


def add_rows(ref, row, values):
    total = jnp.sum(values, axis=0, keepdims=True)

    @pl.when(pl.program_id(0) == 0)
    def _():
        ref[row : row + 1, :] = total

    @pl.when(pl.program_id(0) > 0)
    def _():
        ref[row : row + 1, :] += total


def leave_kernel(attended_ref, w_ref, x_ref, vec_ref, branch_ref, n_ref):
    branch = dot(attended_ref[...], w_ref[...])
    branch_ref[...] = branch
    unit, _ = unit_of(x_ref[...].astype(F32) + vec_ref[2:3] * branch)
    n_ref[...] = (unit * vec_ref[3:4] + vec_ref[4:5]).astype(BF)


def leave(attended, w_attn, x, vecs, block=256):
    rows, width = x.shape
    row = pl.BlockSpec((block, width), lambda i: (i, 0))
    return pl.pallas_call(
        leave_kernel,
        grid=(rows // block,),
        in_specs=[row, pl.BlockSpec((width, width), lambda i: (0, 3)), row, whole((8, width))],
        out_specs=[row, row],
        out_shape=[sds((rows, width), F32), sds((rows, width), BF)],
        compiler_params=vmem_of(20),
        cost_estimate=work(1e9),
        name="leave",
    )(attended, w_attn, x, vecs)


def back_kernel(
    a_ref, b_ref, c_ref, go_ref, branch_ref, x_ref, vec_ref, w_ref, gm_ref, gb_ref, ga_ref, sum_ref
):
    grad = a_ref[...].astype(F32) + b_ref[...].astype(F32) + c_ref[...].astype(F32)
    branch = branch_ref[...]
    unit, inverse = unit_of(x_ref[...].astype(F32) + vec_ref[2:3] * branch)

    @pl.when(pl.program_id(0) == 0)
    def _():
        sum_ref[...] = jnp.zeros_like(sum_ref)

    add_rows(sum_ref, 3, grad * unit)
    add_rows(sum_ref, 4, grad)
    grad_middle = go_ref[...].astype(F32) + unit_back(grad, unit, inverse, vec_ref[3:4])
    gm_ref[...] = grad_middle
    add_rows(sum_ref, 2, grad_middle * branch)
    grad_branch = (vec_ref[2:3] * grad_middle).astype(BF)
    gb_ref[...] = grad_branch
    ga_ref[...] = dot(grad_branch, w_ref[...], "nt").astype(BF)


def back(parts, grad_out, branch, x, vecs, w_attn, block=256):
    rows, width = x.shape
    row = pl.BlockSpec((block, width), lambda i: (i, 0))
    return pl.pallas_call(
        back_kernel,
        grid=(rows // block,),
        in_specs=[row] * 6
        + [whole((8, width)), pl.BlockSpec((width, width), lambda i: (0, 3))],
        out_specs=[row, row, row, whole((8, width))],
        out_shape=[sds((rows, width), F32)] + [sds((rows, width), BF)] * 2 + [sds((8, width), F32)],
        compiler_params=vmem_of(28),
        cost_estimate=work(1e9),
        name="back",
    )(*parts, grad_out, branch, x, vecs, w_attn)


def last_kernel(*refs):
    dq, dk, dv, wq, wk, wv, x_ref, vec_ref, gm_ref, m0, m1, m2, go_ref, branch_ref, mid_ref = refs[:15]
    ig_ref, out_ref, sum_ref = refs[15:]
    grad = dot(dq[...], wq[...], "nt") + dot(dk[...], wk[...], "nt") + dot(dv[...], wv[...], "nt")
    x = x_ref[...].astype(F32)
    unit, inverse = unit_of(x)

    @pl.when(pl.program_id(0) == 0)
    def _():
        sum_ref[...] = mid_ref[...]

    add_rows(sum_ref, 0, grad * unit)
    add_rows(sum_ref, 1, grad)
    ig_ref[...] = gm_ref[...] + unit_back(grad, unit, inverse, vec_ref[0:1])
    mlp = m0[...].astype(F32) + m1[...].astype(F32) + m2[...].astype(F32)
    out_ref[...] = (x + vec_ref[2:3] * branch_ref[...] + vec_ref[5:6] * mlp).astype(BF)
    add_rows(sum_ref, 5, go_ref[...].astype(F32) * mlp)


def last(grads, w_attn, x, vecs, grad_middle, mlp_parts, grad_out, branch, mid_sums, block=256):
    rows, width = x.shape
    row = pl.BlockSpec((block, width), lambda i: (i, 0))
    columns = [pl.BlockSpec((width, width), lambda i, n=n: (0, n)) for n in range(3)]
    return pl.pallas_call(
        last_kernel,
        grid=(rows // block,),
        in_specs=[row] * 3
        + columns
        + [row, whole((8, width))]
        + [row] * 6
        + [whole((8, width))],
        out_specs=[row, row, whole((8, width))],
        out_shape=[sds((rows, width), F32), sds((rows, width), BF), sds((8, width), F32)],
        compiler_params=vmem_of(36),
        cost_estimate=work(1e9),
        name="last",
    )(*grads, w_attn, w_attn, w_attn, x, vecs, grad_middle, *mlp_parts, grad_out, branch, mid_sums)


def set_bias(bias_ref, pos_ref, rows):
    for b in range(rows // WINDOW):
        keys = WINDOW if b == 0 else 2 * WINDOW
        offset = (
            lax.broadcasted_iota(jnp.int32, (keys, WINDOW), 1)
            - lax.broadcasted_iota(jnp.int32, (keys, WINDOW), 0)
            + (keys - WINDOW)
        )
        reach = jnp.minimum(pos_ref[:, b * WINDOW : (b + 1) * WINDOW], WINDOW - 1)
        bias = jnp.where((offset >= 0) & (offset <= reach), 0.0, -1e30)
        bias_ref[b, 2 * WINDOW - keys :, :WINDOW] = bias
        bias_ref[b, 2 * WINDOW - keys :, WINDOW:] = bias


def split_heads(u, low):
    zero = jnp.zeros_like(u)
    return jnp.concatenate([jnp.where(low, u, zero), jnp.where(low, zero, u)], axis=0)


def pair_probs(q, k, bias, low):
    q = split_heads(q, low) * jnp.asarray(0.125, BF)
    scores = dot(k, q, "nt") + bias
    e = jnp.exp(scores - jnp.max(scores, axis=0, keepdims=True))
    return q, e * (1.0 / jnp.sum(e, axis=0, keepdims=True))


def attend_kernel(q_ref, k_ref, v_ref, pos_ref, o_ref, bias_ref):
    rows = q_ref.shape[0]

    @pl.when(pl.program_id(0) == 0)
    def _():
        set_bias(bias_ref, pos_ref, rows)

    low = lax.broadcasted_iota(jnp.int32, (1, 128), 1) < 64
    for c in range(0, q_ref.shape[1], 128):
        pair = slice(c, c + 128)
        for b in range(rows // WINDOW):
            here = slice(b * WINDOW, (b + 1) * WINDOW)
            keys = slice(max(b - 1, 0) * WINDOW, (b + 1) * WINDOW)
            bias = bias_ref[b, 2 * WINDOW - (keys.stop - keys.start) :, :]
            _, probs = pair_probs(q_ref[here, pair], k_ref[keys, pair], bias, low)
            out = dot(probs.astype(BF), v_ref[keys, pair], "tn")
            o_ref[here, pair] = jnp.where(low, out[:WINDOW], out[WINDOW:]).astype(BF)


def attend(qkv, position, pairs=4):
    rows, width = qkv.shape[0], qkv.shape[1] // 3
    steps = width // 128 // pairs
    cols = lambda part: pl.BlockSpec((rows, 128 * pairs), lambda j: (0, j + part * steps))
    return pl.pallas_call(
        attend_kernel,
        grid=(steps,),
        in_specs=[cols(0), cols(1), cols(2), whole((1, rows))],
        out_specs=cols(0),
        out_shape=sds((rows, width), BF),
        scratch_shapes=[pltpu.VMEM((rows // WINDOW, 2 * WINDOW, 2 * WINDOW), F32)],
        compiler_params=vmem_of(16),
        cost_estimate=work(1e9),
        name="attend",
    )(qkv, qkv, qkv, position)


def attend_back_kernel(
    q_ref, k_ref, v_ref, do_ref, pos_ref, cos_ref, sin_ref, dq_ref, dk_ref, dv_ref, bias_ref
):
    rows = q_ref.shape[0]
    blocks = rows // WINDOW

    @pl.when(pl.program_id(0) == 0)
    def _():
        set_bias(bias_ref, pos_ref, rows)

    lane = lax.broadcasted_iota(jnp.int32, (1, 128), 1)
    low, first = lane < 64, (lane % 64) < 32

    def turn_back(u, here):
        return rotate_lanes(u, cos_ref[here, :], -sin_ref[here, :], first).astype(BF)

    for c in range(0, q_ref.shape[1], 128):
        pair = slice(c, c + 128)
        dk, dv = [None] * blocks, [None] * blocks
        for b in range(blocks):
            here = slice(b * WINDOW, (b + 1) * WINDOW)
            keys = slice(max(b - 1, 0) * WINDOW, (b + 1) * WINDOW)
            bias = bias_ref[b, 2 * WINDOW - (keys.stop - keys.start) :, :]
            k = k_ref[keys, pair]
            q, probs = pair_probs(q_ref[here, pair], k, bias, low)
            do = split_heads(do_ref[here, pair], low)
            dp = dot(v_ref[keys, pair], do, "nt")
            delta = jnp.sum(probs * dp, axis=0, keepdims=True)
            ds = (probs * (dp - delta)).astype(BF)
            dq = dot(ds, k, "tn") * 0.125
            dq_ref[here, pair] = turn_back(jnp.where(low, dq[:WINDOW], dq[WINDOW:]), here)
            k_part = dot(ds, q)
            v_part = dot(probs.astype(BF), do)
            for i, kb in enumerate(range(max(b - 1, 0), b + 1)):
                part = slice(i * WINDOW, (i + 1) * WINDOW)
                dk[kb] = k_part[part] if dk[kb] is None else dk[kb] + k_part[part]
                dv[kb] = v_part[part] if dv[kb] is None else dv[kb] + v_part[part]
        for kb in range(blocks):
            here = slice(kb * WINDOW, (kb + 1) * WINDOW)
            dk_ref[here, pair] = turn_back(dk[kb], here)
            dv_ref[here, pair] = dv[kb].astype(BF)


def attend_back(qkv, grad, position, cosine, signed_sine, pairs=2):
    rows, width = qkv.shape[0], qkv.shape[1] // 3
    steps = width // 128 // pairs
    cols = lambda part: pl.BlockSpec((rows, 128 * pairs), lambda j: (0, j + part * steps))
    return pl.pallas_call(
        attend_back_kernel,
        grid=(steps,),
        in_specs=[cols(0), cols(1), cols(2), cols(0), whole((1, rows))] + [whole((rows, 128))] * 2,
        out_specs=[cols(0)] * 3,
        out_shape=[sds((rows, width), BF)] * 3,
        scratch_shapes=[pltpu.VMEM((rows // WINDOW, 2 * WINDOW, 2 * WINDOW), F32)],
        compiler_params=vmem_of(20),
        cost_estimate=work(1e9),
        name="attend_back",
    )(qkv, qkv, qkv, grad, position, cosine, signed_sine)


def mlp_copies(idx, pieces, downs, gate, up, down, sems):
    first, second, last = [], [], []
    half = gate.shape[1] // 2

    def copy(src, dst, group):
        n = len(first) + len(second) + len(last)
        group.append(pltpu.make_async_copy(src, dst, sems.at[n]))

    for i, ref in enumerate(pieces):
        rows = ref.shape[1]
        here = pl.ds(pl.multiple_of(((idx[0] * 2 + idx[1]) ^ i) * rows, rows), rows)
        for c, group in ((0, first), (half, second)):
            cols = pl.ds(c, half)
            for m, target in ((0, gate), (1, up)):
                copy(ref.at[m, :, cols], target.at[here, cols], group)
    for i, ref in enumerate(downs):
        rows = ref.shape[0]
        here = pl.ds(pl.multiple_of(((idx[0] * 2 + idx[1]) ^ i) * rows, rows), rows)
        copy(ref, down.at[here, :], last)
    return first, second, last


def mlp_kernel(last_half, *refs):
    idx, pieces, downs = refs[0], refs[1:9], refs[9:17]
    n_parts, g_parts, scale_ref = refs[17:19], refs[19:21], refs[21]
    refs = refs[22:]
    if last_half:
        before_ref, refs = refs[0], refs[1:]
    gg_out, gu_out = refs[:2]
    gn_parts, mlp_parts = refs[2:4], refs[4:6]
    refs = refs[6:]
    if last_half:
        send_ref, keep_ref, refs = refs[0], refs[1], refs[2:]
    else:
        total_out, refs = refs[0], refs[1:]
    (w_gate, w_up, w_down, n, gm, silu, slope, hidden, gg, gu, gn, mlp, total) = refs[:13]
    sems, n_sems, out_sems = refs[13:]
    rows, width = n.shape
    half, part = rows // 2, w_gate.shape[1]
    first, second, down = mlp_copies(idx, pieces, downs, w_gate, w_up, w_down, sems)
    n_copies, g_copies = [], []
    for k in range(2):
        here = pl.ds(k * half, half)
        n_copies.append(pltpu.make_async_copy(n_parts[k], n.at[here, :], n_sems.at[k]))
        g_copies.append(pltpu.make_async_copy(g_parts[k], gm.at[here, :], n_sems.at[2 + k]))
    before = [pltpu.make_async_copy(before_ref, total, n_sems.at[4])] if last_half else []
    for c in n_copies + first + second + g_copies + down + before:
        c.start()
    outs = []

    def send(src, dst):
        outs.append(pltpu.make_async_copy(src, dst, out_sems.at[len(outs)]))
        outs[-1].start()

    for c in n_copies + first:
        c.wait()
    chunks = [slice(c, c + part // 2) for c in (0, part // 2)]
    for k, cols in enumerate(chunks):
        if k == 1:
            for c in second:
                c.wait()
        gate, up = dot(n[...], w_gate[:, cols]), dot(n[...], w_up[:, cols])
        s = 0.5 * jnp.tanh(0.5 * gate) + 0.5
        act = gate * s
        silu[:, cols] = act
        slope[:, cols] = up * (s + act * (1.0 - s))
        hidden[:, cols] = (act * up).astype(BF)
    for c in g_copies + before:
        c.wait()
    gm[...] = (scale_ref[5:6] * gm[...].astype(F32)).astype(BF)
    for cols in chunks:
        product = dot(hidden[:, cols], gm[...], "tn")
        if last_half:
            product = product + total[cols, :].astype(F32)
        total[cols, :] = product.astype(BF)
    if last_half:
        block = send_ref.shape[1]
        for k in range(send_ref.shape[0]):
            for ref, x in ((send_ref, 1 - idx[1]), (keep_ref, idx[1])):
                at = pl.multiple_of((2 * k + x) * block, block)
                send(total.at[pl.ds(at, block), :], ref.at[k])
    else:
        send(total, total_out)
    for c in down:
        c.wait()
    for cols in chunks:
        gh = dot(gm[...], w_down[cols, :], "nt")
        gg[:, cols] = (gh * slope[:, cols]).astype(BF)
        gu[:, cols] = (gh * silu[:, cols]).astype(BF)
    send(gg, gg_out)
    send(gu, gu_out)
    for k in range(2):
        here = pl.ds(k * half, half)
        product = dot(gg[here, :], w_gate[...], "nt") + dot(gu[here, :], w_up[...], "nt")
        gn[here, :] = product.astype(BF)
        send(gn.at[here, :], gn_parts[k])
        mlp[here, :] = dot(hidden[here, :], w_down[...]).astype(BF)
        send(mlp.at[here, :], mlp_parts[k])
    for c in outs:
        c.wait()


def mlp_both(idx, pieces, downs, n_parts, g_parts, scale, before=None):
    rows, width = n_parts[0].shape
    part = pieces[0].shape[2]
    last_half = before is not None
    split, total = (4, part // 8, width), (part, width)
    in_specs = [SMEM] + [ANY] * 20 + [pl.BlockSpec(memory_space=pltpu.VMEM)]
    out_shape = [sds((2 * rows, part), BF)] * 2 + [sds((rows, width), BF)] * 4
    args = (idx, *pieces, *downs, *n_parts, *g_parts, scale)
    if last_half:
        in_specs.append(ANY)
        args += (before,)
        out_shape += [sds(split, BF)] * 2
    else:
        out_shape.append(sds(total, BF))
    tokens = (2 * rows, width)
    inner = (2 * rows, part)
    return pl.pallas_call(
        lambda *refs: mlp_kernel(last_half, *refs),
        in_specs=in_specs,
        out_specs=[ANY] * len(out_shape),
        out_shape=out_shape,
        scratch_shapes=[
            pltpu.VMEM((width, part), BF),
            pltpu.VMEM((width, part), BF),
            pltpu.VMEM(total, BF),
            pltpu.VMEM(tokens, BF),
            pltpu.VMEM(tokens, BF),
            pltpu.VMEM(inner, F32),
            pltpu.VMEM(inner, F32),
            pltpu.VMEM(inner, BF),
            pltpu.VMEM(inner, BF),
            pltpu.VMEM(inner, BF),
            pltpu.VMEM(tokens, BF),
            pltpu.VMEM(tokens, BF),
            pltpu.VMEM(total, BF),
            pltpu.SemaphoreType.DMA((40,)),
            pltpu.SemaphoreType.DMA((5,)),
            pltpu.SemaphoreType.DMA((14,)),
        ],
        compiler_params=vmem_of(46),
        cost_estimate=work(1e9),
        name="mlp_both",
    )(*args)


def weight_grad_kernel(idx, *refs):
    a_refs, b_refs, send_ref, keep_ref = refs[:8], refs[8:10], refs[10], refs[11]
    total = None
    for p in range(4):
        a = jnp.concatenate([a_refs[2 * p][...], a_refs[2 * p + 1][...]], axis=1)
        rows = a.shape[0]
        part = dot(a, b_refs[p // 2][pl.ds((p % 2) * rows, rows), :], "tn")
        total = part if total is None else total + part
    total = total.astype(BF).reshape((2,) + send_ref.shape[1:])
    half = pl.num_programs(0) // 2

    @pl.when(pl.program_id(0) < half)
    def _():
        send_ref[...] = total

    @pl.when(pl.program_id(0) >= half)
    def _():
        keep_ref[...] = total


def weight_grad(idx, a_parts, b_parts):
    tokens, width = a_parts[0].shape
    part = b_parts[0].shape[1]
    rows = width // 8
    split = (4, rows, part)

    def column(which):
        def place(i, s):
            mine = jnp.where(i < 2, 1 - s[1], s[1])
            return (0, 2 * (2 * (i % 2) + which) + mine)

        return pl.BlockSpec((tokens, rows), place)

    return pl.pallas_call(
        weight_grad_kernel,
        grid_spec=pltpu.PrefetchScalarGridSpec(
            num_scalar_prefetch=1,
            grid=(4,),
            in_specs=[column(0), column(1)] * 4
            + [pl.BlockSpec((2 * tokens, part), lambda i, s: (0, 0))] * 2,
            out_specs=[
                pl.BlockSpec((2, rows, part), lambda i, s: (jnp.minimum(i, 1), 0, 0)),
                pl.BlockSpec((2, rows, part), lambda i, s: (jnp.maximum(i - 2, 0), 0, 0)),
            ],
        ),
        out_shape=[sds(split, BF)] * 2,
        compiler_params=vmem_of(22),
        cost_estimate=work(1e9),
        name="weight_grad",
    )(idx, *[p for p in a_parts for _ in range(2)], *b_parts)


def attn_grad_kernel(idx, q_in, o_in, dq, dk, dv, do, *refs):
    outs, total = refs[:10], refs[10]
    core = idx[3]
    half = dq.shape[1]
    for n, parts in enumerate((((q_in, dq), (q_in, dk)), ((q_in, dv), (o_in, do)))):
        side = idx[1 + n]
        for c, (a, b) in enumerate(parts):
            cols = slice(c * half, (c + 1) * half)
            product = dot(a[...], b[...], "tn").astype(BF)
            total[:, :, :, :, :, cols] = product.reshape(4, 2, 2, 2, 32, half)
            for m in (c, 2, 3, 4):
                to_core = (1 - core) if m < 3 else core
                to_side = (1 - side) if m in (0, 1, 3) else side
                for other in range(2):
                    for k in range(4):
                        x, y = (to_side, other) if n == 0 else (other, to_side)
                        block = total[k, x, y, to_core, :, cols]
                        if m < 2:
                            outs[5 * n + m][other, k] = block
                        else:
                            outs[5 * n + m][other, k, :, cols] = block


def attn_grad(idx, q_in, o_in, dq, dk, dv, do):
    width = q_in.shape[1]
    vmem = pl.BlockSpec(memory_space=pltpu.VMEM)
    one, two = sds((2, 4, 32, width), BF), sds((2, 4, 32, 2 * width), BF)
    return pl.pallas_call(
        attn_grad_kernel,
        in_specs=[SMEM] + [vmem] * 6,
        out_specs=[vmem] * 10,
        out_shape=[one, one, two, two, two] * 2,
        scratch_shapes=[pltpu.VMEM((4, 2, 2, 2, 32, 2 * width), BF)],
        compiler_params=vmem_of(30),
        cost_estimate=work(1e9),
        name="attn_grad",
    )(idx, q_in, o_in, dq, dk, dv, do)


def z_blocks(step, z):
    if step == "near":
        return [1 - z % 2, 3 - z % 2]
    return [2 * (1 - z // 2) + z % 2] if step == "far" else [z]


def z_copies(idx, jobs, buf, sems):
    copies = []
    for step, pairs in jobs:
        for pair in pairs:
            for b in z_blocks(step, idx[0]):
                for ref in pair:
                    at = len(copies)
                    copies.append(pltpu.make_async_copy(ref.at[b], buf.at[at], sems.at[at]))
    return copies


def z_count(jobs):
    return sum(2 * n * (2 if step == "near" else 1) for step, n in jobs)


def z_scratch(jobs, block):
    count = z_count(jobs)
    return [pltpu.VMEM((count,) + block, BF), pltpu.SemaphoreType.DMA((count,))]


def z_near(buf, at, out):
    for k in range(2):
        total = buf[at + 2 * k].astype(F32) + buf[at + 2 * k + 1].astype(F32)
        out[k] = total.astype(BF)


def z_add(buf, at, *more):
    total = buf[at].astype(F32) + buf[at + 1].astype(F32)
    for part in more:
        total = total + part.astype(F32)
    return total.astype(BF)


def near_sum_kernel(n, idx, *refs):
    pairs, (out, buf, sems) = refs[: 2 * n], refs[2 * n :]
    pairs = [pairs[2 * m : 2 * m + 2] for m in range(n)]
    copies = z_copies(idx, [("near", pairs)], buf, sems)
    for copy in copies:
        copy.start()
    for copy in copies:
        copy.wait()
    for m in range(n):
        z_near(buf, 4 * m, out.at[m])


def near_sum(idx, pairs):
    n = len(pairs)
    block = pairs[0][0].shape[1:]
    return pl.pallas_call(
        lambda *refs: near_sum_kernel(n, *refs),
        in_specs=[SMEM] + [ANY] * (2 * n),
        out_specs=pl.BlockSpec(memory_space=pltpu.VMEM),
        out_shape=sds((n, 2) + block, BF),
        scratch_shapes=z_scratch([("near", n)], block),
        compiler_params=vmem_of(10),
        cost_estimate=work(1e9),
        name="near_sum",
    )(idx, *[p for pair in pairs for p in pair])


def first_sum_kernel(idx, a_ref, q_ref, k_ref, b_ref, v_ref, o_ref, near, *refs):
    z_refs, (a_out, b_out, far, gate_near, buf, sems) = refs[:6], refs[6:]
    down, up, gate = z_refs[:2], z_refs[2:4], z_refs[4:6]
    copies = z_copies(idx, [("far", [down, up]), ("near", [gate])], buf, sems)
    for copy in copies:
        copy.start()
    half = q_ref.shape[3]
    for keep, left, right, out in ((a_ref, q_ref, k_ref, a_out), (b_ref, v_ref, o_ref, b_out)):
        for ref, cols in ((left, slice(0, half)), (right, slice(half, 2 * half))):
            total = keep[:, :, :, cols].astype(F32) + ref[...].astype(F32)
            out[:, :, :, cols] = total.astype(BF)
    for copy in copies:
        copy.wait()
    high = idx[0] // 2
    for m in range(2):
        far[m] = z_add(buf, 2 * m, near[m, 1 - high])
    z_near(buf, 4, gate_near)


def first_sum(idx, parts, near, pairs):
    block = near.shape[2:]
    vmem = pl.BlockSpec(memory_space=pltpu.VMEM)
    shape = sds(parts[0].shape, BF)
    return pl.pallas_call(
        first_sum_kernel,
        in_specs=[SMEM] + [vmem] * 7 + [ANY] * 6,
        out_specs=[vmem] * 4,
        out_shape=[shape, shape, sds((2,) + block, BF), sds((2,) + block, BF)],
        scratch_shapes=z_scratch([("far", 2), ("near", 1)], block),
        compiler_params=vmem_of(22),
        cost_estimate=work(1e9),
        name="first_sum",
    )(idx, *parts, near, *[p for pair in pairs for p in pair])


def second_sum_kernel(idx, a0, a1, a2, b0, b1, b2, gate_near, *refs):
    gate, (a_away, b_away, gate_far, buf, sems) = refs[:2], refs[2:]
    copies = z_copies(idx, [("far", [gate])], buf, sems)
    i = pl.program_id(0)

    @pl.when(i == 0)
    def _():
        for copy in copies:
            copy.start()

    for p0, p1, p2, out in ((a0, a1, a2, a_away), (b0, b1, b2, b_away)):
        out[...] = (p0[...].astype(F32) + p1[...].astype(F32) + p2[...].astype(F32)).astype(BF)

    @pl.when(i == pl.num_programs(0) - 1)
    def _():
        for copy in copies:
            copy.wait()
        gate_far[...] = z_add(buf, 0, gate_near[1 - idx[0] // 2])


def stay_sum_kernel(idx, a0, a1, a2, b0, b1, b2, near, far, *refs):
    pairs, (a_stay, b_stay, own, buf, sems) = refs[:4], refs[4:]
    copies = z_copies(idx, [("total", [pairs[:2], pairs[2:]])], buf, sems)
    i = pl.program_id(0)

    @pl.when(i == 0)
    def _():
        for copy in copies:
            copy.start()

    for p0, p1, p2, out in ((a0, a1, a2, a_stay), (b0, b1, b2, b_stay)):
        out[...] = (p0[...].astype(F32) + p1[...].astype(F32) + p2[...].astype(F32)).astype(BF)

    @pl.when(i == pl.num_programs(0) - 1)
    def _():
        for copy in copies:
            copy.wait()
        for m in range(2):
            own[m] = z_add(buf, 2 * m, near[m, idx[0] // 2], far[m])


def half_sum(kernel, idx, parts, away, more, pairs, outs, jobs, mib, name):
    _, blocks, rows, cols = parts[0].shape
    block = pairs[0][0].shape[1:]
    side = lambda at: pl.BlockSpec(
        (None, 2, rows, cols), lambda i, s: (1 - s[at] if away else s[at], i, 0, 0)
    )
    out = pl.BlockSpec((2, rows, cols), lambda i, s: (i, 0, 0))
    return pl.pallas_call(
        kernel,
        grid_spec=pltpu.PrefetchScalarGridSpec(
            num_scalar_prefetch=1,
            grid=(blocks // 2,),
            in_specs=[side(2)] * 3
            + [side(1)] * 3
            + [pl.BlockSpec(p.shape, lambda i, s, n=p.ndim: (0,) * n) for p in more]
            + [ANY] * (2 * len(pairs)),
            out_specs=[out, out]
            + [pl.BlockSpec(shape, lambda i, s, n=len(shape): (0,) * n) for shape in outs],
            scratch_shapes=z_scratch(jobs, block),
        ),
        out_shape=[sds((blocks, rows, cols), BF)] * 2 + [sds(shape, BF) for shape in outs],
        compiler_params=vmem_of(mib),
        cost_estimate=work(1e9),
        name=name,
    )(idx, *parts, *more, *[p for pair in pairs for p in pair])


def second_sum(idx, parts, gate_near, pair):
    block = gate_near.shape[1:]
    return half_sum(
        second_sum_kernel, idx, parts, True, [gate_near], [pair], [block], [("far", 1)], 14, "second_sum"
    )


def stay_sum(idx, parts, near, far, pairs):
    return half_sum(
        stay_sum_kernel, idx, parts, False, [near, far], pairs, [far.shape], [("total", 2)], 56, "stay_sum"
    )


def third_sum_kernel(idx, a0, a1, b0, b1, small, own, gate_near, gate_far, *refs):
    gate, (own_out, mine, s1, s2, s3, buf, sems) = refs[:2], refs[2:]
    copies = z_copies(idx, [("total", [gate])], buf, sems)
    for copy in copies:
        copy.start()
    half, width = a0.shape[2], 2 * a0.shape[2]
    for k, out in enumerate((mine, s1, s2, s3)):
        z = idx[0] ^ k
        for p0, p1, low in ((a0, a1, 0), (b0, b1, half)):
            total = p0[z].astype(F32) + p1[z].astype(F32)
            out[:, low : low + half] = total.astype(out.dtype)
        out[:, width:] = small[z].astype(out.dtype)
    for copy in copies:
        copy.wait()
    own_out[pl.ds(0, 2)] = own[...]
    own_out[2] = z_add(buf, 0, gate_near[idx[0] // 2], gate_far[...])


def third_sum(idx, a_stay, a_y, b_stay, b_x, small, own, gate_near, gate_far, pair):
    vmem = pl.BlockSpec(memory_space=pltpu.VMEM)
    _, rows, half = a_stay.shape
    cols = 2 * half + small.shape[2]
    block = gate_far.shape
    return pl.pallas_call(
        third_sum_kernel,
        in_specs=[SMEM] + [vmem] * 8 + [ANY] * 2,
        out_specs=[vmem] * 5,
        out_shape=[sds((3,) + block, BF), sds((rows, cols), F32)] + [sds((rows, cols), BF)] * 3,
        scratch_shapes=z_scratch([("total", 1)], block),
        compiler_params=vmem_of(16),
        cost_estimate=work(1e9),
        name="third_sum",
    )(idx, a_stay, a_y, b_stay, b_x, small, own, gate_near, gate_far, *pair)


def place_kernel(n_small, idx, own, y_ref, core_ref, both_ref, *outs):
    rep = idx[2] * 2 + idx[3]
    rows = own.shape[0]
    wide, narrow = outs, ()
    if n_small:
        wide, narrow, tall = outs[: -1 - n_small], outs[-1 - n_small : -1], outs[-1]
    for ref, d in ((own, 0), (y_ref, 2), (core_ref, 1), (both_ref, 3)):
        low = 0
        for out in wide:
            cols = out.shape[2]
            out[pl.ds(rep ^ d, 1)] = ref[:, low : low + cols].astype(F32)[None]
            low += cols
        if n_small:
            at = pl.multiple_of((rep ^ d) * rows, rows)
            tall[pl.ds(at, rows), :] = ref[:, low : low + 128].astype(F32)
    if n_small:
        turned = tall[...].T
        for k, out in enumerate(narrow):
            out[...] = turned[k : k + 1]


def place_rows(idx, own, other_y, other_core, other_both, widths, n_small=0):
    rows = own.shape[0]
    vmem = pl.BlockSpec(memory_space=pltpu.VMEM)
    outs = pl.pallas_call(
        lambda *refs: place_kernel(n_small, *refs),
        in_specs=[SMEM] + [vmem] * 4,
        out_specs=[vmem] * (len(widths) + n_small),
        out_shape=[sds((4, rows, w), F32) for w in widths] + [sds((1, 4 * rows), F32)] * n_small,
        scratch_shapes=[pltpu.VMEM((4 * rows, 128), F32)] if n_small else [],
        compiler_params=vmem_of(16),
        cost_estimate=work(1e9),
        name="place_rows",
    )(idx, own, other_y, other_core, other_both)
    n = len(widths)
    return [out.reshape(4 * rows, -1) for out in outs[:n]] + [out[0] for out in outs[n:]]


def place_mlp_kernel(idx, own_ref, y_ref, core_ref, both_ref, down_out, up_out, gate_out):
    rep = idx[2] * 2 + idx[3]
    parts = ((own_ref, 0), (y_ref, 2), (core_ref, 1), (both_ref, 3))
    for ref, d in parts:
        down_out[pl.ds(rep ^ d, 1)] = ref[0].astype(F32)[None]
    for m, out in ((1, up_out), (2, gate_out)):
        for ref, d in parts:
            for g in range(own_ref.shape[2] // 128):
                at = pl.multiple_of((g * 4 + (rep ^ d)) * 128, 128)
                out[:, pl.ds(at, 128)] = ref[m, :, g * 128 : (g + 1) * 128].astype(F32)


def place_mlp(idx, own, other_y, other_core, other_both):
    _, rows, cols = own.shape
    vmem = pl.BlockSpec(memory_space=pltpu.VMEM)
    down, up, gate = pl.pallas_call(
        place_mlp_kernel,
        in_specs=[SMEM] + [vmem] * 4,
        out_specs=[vmem] * 3,
        out_shape=[sds((4, rows, cols), F32)] + [sds((rows, 4 * cols), F32)] * 2,
        compiler_params=vmem_of(16),
        cost_estimate=work(1e9),
        name="place_mlp",
    )(idx, own, other_y, other_core, other_both)
    return down.reshape(4 * rows, cols), up, gate


def share_kernel(idx, raw_ref, here_ref, there_ref):
    rep = idx[2] * 2 + idx[3]
    for d in range(4):
        out = (here_ref, there_ref)[d // 2]
        for g in range(out.shape[3] // 128):
            at = pl.multiple_of((g * 4 + (rep ^ d)) * 128, 128)
            out[d % 2, :, :, g * 128 : (g + 1) * 128] = raw_ref[:, :, pl.ds(at, 128)]


def share(idx, raw):
    _, rows, ff = raw.shape
    vmem = pl.BlockSpec(memory_space=pltpu.VMEM)
    return pl.pallas_call(
        share_kernel,
        in_specs=[SMEM, vmem],
        out_specs=[vmem] * 2,
        out_shape=[sds((2, 2, rows, ff // 4), BF)] * 2,
        compiler_params=vmem_of(8),
        cost_estimate=work(1e9),
        name="share",
    )(idx, raw)


def join_kernel(idx, own, y_ref, core_ref, out_ref):
    rep = idx[2] * 2 + idx[3]
    rows = own.shape[2]
    parts = ((own.at[0], 0), (y_ref.at[0], 2), (core_ref.at[0], 1), (core_ref.at[1], 3))
    for ref, d in parts:
        at = pl.multiple_of((rep ^ d) * rows, rows)
        out_ref[:, pl.ds(at, rows), :] = ref[...]


def join(idx, own, other_y, other_core):
    rows, part = own.shape[2:]
    vmem = pl.BlockSpec(memory_space=pltpu.VMEM)
    return pl.pallas_call(
        join_kernel,
        in_specs=[SMEM] + [vmem] * 3,
        out_specs=vmem,
        out_shape=sds((2, 4 * rows, part), BF),
        compiler_params=vmem_of(8),
        cost_estimate=work(1e9),
        name="join",
    )(idx, own, other_y, other_core)


def tuned(mesh):
    swap_bits = make_links(8, 4)

    def swap(value, name):
        return swap_bits(value, *BITS[name])

    def add(a, b):
        return (a.astype(F32) + b.astype(F32)).astype(BF)

    def along(value, index, axis):
        return lax.dynamic_index_in_dim(value, index, axis, keepdims=False)

    def shards(
        inputs,
        lengths,
        ln1_gain,
        ln1_bias,
        w_qkv,
        w_out,
        scale_attn,
        ln2_gain,
        ln2_bias,
        w_gate,
        w_up,
        w_down,
        scale_mlp,
        grad_out,
    ):
        count, width = inputs.shape
        head_width = width // HEADS
        group, rep = lax.axis_index("group"), lax.axis_index("rep")
        z, x, y, core = group // 2, group % 2, rep // 2, rep % 2
        idx = jnp.stack([z, x, y, core]).astype(jnp.int32)

        vectors = jnp.stack([ln1_gain, ln1_bias, scale_attn, ln2_gain, ln2_bias, scale_mlp], axis=1)
        vectors = jnp.pad(vectors, ((0, 0), (0, 122)))
        bundle = jnp.concatenate([w_qkv, w_out, vectors], axis=1)[None]
        from_z = [swap(bundle, n) for n in ("z1", "z2", "z3")]
        raw = jnp.stack([w_gate, w_up])
        raw_x = swap(raw, "x")
        share_here, share_there = share(idx, raw)
        share_y = swap(share_there, "y")

        segment, position = clip_layout(lengths[0], count)
        cosine, sine = lane_tables(position, head_width)
        position = position[None, :]

        share_core = swap(jnp.stack([share_here[1], share_y[1]]), "core")
        gu0 = join(idx, share_here, share_y, share_core)
        dnx0 = swap(w_down, "x")
        share_here, share_there = share(idx, raw_x)
        *from_z, gu0, dnx0, cosine, sine, position, share_here, share_there = window(
            *from_z, gu0, dnx0, cosine, sine, position, share_here, share_there
        )
        near = jnp.concatenate([bundle] + from_z)
        near, gu0, share_here, share_there = window(near, gu0, share_here, share_there)
        far_x, far_y = swap(near, "x"), swap(near, "y")
        gu1, dn1, dn2 = swap(gu0, "z1"), swap(w_down, "z1"), swap(w_down, "z2")

        far_x, far_y, gu0, gu1, dn1, dn2, near = window(far_x, far_y, gu0, gu1, dn1, dn2, near)
        both, came_near = swap(far_x, "y"), swap(near, "core")
        gu2, gux1, dnx1 = swap(gu0, "z2"), swap(gu1, "x"), swap(dn1, "x")

        have = [near, far_x, far_y, both]
        gu0, gu2, gux1, dnx1, dn2, grad_out, came_near, *have = window(
            gu0, gu2, gux1, dnx1, dn2, grad_out, came_near, *have
        )
        came = [came_near] + [swap(p, "core") for p in have[1:]]
        gu3, go_y = swap(gu0, "z3"), swap(grad_out, "y")
        gux2, dnx2 = swap(gu2, "x"), swap(dn2, "x")
        *came, cosine, sine, position = window(*came, cosine, sine, position)

        qkv, normed, w_attn, vecs = project(idx, have, came, inputs, cosine, sine)
        qkv, gux2, dnx2, gu3, w_down, share_there = window(
            qkv, gux2, dnx2, gu3, w_down, share_there
        )
        gux3, dn3, share_y = swap(gu3, "x"), swap(w_down, "z3"), swap(share_there, "y")
        attended = attend(qkv, position)
        attended, go_y, gux3, dn3, share_y, share_here, grad_out = window(
            attended, go_y, gux3, dn3, share_y, share_here, grad_out
        )
        share_core = swap(jnp.stack([share_here[1], share_y[1]]), "core")
        gux0 = join(idx, share_here, share_y, share_core)
        dnx3, go_core = swap(dn3, "x"), swap(grad_out, "core")
        branch, n_own = leave(attended, w_attn, inputs, vecs)
        n_own, gux0, dnx3, go_core, go_y = window(n_own, gux0, dnx3, go_core, go_y)

        n_y, n_core = swap(n_own, "y"), swap(n_own, "core")
        n_core, go_y = window(n_core, go_y)
        go_yc = swap(go_y, "core")
        pieces = (gu0, gux0, gu1, gux1, gu2, gux2, gu3, gux3)
        downs = (w_down, dnx0, dn1, dnx1, dn2, dnx2, dn3, dnx3)
        gg_a, gu_a, gn_own, gn_core, mlp_own, mlp_core, total = mlp_both(
            idx, pieces, downs, (n_own, n_core), (grad_out, go_core), vecs
        )
        n_y, go_y, go_yc, gn_core = window(n_y, go_y, go_yc, gn_core)
        n_yc = swap(n_y, "core")
        n_y, n_yc = window(n_y, n_yc)
        gn_core, mlp_core = swap(gn_core, "core"), swap(mlp_core, "core")
        gg_b, gu_b, gn_y, gn_yc, mlp_y, mlp_yc, down_send, down_keep = mlp_both(
            idx, pieces, downs, (n_y, n_yc), (go_y, go_yc), vecs, total
        )
        gn_y, gn_yc, gn_core, mlp_core, down_send = window(gn_y, gn_yc, gn_core, mlp_core, down_send)
        down_x = swap(down_send, "x")
        gn_yc = swap(gn_yc, "core")
        gn_y, gn_yc = window(gn_y, gn_yc)
        gn_send, gu_b, mlp_yc = window(add(gn_y, gn_yc), gu_b, mlp_yc)
        gn_y = swap(gn_send, "y")
        mlp_yc = swap(mlp_yc, "core")

        n_all = (n_own, n_core, n_y, n_yc)
        up_send, up_keep = weight_grad(idx, n_all, (gu_a, gu_b))
        gate_send, gate_keep = weight_grad(idx, n_all, (after(gg_a, up_send), gg_b))
        gate_send, up_send, mlp_yc, down_x = window(gate_send, up_send, mlp_yc, down_x)
        up_x = swap(up_send, "x")
        down_near = near_sum(idx, [(down_keep, down_x)])
        gn_y, mlp_send, down_near = window(gn_y, add(mlp_y, mlp_yc), down_near)
        mlp_y, down_near = swap(mlp_send, "y"), swap(down_near, "z1")

        grad_middle, grad_branch, grad_attended, mid_sums = back(
            (gn_own, gn_core, gn_y), grad_out, branch, inputs, vecs, w_attn
        )
        grad_attended, gate_send = window(grad_attended, gate_send)
        gate_x = swap(gate_send, "x")

        dq, dk, dv = attend_back(qkv, grad_attended, position, cosine, sine)
        dq, up_x, down_near = window(dq, up_x, down_near)
        up_near, dq = window(near_sum(idx, [(up_keep, up_x)]), dq)
        up_near = swap(up_near, "z1")
        grads = attn_grad(idx, normed, attended, dq, dk, dv, grad_branch)
        gate_x, up_near, mlp_y, *grads = window(gate_x, up_near, mlp_y, *grads)
        near = jnp.concatenate([down_near, up_near])
        pairs = [(down_keep, down_x), (up_keep, up_x), (gate_keep, gate_x)]
        q_send, k_send, a_send, a_keep, a_keep_here = grads[:5]
        v_send, o_send, b_send, b_keep, b_keep_here = grads[5:]

        away = [swap(v, "core") for v in (q_send, k_send, v_send, o_send)]
        late = (near, dq, dk, dv, mlp_y, a_send, b_send)
        *away, near, dq, dk, dv, mlp_y, a_send, b_send = window(*away, *late)
        a_core, b_core = swap(a_send, "core"), swap(b_send, "core")
        a_away, b_away, far, gate_near = first_sum(
            idx, (a_keep, *away[:2], b_keep, *away[2:]), near, pairs
        )
        late = (a_core, b_core, dq, dk, dv, mlp_y)
        a_away, b_away, far, gate_near, *late = window(a_away, b_away, far, gate_near, *late)
        a_core, b_core, dq, dk, dv, mlp_y = late
        a_x, b_y = swap(a_away, "x"), swap(b_away, "y")
        gate_near = swap(gate_near, "z1")
        far = swap(far, "z2")
        input_grad, block_out, small = last(
            (dq, dk, dv),
            w_attn,
            inputs,
            vecs,
            grad_middle,
            (mlp_own, mlp_core, mlp_y),
            grad_out,
            branch,
            mid_sums,
        )
        small = small + swap(small, "core")
        small = small + swap(small, "x")
        far, a_x, b_y, gate_near, small = window(far, a_x, b_y, gate_near, small)
        parts = (a_keep_here, a_core, a_x, b_keep_here, b_core, b_y)
        a_away, b_away, gate_far = second_sum(idx, parts, gate_near, pairs[2])
        a_away, b_away, gate_far, small, *parts = window(a_away, b_away, gate_far, small, *parts)
        a_y, b_x, gate_far = swap(a_away, "y"), swap(b_away, "x"), swap(gate_far, "z2")
        a_stay, b_stay, own = stay_sum(idx, parts, near, far, pairs[:2])
        small = small + swap(small, "y")
        rows_of = small[:6].reshape(6, 4, 2, 2, 2, 32)
        rows_of = along(along(along(rows_of, x, 2), y, 2), core, 2)
        rows_of = jnp.pad(rows_of.transpose(1, 2, 0), ((0, 0), (0, 0), (0, 122))).astype(BF)
        a_y, b_x, rows_of, gate_far = window(a_y, b_x, rows_of, gate_far)
        own, mine, *sends = third_sum(
            idx, a_stay, a_y, b_stay, b_x, rows_of, own, gate_near, gate_far, pairs[2]
        )
        *sends, own, mine = window(*sends, own, mine)
        got = [swap(v, n) for v, n in zip(sends, ("z1", "z2", "z3"))]
        own_y, own_core = swap(own, "y"), swap(own, "core")
        *got, own, own_y, own_core = window(*got, own, own_y, own_core)
        mine = mine + (got[0].astype(F32) + got[1].astype(F32) + got[2].astype(F32))
        mine, own, own_y, own_core = window(mine.astype(BF), own, own_y, own_core)
        other, mine_core, own_both = swap(mine, "y"), swap(mine, "core"), swap(own_y, "core")
        w_down_grad, w_up_grad, w_gate_grad = place_mlp(idx, own, own_y, own_core, own_both)
        other, mine_core, w_down_grad, w_up_grad, w_gate_grad = window(
            other, mine_core, w_down_grad, w_up_grad, w_gate_grad
        )
        other_core = swap(other, "core")
        w_qkv_grad, w_out_grad, *small = place_rows(
            idx, mine, other, mine_core, other_core, (3 * width, width), 6
        )
        return (
            block_out,
            input_grad,
            small[0],
            small[1],
            w_qkv_grad,
            w_out_grad,
            small[2],
            small[3],
            small[4],
            w_gate_grad,
            w_up_grad,
            w_down_grad,
            small[5],
        )

    return shards


def plain(mesh):
    n_group, n_rep = mesh.shape["group"], mesh.shape["rep"]
    swap = make_links(n_group, n_rep)

    def gather_group(piece, group):
        return lax.all_gather(piece, "group", axis=0)
    def gather_all(piece, group, rep):
        full = lax.all_gather(piece, AXES, axis=0)
        return full.reshape((n_group, n_rep) + piece.shape)

    def gather_rep(piece):
        low = jnp.concatenate([piece, swap(piece, 0, 2)], axis=0)
        return jnp.concatenate([low, swap(low, 0, 1)], axis=0)

    def scatter_rep(blocks):
        half = blocks.shape[0] // 2
        low = blocks[:half].astype(F32) + swap(blocks[half:], 0, 1).astype(F32)
        quarter = half // 2
        return low[:quarter] + swap(low[quarter:].astype(BF), 0, 2).astype(F32)

    def scatter_group(grads, group):
        return lax.psum_scatter(grads, "group", scatter_dimension=0, tiled=False).astype(F32)

    def whole_rep(piece, rep):
        piece = piece.astype(BF)
        return lax.all_gather(piece, "rep", axis=0).astype(F32)

    def scatter_attn(grads, group, rep):
        part = lax.psum_scatter(grads, "group", scatter_dimension=0, tiled=True)
        return lax.psum(part, "rep").astype(F32)

    def sum_all(value):
        return lax.psum(value, AXES)

    def shards(
        inputs,
        lengths,
        ln1_gain,
        ln1_bias,
        w_qkv,
        w_out,
        scale_attn,
        ln2_gain,
        ln2_bias,
        w_gate,
        w_up,
        w_down,
        scale_mlp,
        grad_out,
    ):
        count, width = inputs.shape
        head_width = width // HEADS
        group, rep = lax.axis_index("group"), lax.axis_index("rep")
        rows = w_qkv.shape[0]
        ff = w_gate.shape[1]
        part_ff = ff // n_rep
        vectors = jnp.stack([ln1_gain, ln1_bias, scale_attn, ln2_gain, ln2_bias, scale_mlp], axis=1)
        vectors = jnp.pad(vectors, ((0, 0), (0, 128 - vectors.shape[1])))
        bundle = jnp.concatenate([w_qkv, w_out, vectors], axis=1)
        attn_full = gather_all(bundle, group, rep).reshape(width, -1)
        qkv_full = attn_full[:, : 3 * width]
        out_full = attn_full[:, 3 * width : 4 * width]
        vecs = attn_full[:, 4 * width : 4 * width + 6].T.astype(F32)
        gain_one, bias_one, attn_scale, gain_two, bias_two, mlp_scale = [vecs[i] for i in range(6)]

        def columns(w):
            blocks = w.reshape(rows, n_group, n_rep, ff // (n_group * n_rep))
            return blocks.transpose(2, 0, 1, 3).reshape(n_rep, rows, part_ff)

        pair = jnp.stack([columns(w_gate), columns(w_up)], axis=1)
        came = [pick(pair, rep)] + [swap(pick(pair, rep ^ d), 0, d) for d in (1, 2, 3)]
        came = jnp.stack(came)
        gate_up = jnp.stack([pick(came, rep ^ j) for j in range(n_rep)], axis=1)
        gate_up = gate_up.reshape(2, n_rep * rows, part_ff)
        down_rows = w_down.shape[0]
        gate_all = gather_group(gate_up[0], group).reshape(width, part_ff)
        up_all = gather_group(gate_up[1], group).reshape(width, part_ff)
        down_all = gather_group(w_down, group).reshape(part_ff, width)

        cot_all = gather_rep(grad_out)

        segment, position = clip_layout(lengths[0], count)
        cosine, sine = rotary_tables(position, head_width)
        frames = inputs.astype(F32)
        unit_one, inverse_one = norm_parts(frames)
        normed = (unit_one * gain_one + bias_one).astype(BF)
        projected = jnp.dot(normed, qkv_full, preferred_element_type=F32)
        queries = rotate(
            projected[:, :width].reshape(count, HEADS, head_width), cosine, sine
        ).astype(BF)
        keys_rot = rotate(
            projected[:, width : 2 * width].reshape(count, HEADS, head_width), cosine, sine
        ).astype(BF)
        values = projected[:, 2 * width :].reshape(count, HEADS, head_width).astype(BF)
        attended, log_totals = attention_forward(queries, keys_rot, values, segment, count, WINDOW)
        attended = attended.reshape(count, width).astype(BF)
        branch = jnp.dot(attended, out_full, preferred_element_type=F32)
        middle = frames + attn_scale * branch
        unit_two, inverse_two = norm_parts(middle)
        normed_two = (unit_two * gain_two + bias_two).astype(BF)

        normed_all = gather_rep(normed_two)
        gate = jnp.dot(normed_all, gate_all, preferred_element_type=F32)
        up_value = jnp.dot(normed_all, up_all, preferred_element_type=F32)
        sigmoid_gate = jax.nn.sigmoid(gate)
        silu_gate = gate * sigmoid_gate
        hidden = (silu_gate * up_value).astype(BF)
        mlp_part = jnp.dot(hidden, down_all, preferred_element_type=F32).astype(BF)
        mlp = scatter_rep(mlp_part)
        block_out = (middle + mlp_scale * mlp).astype(BF)
        cotangent = grad_out.astype(F32)
        scale_mlp_grad = jnp.sum(cotangent * mlp, axis=0)
        grad_mlp = (mlp_scale * cot_all.astype(F32)).astype(BF)

        def grad_blocks(a, b):
            out = jnp.einsum("td,te->de", a, b, preferred_element_type=F32).astype(BF)
            return out.reshape(n_group, out.shape[0] // n_group, out.shape[1])

        w_down_part = scatter_group(grad_blocks(hidden, grad_mlp), group)
        grad_hidden = jnp.einsum("td,fd->tf", grad_mlp, down_all, preferred_element_type=F32)
        grad_gate = (
            grad_hidden * up_value * sigmoid_gate * (1.0 + gate * (1.0 - sigmoid_gate))
        ).astype(BF)
        grad_up = (grad_hidden * silu_gate).astype(BF)
        grad_normed_part = jnp.einsum(
            "tf,df->td", grad_gate, gate_all, preferred_element_type=F32
        ) + jnp.einsum("tf,df->td", grad_up, up_all, preferred_element_type=F32)
        grad_normed_two = scatter_rep(grad_normed_part.astype(BF))
        w_gate_part = scatter_group(grad_blocks(normed_all, grad_gate), group)
        w_up_part = scatter_group(grad_blocks(normed_all, grad_up), group)

        def hidden_columns(part):
            full = whole_rep(part, rep)
            full = full.reshape(n_rep, full.shape[1], n_group, ff // (n_group * n_rep))
            return full.transpose(1, 2, 0, 3).reshape(full.shape[1], ff)

        w_gate_grad = hidden_columns(w_gate_part)
        w_up_grad = hidden_columns(w_up_part)
        w_down_grad = whole_rep(w_down_part, rep).reshape(n_rep * down_rows, width)

        ln2_gain_grad = jnp.sum(grad_normed_two * unit_two, axis=0)
        ln2_bias_grad = jnp.sum(grad_normed_two, axis=0)
        grad_middle = cotangent + norm_back(grad_normed_two, unit_two, inverse_two, gain_two)
        scale_attn_grad = jnp.sum(grad_middle * branch, axis=0)
        grad_branch = (attn_scale * grad_middle).astype(BF)
        w_out_part = jnp.einsum("td,te->de", attended, grad_branch, preferred_element_type=F32)
        w_out_grad = scatter_attn(w_out_part.astype(BF), group, rep)
        grad_attended = jnp.einsum(
            "te,de->td", grad_branch, out_full, preferred_element_type=F32
        ).astype(BF)
        grad_queries, grad_keys, grad_values = attention_backward(
            queries,
            keys_rot,
            values,
            grad_attended.reshape(count, HEADS, head_width),
            log_totals,
            segment,
            count,
            WINDOW,
        )
        grad_projected = jnp.concatenate(
            [
                rotate_back(grad_queries, cosine, sine).reshape(count, width),
                rotate_back(grad_keys, cosine, sine).reshape(count, width),
                grad_values.reshape(count, width),
            ],
            axis=1,
        ).astype(BF)
        w_qkv_part = jnp.einsum("td,te->de", normed, grad_projected, preferred_element_type=F32)
        w_qkv_grad = scatter_attn(w_qkv_part.astype(BF), group, rep)
        grad_normed = jnp.einsum(
            "te,de->td", grad_projected, qkv_full, preferred_element_type=F32
        )
        ln1_gain_grad = jnp.sum(grad_normed * unit_one, axis=0)
        ln1_bias_grad = jnp.sum(grad_normed, axis=0)
        input_grad = grad_middle + norm_back(grad_normed, unit_one, inverse_one, gain_one)
        small = sum_all(
            jnp.stack(
                [
                    ln1_gain_grad,
                    ln1_bias_grad,
                    scale_attn_grad,
                    ln2_gain_grad,
                    ln2_bias_grad,
                    scale_mlp_grad,
                ]
            )
        )
        own = width // n_group
        small = lax.dynamic_slice_in_dim(small, group * own, own, 1)
        return (
            block_out,
            input_grad,
            small[0],
            small[1],
            w_qkv_grad,
            w_out_grad,
            small[2],
            small[3],
            small[4],
            w_gate_grad,
            w_up_grad,
            w_down_grad,
            small[5],
        )

    return shards


def solution(mesh):
    n_group, n_rep = mesh.shape["group"], mesh.shape["rep"]
    shards = tuned(mesh) if n_group == 8 and n_rep == 4 else plain(mesh)
    rowed, flat = P(AXES, None), P(AXES)
    in_specs = (
        rowed, rowed, flat, flat, rowed, rowed, flat, flat, flat, rowed, rowed, rowed, flat, rowed,
    )
    own_rows, own_flat = P("group", None), P("group")
    out_specs = (
        rowed, rowed, own_flat, own_flat, own_rows, own_rows, own_flat, own_flat, own_flat,
        own_rows, own_rows, own_rows, own_flat,
    )
    return jax.shard_map(shards, mesh=mesh, in_specs=in_specs, out_specs=out_specs, check_vma=False)
```
